32 devices in a mesh: row: 8 (over z, x), col: 4 (over y, core).
Axes of the slice: x: 2, y: 2, z: 4, core: 2. Of those that a mesh axis runs over, the one named last changes fastest.
Arguments:
- tile_u: bfloat16 [16, 8, 1024, 128], P('row', 'col'), may hold values from -6 to 6
- tile_v: bfloat16 [16, 8, 128, 1024], P('row', 'col'), may hold values from -0.5 to 0.5
- tile_ranks: int32 [16, 8], P('row', 'col'), may hold values from 32 to 128
- inverses: bfloat16 [2, 1024, 1024], replicated, may hold values from -0.005859375 to 0.005859375
- panel_order: int32 [2, 2], replicated, may hold values from 0 to 15, as said below
Outputs:
- trailing: bfloat16 [16, 8, 1024, 1024], P('row', 'col')
The draws below stay inside these ranges and needn't reach their ends.
Inputs may be any that keep to these rules, and one draw needn't show every extreme that they name: `panel_order`: column 0 names 2 different tile rows, below 16; column 1 names 2 different tile columns, below 8; the last tile row and the last tile column are always among them.
All inputs are finite; a program needn't handle non-finite values.
Results may differ from the reference program's by a relative error of at most 0.0075.
Values may be sent and summed in bfloat16 or wider, within the bound.
No kernel may reach another device: no remote copies, remote signals or barrier semaphores. Data moves between devices by JAX's collectives and lax.ppermute only.
A program may use at most 128 MiB of HBM per device.

```python
import jax
import jax.numpy as jnp
from jax import lax

B = 1024
RK = 128
STEPS = 2
TILE_ROWS = 16
TILE_COLS = 8


def pick_with_last(key, count):
    earlier = jax.random.permutation(jax.random.fold_in(key, 1), count - 1)[:STEPS - 1].astype(jnp.int32)
    joined = jnp.concatenate([earlier, jnp.full((1,), count - 1, dtype=jnp.int32)])
    return jax.random.permutation(jax.random.fold_in(key, 2), joined)


def draw_panel_order(key, part):
    row_pick = pick_with_last(jax.random.fold_in(key, 11), TILE_ROWS)
    column_pick = pick_with_last(jax.random.fold_in(key, 12), TILE_COLS)
    return jnp.stack([row_pick, column_pick], axis=1).astype(jnp.int32)


def with_ends(values, key, low, high):
    longest = values.shape.index(max(values.shape))
    spots = []
    for shift in (0, 1):
        where = [jax.random.randint(jax.random.fold_in(key, axis), (), 0, length) for axis, length in enumerate(values.shape)]
        where[longest] = (where[longest] + shift) % values.shape[longest]
        spots.append(tuple(where))
    return values.at[spots[0]].set(low).at[spots[1]].set(high)


def block_levels(key, dims, split, least, top_value):
    level, own = 1.0, jax.random.fold_in(key, 6)
    for dim, parts in split:
        heights = jnp.exp(jax.random.uniform(jax.random.fold_in(own, dim), (parts,), jnp.float32, least / len(split), top_value / len(split)))
        level = level * jnp.repeat(heights, dims[dim] // parts).reshape([-1 if axis == dim else 1 for axis in range(len(dims))])
    return level


def gaussian(own_key, shape, scale, reach, shards=(), kind=jnp.bfloat16):
    drawn = scale * jax.random.normal(own_key, shape, jnp.float32)
    if shards:
        drawn = drawn * block_levels(own_key, shape, shards, -0.22, 0.18)
    return jnp.clip(drawn, -reach, reach).astype(kind)


def setup_inputs(seed: int = 0) -> dict:
    splits = jax.random.split(jax.random.key(seed), 6)
    return {
        "tile_u": gaussian(splits[0], (TILE_ROWS, TILE_COLS, B, RK), 1.0, 6.0, ((0, 8), (1, 4))),
        "tile_v": gaussian(splits[1], (TILE_ROWS, TILE_COLS, RK, B), RK ** -0.5, 0.5, ((0, 8), (1, 4))),
        "tile_ranks": with_ends(jax.random.randint(splits[2], (TILE_ROWS, TILE_COLS), RK // 4, RK + 1), jax.random.fold_in(splits[2], 1), RK // 4, RK).astype(jnp.int32),
        "inverses": gaussian(splits[3], (STEPS, B, B), (B * B) ** -0.5, 0.005859375),
        "panel_order": draw_panel_order(jax.random.fold_in(splits[5], 71), 0),
    }


def reference(tile_u, tile_v, tile_ranks, inverses, panel_order):
    kept_rows = (jnp.arange(RK, dtype=jnp.int32)[None, None, :] < tile_ranks[:, :, None]).astype(tile_v.dtype)
    left_factors = tile_u
    right_factors = tile_v * kept_rows[..., None]
    row_global = jnp.arange(TILE_ROWS, dtype=jnp.int32)
    column_global = jnp.arange(TILE_COLS, dtype=jnp.int32)
    row_done = jnp.zeros((TILE_ROWS,), dtype=jnp.bool_)
    column_done = jnp.zeros((TILE_COLS,), dtype=jnp.bool_)
    for step_index in range(STEPS):
        pivot_row = panel_order[step_index, 0]
        pivot_column = panel_order[step_index, 1]
        row_done = jnp.logical_or(row_done, row_global == pivot_row)
        column_done = jnp.logical_or(column_done, column_global == pivot_column)
        update_mask = jnp.logical_and(jnp.logical_not(row_done)[:, None], jnp.logical_not(column_done)[None, :]).astype(jnp.float32)
        column_left = lax.dynamic_index_in_dim(left_factors, pivot_column, 1, keepdims=False)
        column_right = lax.dynamic_index_in_dim(right_factors, pivot_column, 1, keepdims=False)
        pivot_left = lax.dynamic_index_in_dim(left_factors, pivot_row, 0, keepdims=False)
        pivot_right = lax.dynamic_index_in_dim(right_factors, pivot_row, 0, keepdims=False)
        solved = jnp.einsum("bd,cdk->cbk", inverses[step_index].astype(jnp.float32), pivot_left.astype(jnp.float32), precision=lax.Precision.HIGHEST).astype(jnp.bfloat16)
        core_block = jnp.einsum("rkb,cbs->rcks", column_right.astype(jnp.float32), solved.astype(jnp.float32), precision=lax.Precision.HIGHEST)
        core_block = core_block.astype(jnp.bfloat16)
        pivot_wide = pivot_right.astype(jnp.float32)

        def update_row(pair_rows):
            core_row, mask_row = pair_rows
            joined = jnp.einsum("cks,csb->ckb", core_row.astype(jnp.float32), pivot_wide)
            return (joined * (-mask_row)[:, None, None]).astype(jnp.bfloat16)

        update = lax.map(update_row, (core_block, update_mask))
        spread = jnp.broadcast_to(column_left[:, None], (TILE_ROWS, TILE_COLS) + column_left.shape[1:])
        left_factors = jnp.concatenate([left_factors, spread], axis=3)
        right_factors = jnp.concatenate([right_factors, update], axis=2)

    def form_row(pair_rows):
        left_row, right_row = pair_rows
        return jnp.einsum("cbk,ckd->cbd", left_row.astype(jnp.float32), right_row.astype(jnp.float32)).astype(jnp.bfloat16)

    return lax.map(form_row, (left_factors, right_factors))
```

```python
import jax
import jax.numpy as jnp
from jax import lax
from jax.sharding import PartitionSpec as P

F32 = jnp.float32
BF16 = jnp.bfloat16


def pick(array, index, axis=0):
    return lax.dynamic_index_in_dim(array, index, axis, keepdims=False)


def spread(parts, axis, n, root):
    me = lax.axis_index(axis)
    side = me % 2
    known = isinstance(root, int)
    bits = [1 << b for b in range(1, n.bit_length() - 1)]
    if known:
        bits = bits[::-1]
    holders = {root} if known else set(range(n))

    def swap(block, bit, senders):
        return lax.ppermute(block, axis, [(s, s ^ bit) for s in sorted(senders)])

    mine = pick(parts, side)
    if n > 1:
        got = swap(pick(parts, 1 - side), 1, holders)
        mine = jnp.where(root % 2 == side, mine, got)
        if known:
            holders = {root, root ^ 1}
    for bit in bits:
        got = swap(mine, bit, holders)
        mine = jnp.where((root & bit) == (me & bit), mine, got)
        if known:
            holders |= {h ^ bit for h in holders}
    if n == 1:
        return parts
    other = swap(mine, 1, holders)
    first = jnp.where(side == 0, mine, other)
    second = jnp.where(side == 0, other, mine)
    return jnp.stack([first, second])


def dot(a, b):
    return jnp.matmul(a, b, preferred_element_type=F32)


def make(rows_n, cols_n):
    def on_device(tile_u, tile_v, tile_ranks, inverses, panel_order):
        rows_here, cols_here = tile_u.shape[:2]
        rank = tile_u.shape[3]
        last_row = rows_n * rows_here - 1
        last_col = cols_n * cols_here - 1
        row_last_first = panel_order[0, 0] == last_row
        col_last_first = panel_order[0, 1] == last_col
        row_dyn = jnp.where(row_last_first, panel_order[1, 0], panel_order[0, 0])
        col_dyn = jnp.where(col_last_first, panel_order[1, 1], panel_order[0, 1])

        kept = jnp.arange(rank, dtype=jnp.int32)[None, None, :, None] < tile_ranks[:, :, None, None]
        right = jnp.where(kept, tile_v, jnp.zeros((), BF16))

        def by_row(tiles):
            fixed = spread(tiles[rows_here - 1], "row", rows_n, rows_n - 1)
            moving = spread(pick(tiles, row_dyn % rows_here), "row", rows_n, row_dyn // rows_here)
            return (jnp.where(row_last_first, fixed, moving), jnp.where(row_last_first, moving, fixed))

        def by_col(fixed, moving):
            fixed = spread(fixed, "col", cols_n, cols_n - 1)
            moving = spread(moving, "col", cols_n, col_dyn // cols_here)
            return (jnp.where(col_last_first, fixed, moving), jnp.where(col_last_first, moving, fixed))

        def panel(tiles):
            return by_col(tiles[:, cols_here - 1], pick(tiles, col_dyn % cols_here, 1))

        def halves(tile):
            return tile.reshape(2, tile.shape[0] // 2, tile.shape[1])

        def cross(one, two):
            for_last = jnp.where(col_last_first, two[cols_here - 1], one[cols_here - 1])
            local = col_dyn % cols_here
            for_dyn = jnp.where(col_last_first, pick(one, local), pick(two, local))
            a, b = by_col(halves(for_last), halves(for_dyn))
            return a.reshape(one.shape[1:]), b.reshape(one.shape[1:])

        up1, up2 = by_row(tile_u)
        vq1, vq2 = panel(right)
        u21, u12 = cross(up1, up2)
        vp1, vp2 = by_row(right)
        v21, v12 = cross(vp1, vp2)
        uq1, uq2 = panel(tile_u)

        wide = cols_here * rank
        s1 = dot(inverses[0], jnp.concatenate([up1[j] for j in range(cols_here)] + [u12], axis=1)).astype(BF16)
        s2 = dot(inverses[1], jnp.concatenate([up2[j] for j in range(cols_here)] + [u21], axis=1)).astype(BF16)
        tall = rows_here * rank
        c1 = dot(jnp.concatenate([vq1.reshape(tall, -1), v21]), s1).astype(BF16)
        c2 = dot(jnp.concatenate([vq2.reshape(tall, -1), v12]), s2).astype(BF16)

        row_global = lax.axis_index("row") * rows_here + jnp.arange(rows_here, dtype=jnp.int32)
        col_global = lax.axis_index("col") * cols_here + jnp.arange(cols_here, dtype=jnp.int32)
        p1, p2 = panel_order[0, 0], panel_order[1, 0]
        q1, q2 = panel_order[0, 1], panel_order[1, 1]
        open1 = (row_global != p1)[:, None] & (col_global != q1)[None, :]
        open2 = open1 & (row_global != p2)[:, None] & (col_global != q2)[None, :]
        m1 = open1.astype(F32)
        m2 = open2.astype(F32)

        def block(c, i, j):
            return c[i * rank:(i + 1) * rank, j * rank:(j + 1) * rank]

        outs = []
        for i in range(rows_here):
            line = []
            for j in range(cols_here):
                c1_p2j = block(c1, rows_here, j)
                c1_iq2 = block(c1, i, cols_here)
                below = jnp.concatenate([block(c2, rows_here, j), block(c2, rows_here, cols_here)], axis=1)
                low = -dot(c1_iq2, below)
                low_a, low_b = low[:, :rank], low[:, rank:].astype(BF16)
                high_a, high_b = block(c2, i, j), block(c2, i, cols_here)
                m_q1p1 = -m1[i, j] * block(c1, i, j).astype(F32) + m2[i, j] * dot(low_b, c1_p2j)
                m_q1p2 = -m2[i, j] * low_a
                m_q2p1 = m2[i, j] * dot(high_b, c1_p2j)
                m_q2p2 = -m2[i, j] * high_a.astype(F32)
                mix = jnp.concatenate([
                    jnp.concatenate([m_q1p1, m_q1p2], axis=1),
                    jnp.concatenate([m_q2p1, m_q2p2], axis=1)]).astype(BF16)
                change = dot(mix, jnp.concatenate([vp1[j], vp2[j]])).astype(BF16)
                line.append(jnp.concatenate([right[i, j], change]))
            outs.append(jnp.stack(line))
        right_all = jnp.stack(outs)
        left_all = jnp.concatenate([
            tile_u,
            jnp.broadcast_to(uq1[:, None], tile_u.shape),
            jnp.broadcast_to(uq2[:, None], tile_u.shape)], axis=3)
        return jnp.einsum("rcbk,rckd->rcbd", left_all, right_all, preferred_element_type=F32).astype(BF16)

    return on_device


def solution(mesh):
    placed = (P("row", "col", None, None), P("row", "col", None, None), P("row", "col"), P(), P())
    return jax.shard_map(
        make(mesh.shape["row"], mesh.shape["col"]),
        mesh=mesh,
        in_specs=placed,
        out_specs=P("row", "col", None, None),
        check_vma=False,
    )
```

```python
import jax
import jax.numpy as jnp
from jax import lax
from jax.experimental import pallas as pl
from jax.experimental.pallas import tpu as pltpu
from jax.sharding import PartitionSpec as P

F32 = jnp.float32
BF16 = jnp.bfloat16
VMEM_BYTES = 48 * 1024 * 1024
WHOLE = pl.BlockSpec(memory_space=pltpu.VMEM)
SCALARS = pl.BlockSpec(memory_space=pltpu.SMEM)


def params():
    return pltpu.CompilerParams(vmem_limit_bytes=VMEM_BYTES)


def dot(a, b):
    return jnp.dot(a, b, preferred_element_type=F32)


def swap(block, axis, n, bit, senders=None):
    if senders is None:
        pairs = [(s, s ^ bit) for s in range(n)]
    else:
        used = set(senders) | {s ^ bit for s in senders}
        pairs = [(s, s ^ bit) for s in sorted(senders)]
        pairs += [(d, d) for d in range(n) if d not in used]
    return lax.ppermute(block, axis, pairs)


def upper_bits(n):
    return [1 << b for b in range(1, n.bit_length() - 1)]


def lanes_moving(keep, give, axis, n, root):
    me = lax.axis_index(axis)
    got = swap(give, axis, n, 1)
    mine = jnp.where(((root ^ me) & 1) == 0, keep, got)
    for bit in upper_bits(n):
        got = swap(mine, axis, n, bit)
        mine = jnp.where(((root ^ me) & bit) == 0, mine, got)
    return mine


def lanes_fixed(keep, give, axis, n):
    me = lax.axis_index(axis)
    root = n - 1
    got = swap(give, axis, n, 1, {root})
    mine = jnp.where(me == (root ^ 1), got, keep)
    holders = {root, root ^ 1}
    for bit in upper_bits(n)[::-1]:
        got = swap(mine, axis, n, bit, holders)
        mine = jnp.where(((root ^ me) & bit) == 0, mine, got)
        holders |= {h ^ bit for h in holders}
    return mine


def prep_kernel(info, ranks, u, v, *outs):
    (rs_uk, rs_ug, rd_uk, rd_ug, rs_vk, rs_vg, rd_vk, rd_vg, cs_k, cs_g, cd_k, cd_g) = outs
    rows, cols = u.shape[:2]
    rank, width = v.shape[2:]
    row_dyn, col_dyn, row_side, col_side = info[0], info[1], info[2], info[3]

    def kept(i, j):
        row = lax.broadcasted_iota(jnp.int32, (rank, width), 0)
        return jnp.where(row < ranks[i, j], v[i, j], jnp.zeros((), v.dtype))

    for i, (u_outs, v_outs) in ((rows - 1, ((rs_uk, rs_ug), (rs_vk, rs_vg))), (row_dyn, ((rd_uk, rd_ug), (rd_vk, rd_vg)))):
        for slot, j in enumerate((row_side, 1 - row_side)):
            u_outs[slot][...] = u[i, j]
            v_outs[slot][...] = kept(i, j)
    for j, outs_here in ((cols - 1, (cs_k, cs_g)), (col_dyn, (cd_k, cd_g))):
        for slot, i in enumerate((col_side, 1 - col_side)):
            outs_here[slot][0] = u[i, j]
            value = kept(i, j)
            for k in range(width // rank):
                outs_here[slot][1, k * rank:(k + 1) * rank, :] = value[:, k * rank:(k + 1) * rank]


def solve_kernel(inverses, *refs):
    tiles, out = refs[:-1], refs[-1]
    per = len(tiles) // 2
    rank = tiles[0].shape[1]
    for s in range(2):
        joined = jnp.concatenate([t[...] for t in tiles[s * per:(s + 1) * per]], axis=1)
        out[s] = dot(inverses[s], joined).astype(BF16)


def core_kernel(solved, q1, q2, v21, v12, out):
    rank = v21.shape[0]
    count = v21.shape[1] // rank
    for s, (panel, more) in enumerate(((q1, v21), (q2, v12))):
        rows = panel.shape[0]
        lines = [jnp.concatenate([panel[i, k * rank:(k + 1) * rank, :] for k in range(count)], axis=1) for i in range(rows)]
        tall = jnp.concatenate(lines + [more[...]], axis=0)
        out[s] = dot(tall, solved[s]).astype(BF16)


def final_kernel(info, ranks, u, v, uq1, uq2, vp1, vp2, cores, out):
    i, j = pl.program_id(0), pl.program_id(1)
    rank, width = v.shape[2:]
    rows_here, cols_here = pl.num_programs(0), pl.num_programs(1)
    row, col = info[0] + i, info[1] + j
    open1 = jnp.logical_and(row != info[2], col != info[4])
    open2 = jnp.logical_and(open1, jnp.logical_and(row != info[3], col != info[5]))
    m1 = jnp.where(open1, F32(1), F32(0))
    m2 = jnp.where(open2, F32(1), F32(0))
    edge_r, edge_c = cores.shape[1] - rank, cores.shape[2] - rank
    top, left = pl.ds(pl.multiple_of(i * rank, rank), rank), pl.ds(pl.multiple_of(j * rank, rank), rank)
    foot, side = pl.ds(edge_r, rank), pl.ds(edge_c, rank)
    c1_ij, c1_iq2, c1_p2j = cores[0, top, left], cores[0, top, side], cores[0, foot, left]
    high_a, high_b = cores[1, top, left], cores[1, top, side]
    low_a = -dot(c1_iq2, cores[1, foot, left])
    low_b = -dot(c1_iq2, cores[1, foot, side])
    q1p1 = m2 * dot(low_b.astype(BF16), c1_p2j) - m1 * c1_ij.astype(F32)
    q2p1 = m2 * dot(high_b, c1_p2j)
    mix = jnp.concatenate([
        jnp.concatenate([q1p1, -m2 * low_a], axis=1),
        jnp.concatenate([q2p1, -m2 * high_a.astype(F32)], axis=1)], axis=0).astype(BF16)
    change = dot(mix, jnp.concatenate([vp1[0], vp2[0]], axis=0)).astype(BF16)
    line = lax.broadcasted_iota(jnp.int32, (rank, width), 0)
    own = jnp.where(line < ranks[i, j], v[0, 0], jnp.zeros((), BF16))
    right = jnp.concatenate([own, change], axis=0)
    out[0, 0] = dot(jnp.concatenate([u[0, 0], uq1[0], uq2[0]], axis=1), right).astype(BF16)


def make(rows_n, cols_n):
    def on_device(tile_u, tile_v, tile_ranks, inverses, panel_order):
        rows, cols, width, rank = tile_u.shape
        me_row, me_col = lax.axis_index("row"), lax.axis_index("col")
        p1, p2 = panel_order[0, 0], panel_order[1, 0]
        q1, q2 = panel_order[0, 1], panel_order[1, 1]
        row_first = p1 == rows_n * rows - 1
        col_first = q1 == cols_n * cols - 1
        row_dyn = jnp.where(row_first, p2, p1)
        col_dyn = jnp.where(col_first, q2, q1)
        side_r, side_c = me_row % 2, me_col % 2

        tall = jax.ShapeDtypeStruct((width, rank), BF16)
        flat = jax.ShapeDtypeStruct((rank, width), BF16)
        pair = jax.ShapeDtypeStruct((2, width, rank), BF16)
        cut = pl.pallas_call(
            prep_kernel,
            out_shape=[tall] * 4 + [flat] * 4 + [pair] * 4,
            in_specs=[SCALARS, SCALARS, WHOLE, WHOLE],
            out_specs=[WHOLE] * 12,
            compiler_params=params(),
        )(jnp.stack([row_dyn % rows, col_dyn % cols, side_r, side_c]).astype(jnp.int32), tile_ranks, tile_u, tile_v)
        rs_uk, rs_ug, rd_uk, rd_ug, rs_vk, rs_vg, rd_vk, rd_vg, cs_k, cs_g, cd_k, cd_g = cut

        def by_row(fixed_keep, fixed_give, moving_keep, moving_give):
            fixed = lanes_fixed(fixed_keep, fixed_give, "row", rows_n)
            moving = lanes_moving(moving_keep, moving_give, "row", rows_n, row_dyn // rows)
            mine = jnp.stack([jnp.where(row_first, fixed, moving), jnp.where(row_first, moving, fixed)])
            other = swap(mine, "row", rows_n, 1)
            return [jnp.stack([jnp.where(side_r == 0, mine[s], other[s]), jnp.where(side_r == 0, other[s], mine[s])]) for s in range(2)]

        def cross(one, two):
            shape = one.shape[1:]
            cand = jnp.stack([jnp.where(q1 % cols == 0, two[0], two[1]), jnp.where(q2 % cols == 0, one[0], one[1])])
            cand = cand.reshape(2, 2, shape[0] // 2, shape[1])
            keep = jnp.where(side_c == 0, cand[:, 0], cand[:, 1])
            give = jnp.where(side_c == 0, cand[:, 1], cand[:, 0])
            root = jnp.stack([q1 // cols, q2 // cols])[:, None, None]
            mine = lanes_moving(keep, give, "col", cols_n, root)
            other = swap(mine, "col", cols_n, 1)
            first, second = jnp.where(side_c == 0, mine, other), jnp.where(side_c == 0, other, mine)
            both = jnp.concatenate([first, second], axis=1)
            return both[0], both[1]

        up1, up2 = by_row(rs_uk, rs_ug, rd_uk, rd_ug)
        fixed = lanes_fixed(cs_k, cs_g, "col", cols_n)
        moving = lanes_moving(cd_k, cd_g, "col", cols_n, col_dyn // cols)
        mine = jnp.stack([jnp.where(col_first, fixed, moving), jnp.where(col_first, moving, fixed)])
        other = swap(mine, "col", cols_n, 1)
        first, second = jnp.where(side_c == 0, mine, other), jnp.where(side_c == 0, other, mine)
        uq1, uq2 = (jnp.stack([first[s, 0], second[s, 0]]) for s in range(2))
        vq1, vq2 = (jnp.stack([first[s, 1], second[s, 1]]) for s in range(2))
        u21, u12 = cross(up1, up2)
        vp1, vp2 = by_row(rs_vk, rs_vg, rd_vk, rd_vg)
        v21, v12 = cross(vp1, vp2)

        solved = pl.pallas_call(
            solve_kernel,
            out_shape=jax.ShapeDtypeStruct((2, width, 3 * rank), BF16),
            in_specs=[WHOLE] * 7,
            out_specs=WHOLE,
            compiler_params=params(),
            cost_estimate=pl.CostEstimate(flops=12 * width * width * rank, bytes_accessed=16 * width * rank + 4 * width * width, transcendentals=0),
        )(inverses, up1[0], up1[1], u12, up2[0], up2[1], u21)
        cores = pl.pallas_call(
            core_kernel,
            out_shape=jax.ShapeDtypeStruct((2, 3 * rank, 3 * rank), BF16),
            in_specs=[WHOLE] * 5,
            out_specs=WHOLE,
            compiler_params=params(),
        )(solved, vq1, vq2, v21, v12)

        info = jnp.stack([me_row * rows, me_col * cols, p1, p2, q1, q2]).astype(jnp.int32)
        return pl.pallas_call(
            final_kernel,
            out_shape=jax.ShapeDtypeStruct((rows, cols, width, width), BF16),
            grid=(rows, cols),
            in_specs=[
                SCALARS, SCALARS,
                pl.BlockSpec((1, 1, width, rank), lambda i, j: (i, j, 0, 0)),
                pl.BlockSpec((1, 1, rank, width), lambda i, j: (i, j, 0, 0)),
                pl.BlockSpec((1, width, rank), lambda i, j: (i, 0, 0)),
                pl.BlockSpec((1, width, rank), lambda i, j: (i, 0, 0)),
                pl.BlockSpec((1, rank, width), lambda i, j: (j, 0, 0)),
                pl.BlockSpec((1, rank, width), lambda i, j: (j, 0, 0)),
                WHOLE],
            out_specs=pl.BlockSpec((1, 1, width, width), lambda i, j: (i, j, 0, 0)),
            compiler_params=params(),
        )(info, tile_ranks, tile_u, tile_v, uq1, uq2, vp1, vp2, cores)

    return on_device


def solution(mesh):
    placed = (P("row", "col", None, None), P("row", "col", None, None), P("row", "col"), P(), P())
    return jax.shard_map(
        make(mesh.shape["row"], mesh.shape["col"]),
        mesh=mesh,
        in_specs=placed,
        out_specs=P("row", "col", None, None),
        check_vma=False,
    )
```

```python
import functools

import jax
import jax.numpy as jnp
from jax import lax
from jax.experimental import pallas as pl
from jax.experimental.pallas import tpu as pltpu
from jax.sharding import PartitionSpec as P

F32 = jnp.float32
BF16 = jnp.bfloat16
VMEM_BYTES = 48 * 1024 * 1024
WHOLE = pl.BlockSpec(memory_space=pltpu.VMEM)
SCALARS = pl.BlockSpec(memory_space=pltpu.SMEM)


def params():
    return pltpu.CompilerParams(vmem_limit_bytes=VMEM_BYTES)


def dot(a, b):
    return jnp.dot(a, b, preferred_element_type=F32)


def swap(block, axis, n, bit, senders=None):
    senders = range(n) if senders is None else sorted(senders)
    return lax.ppermute(block, axis, [(s, s ^ bit) for s in senders])


def member(me, devices):
    return (sum(1 << d for d in devices) >> me) & 1 == 1


def upper_bits(n):
    return [1 << b for b in range(1, n.bit_length() - 1)]


def lanes_moving(keep, give, axis, n, root):
    me = lax.axis_index(axis)
    got = swap(give, axis, n, 1)
    mine = jnp.where(((root ^ me) & 1) == 0, keep, got)
    for bit in upper_bits(n):
        got = swap(mine, axis, n, bit)
        mine = jnp.where(((root ^ me) & bit) == 0, mine, got)
    return mine


def lanes_known(keeps, gives, axis, n, roots):
    me = lax.axis_index(axis)
    mine = list(keeps)
    holders = [{r} for r in roots]
    for bit in [1] + upper_bits(n)[::-1]:
        sends = gives if bit == 1 else mine
        targets = [{h ^ bit for h in hold} for hold in holders]
        if holders[0] & holders[1]:
            got = [swap(sends[k], axis, n, bit, holders[k]) for k in range(2)]
        else:
            both = jnp.where(member(me, holders[1]), sends[1], sends[0])
            got = [swap(both, axis, n, bit, holders[0] | holders[1])] * 2
        mine = [jnp.where(member(me, targets[k]), got[k], mine[k]) for k in range(2)]
        holders = [holders[k] | targets[k] for k in range(2)]
    return mine


def prep_kernel(order, ranks, u, v, *outs, last_row, last_col):
    (rs_uk, rs_ug, rd_uk, rd_ug, rs_vk, rs_vg, rd_vk, rd_vg, c_k, c_g) = outs
    rows, cols = u.shape[:2]
    rank, width = v.shape[2:]
    row_dyn = lax.rem(jnp.where(order[0, 0] == last_row, order[1, 0], order[0, 0]), rows)
    col_dyn = lax.rem(jnp.where(order[0, 1] == last_col, order[1, 1], order[0, 1]), cols)
    row_side = lax.rem(lax.axis_index("row"), 2)
    col_side = lax.rem(lax.axis_index("col"), 2)

    def kept(i, j):
        row = lax.broadcasted_iota(jnp.int32, (rank, width), 0)
        return jnp.where(row < ranks[i, j], v[i, j], jnp.zeros((), v.dtype))

    for i, (u_outs, v_outs) in ((rows - 1, ((rs_uk, rs_ug), (rs_vk, rs_vg))), (row_dyn, ((rd_uk, rd_ug), (rd_vk, rd_vg)))):
        for slot, j in enumerate((row_side, 1 - row_side)):
            u_outs[slot][...] = u[i, j]
            v_outs[slot][...] = kept(i, j)
    for which, j in enumerate((cols - 1, col_dyn)):
        for slot, i in enumerate((col_side, 1 - col_side)):
            out = (c_k, c_g)[slot]
            out[which, 0] = u[i, j]
            value = kept(i, j)
            for k in range(width // rank):
                out[which, 1, k * rank:(k + 1) * rank, :] = value[:, k * rank:(k + 1) * rank]


def solve_kernel(inverses, *refs):
    tiles, out = refs[:-1], refs[-1]
    per = len(tiles) // 2
    rank = tiles[0].shape[1]
    for s in range(2):
        joined = jnp.concatenate([t[...] for t in tiles[s * per:(s + 1) * per]], axis=1)
        out[s] = dot(inverses[s], joined).astype(BF16)


def core_kernel(solved, q1, q2, v21, v12, out):
    rank = v21.shape[0]
    count = v21.shape[1] // rank
    for s, (panel, more) in enumerate(((q1, v21), (q2, v12))):
        rows = panel.shape[0]
        lines = [jnp.concatenate([panel[i, k * rank:(k + 1) * rank, :] for k in range(count)], axis=1) for i in range(rows)]
        tall = jnp.concatenate(lines + [more[...]], axis=0)
        out[s] = dot(tall, solved[s]).astype(BF16)


def final_kernel(order, ranks, u, v, uq1, uq2, vp1, vp2, cores, out):
    i, j = pl.program_id(0), pl.program_id(1)
    rank, width = v.shape[2:]
    row = lax.axis_index("row") * pl.num_programs(0) + i
    col = lax.axis_index("col") * pl.num_programs(1) + j
    open1 = jnp.logical_and(row != order[0, 0], col != order[0, 1])
    open2 = jnp.logical_and(open1, jnp.logical_and(row != order[1, 0], col != order[1, 1]))
    m1 = jnp.where(open1, F32(1), F32(0))
    m2 = jnp.where(open2, F32(1), F32(0))
    edge_r, edge_c = cores.shape[1] - rank, cores.shape[2] - rank
    top, left = pl.ds(pl.multiple_of(i * rank, rank), rank), pl.ds(pl.multiple_of(j * rank, rank), rank)
    foot, side = pl.ds(edge_r, rank), pl.ds(edge_c, rank)
    c1_ij, c1_iq2, c1_p2j = cores[0, top, left], cores[0, top, side], cores[0, foot, left]
    high_a, high_b = cores[1, top, left], cores[1, top, side]
    low_a = -dot(c1_iq2, cores[1, foot, left])
    low_b = -dot(c1_iq2, cores[1, foot, side])
    q1p1 = m2 * dot(low_b.astype(BF16), c1_p2j) - m1 * c1_ij.astype(F32)
    q2p1 = m2 * dot(high_b, c1_p2j)
    mix = jnp.concatenate([
        jnp.concatenate([q1p1, -m2 * low_a], axis=1),
        jnp.concatenate([q2p1, -m2 * high_a.astype(F32)], axis=1)], axis=0).astype(BF16)
    change = dot(mix, jnp.concatenate([vp1[0], vp2[0]], axis=0)).astype(BF16)
    line = lax.broadcasted_iota(jnp.int32, (rank, width), 0)
    own = jnp.where(line < ranks[i, j], v[0, 0], jnp.zeros((), BF16))
    right = jnp.concatenate([own, change], axis=0)
    out[0, 0] = dot(jnp.concatenate([u[0, 0], uq1[0], uq2[0]], axis=1), right).astype(BF16)


def make(rows_n, cols_n):
    def on_device(tile_u, tile_v, tile_ranks, inverses, panel_order):
        rows, cols, width, rank = tile_u.shape
        me_row, me_col = lax.axis_index("row"), lax.axis_index("col")
        p1, p2 = panel_order[0, 0], panel_order[1, 0]
        q1, q2 = panel_order[0, 1], panel_order[1, 1]
        row_first = p1 == rows_n * rows - 1
        col_first = q1 == cols_n * cols - 1
        row_dyn = jnp.where(row_first, p2, p1)
        col_dyn = jnp.where(col_first, q2, q1)
        side_r, side_c = me_row % 2, me_col % 2

        tall = jax.ShapeDtypeStruct((width, rank), BF16)
        flat = jax.ShapeDtypeStruct((rank, width), BF16)
        quad = jax.ShapeDtypeStruct((2, 2, width, rank), BF16)
        cut = pl.pallas_call(
            functools.partial(prep_kernel, last_row=rows_n * rows - 1, last_col=cols_n * cols - 1),
            out_shape=[tall] * 4 + [flat] * 4 + [quad] * 2,
            in_specs=[SCALARS, SCALARS, WHOLE, WHOLE],
            out_specs=[WHOLE] * 10,
            compiler_params=params(),
        )(panel_order, tile_ranks, tile_u, tile_v)

        def by_row(root, fixed_keep, fixed_give, moving_keep, moving_give):
            if root is None:
                fixed, moving = (
                    lanes_moving(k, g, "row", rows_n, r)
                    for k, g, r in ((fixed_keep, fixed_give, rows_n - 1), (moving_keep, moving_give, row_dyn // rows)))
            else:
                fixed, moving = lanes_known(
                    (fixed_keep, moving_keep), (fixed_give, moving_give), "row", rows_n, (rows_n - 1, root))
            mine = jnp.stack([jnp.where(row_first, fixed, moving), jnp.where(row_first, moving, fixed)])
            other = swap(mine, "row", rows_n, 1)
            return [jnp.stack([jnp.where(side_r == 0, mine[s], other[s]), jnp.where(side_r == 0, other[s], mine[s])]) for s in range(2)]

        def by_col(keep, give, roots):
            mine = lanes_moving(keep, give, "col", cols_n, roots)
            other = swap(mine, "col", cols_n, 1)
            return jnp.where(side_c == 0, mine, other), jnp.where(side_c == 0, other, mine)

        def cross(one, two):
            shape = one.shape[1:]
            cand = jnp.stack([jnp.where(q1 % cols == 0, two[0], two[1]), jnp.where(q2 % cols == 0, one[0], one[1])])
            cand = cand.reshape(2, 2, shape[0] // 2, shape[1])
            keep = jnp.where(side_c == 0, cand[:, 0], cand[:, 1])
            give = jnp.where(side_c == 0, cand[:, 1], cand[:, 0])
            both = jnp.concatenate(by_col(keep, give, jnp.stack([q1 // cols, q2 // cols])[:, None, None]), axis=1)
            return both[0], both[1]

        def gather(root, rs_uk, rs_ug, rd_uk, rd_ug, rs_vk, rs_vg, rd_vk, rd_vg, c_k, c_g):
            up1, up2 = by_row(root, rs_uk, rs_ug, rd_uk, rd_ug)
            first, second = by_col(c_k, c_g, jnp.stack([cols_n - 1, col_dyn // cols])[:, None, None, None])
            (u21, u12), (vp1, vp2) = cross(up1, up2), by_row(root, rs_vk, rs_vg, rd_vk, rd_vg)
            return up1, up2, u21, u12, vp1, vp2, first, second

        if rows_n <= 8:
            got = lax.switch(row_dyn // rows, [functools.partial(gather, r) for r in range(rows_n)], *cut)
        else:
            got = gather(None, *cut)
        up1, up2, u21, u12, vp1, vp2, first, second = got
        v21, v12 = cross(vp1, vp2)
        uq_fixed, uq_moving = (jnp.stack([first[s, 0], second[s, 0]]) for s in range(2))
        vq_fixed, vq_moving = (jnp.stack([first[s, 1], second[s, 1]]) for s in range(2))
        uq1, uq2 = jnp.where(col_first, uq_fixed, uq_moving), jnp.where(col_first, uq_moving, uq_fixed)
        vq1, vq2 = jnp.where(col_first, vq_fixed, vq_moving), jnp.where(col_first, vq_moving, vq_fixed)

        solved = pl.pallas_call(
            solve_kernel,
            out_shape=jax.ShapeDtypeStruct((2, width, 3 * rank), BF16),
            in_specs=[WHOLE] * 7,
            out_specs=WHOLE,
            compiler_params=params(),
            cost_estimate=pl.CostEstimate(flops=12 * width * width * rank, bytes_accessed=16 * width * rank + 4 * width * width, transcendentals=0),
        )(inverses, up1[0], up1[1], u12, up2[0], up2[1], u21)
        cores = pl.pallas_call(
            core_kernel,
            out_shape=jax.ShapeDtypeStruct((2, 3 * rank, 3 * rank), BF16),
            in_specs=[WHOLE] * 5,
            out_specs=WHOLE,
            compiler_params=params(),
        )(solved, vq1, vq2, v21, v12)

        return pl.pallas_call(
            final_kernel,
            out_shape=jax.ShapeDtypeStruct((rows, cols, width, width), BF16),
            grid=(rows, cols),
            in_specs=[
                SCALARS, SCALARS,
                pl.BlockSpec((1, 1, width, rank), lambda i, j: (i, j, 0, 0)),
                pl.BlockSpec((1, 1, rank, width), lambda i, j: (i, j, 0, 0)),
                pl.BlockSpec((1, width, rank), lambda i, j: (i, 0, 0)),
                pl.BlockSpec((1, width, rank), lambda i, j: (i, 0, 0)),
                pl.BlockSpec((1, rank, width), lambda i, j: (j, 0, 0)),
                pl.BlockSpec((1, rank, width), lambda i, j: (j, 0, 0)),
                WHOLE],
            out_specs=pl.BlockSpec((1, 1, width, width), lambda i, j: (i, j, 0, 0)),
            compiler_params=params(),
        )(panel_order, tile_ranks, tile_u, tile_v, uq1, uq2, vp1, vp2, cores)

    return on_device


def solution(mesh):
    placed = (P("row", "col", None, None), P("row", "col", None, None), P("row", "col"), P(), P())
    return jax.shard_map(
        make(mesh.shape["row"], mesh.shape["col"]),
        mesh=mesh,
        in_specs=placed,
        out_specs=P("row", "col", None, None),
        check_vma=False,
    )
```

```python
import functools

import jax
import jax.numpy as jnp
from jax import lax
from jax.experimental import pallas as pl
from jax.experimental.pallas import tpu as pltpu
from jax.sharding import PartitionSpec as P

F32 = jnp.float32
BF16 = jnp.bfloat16
VMEM_BYTES = 48 * 1024 * 1024
WHOLE = pl.BlockSpec(memory_space=pltpu.VMEM)
SCALARS = pl.BlockSpec(memory_space=pltpu.SMEM)


def params():
    return pltpu.CompilerParams(vmem_limit_bytes=VMEM_BYTES)


def dot(a, b):
    return jnp.dot(a, b, preferred_element_type=F32)


def swap(block, axis, n, bit, senders=None):
    senders = range(n) if senders is None else sorted(senders)
    return lax.ppermute(block, axis, [(s, s ^ bit) for s in senders])


def upper_bits(n):
    return [1 << b for b in range(1, n.bit_length() - 1)]


def after(value, *others):
    return lax.optimization_barrier((value,) + others)[0]


class Lane:
    def __init__(self, keep, give, axis, n, root):
        self.mine, self.axis, self.n, self.root = keep, axis, n, root
        self.me = lax.axis_index(axis)
        self.known = isinstance(root, int)
        self.holders = {root} if self.known else None
        self.bits = upper_bits(n)[::-1] if self.known else upper_bits(n)
        self.move(1, give)

    def move(self, bit, value):
        got = swap(value, self.axis, self.n, bit, self.holders)
        if self.known:
            self.holders = self.holders | {h ^ bit for h in self.holders}
        same = ((self.root ^ self.me) & bit) == 0
        if self.known and bit == 1:
            same = self.me != (self.root ^ 1)
        self.mine = jnp.where(same, self.mine, got)

    def step(self, k, *others):
        if others:
            self.mine = after(self.mine, *others)
        self.move(self.bits[k], self.mine)


def prep_kernel(order, ranks, u, v, *refs, last_row, last_col):
    rs_uk, rs_ug, rd_uk, rd_ug, rs_vk, rs_vg, rd_vk, rd_vg, c_k, c_g, held, v_sem, u_sems = refs
    rows, cols = u.shape[:2]
    rank, width = v.shape[2:]
    row_dyn = lax.rem(jnp.where(order[0, 0] == last_row, order[1, 0], order[0, 0]), rows)
    col_dyn = lax.rem(jnp.where(order[0, 1] == last_col, order[1, 1], order[0, 1]), cols)
    row_side = lax.rem(lax.axis_index("row"), 2)
    col_side = lax.rem(lax.axis_index("col"), 2)

    fetch = pltpu.make_async_copy(v, held, v_sem)
    fetch.start()
    copies = []
    for i, outs in ((rows - 1, (rs_uk, rs_ug)), (row_dyn, (rd_uk, rd_ug))):
        for slot, j in enumerate((row_side, 1 - row_side)):
            copies.append((u.at[i, j], outs[slot]))
    for which, j in enumerate((cols - 1, col_dyn)):
        for slot, i in enumerate((col_side, 1 - col_side)):
            copies.append((u.at[i, j], (c_k, c_g)[slot].at[which, 0]))
    copies = [pltpu.make_async_copy(a, b, u_sems.at[k]) for k, (a, b) in enumerate(copies)]
    for copy in copies:
        copy.start()
    fetch.wait()

    def kept(i, j):
        row = lax.broadcasted_iota(jnp.int32, (rank, width), 0)
        return jnp.where(row < ranks[i, j], held[i, j], jnp.zeros((), v.dtype))

    for i, outs in ((rows - 1, (rs_vk, rs_vg)), (row_dyn, (rd_vk, rd_vg))):
        for slot, j in enumerate((row_side, 1 - row_side)):
            outs[slot][...] = kept(i, j)
    for which, j in enumerate((cols - 1, col_dyn)):
        for slot, i in enumerate((col_side, 1 - col_side)):
            value = kept(i, j)
            for k in range(width // rank):
                (c_k, c_g)[slot][which, 1, k * rank:(k + 1) * rank, :] = value[:, k * rank:(k + 1) * rank]
    for copy in copies:
        copy.wait()


def solve_kernel(order, inverses, fixed, moving, out, *, last_row):
    fixed_first = order[0, 0] == last_row
    out[0] = dot(inverses[0], jnp.where(fixed_first, fixed[...], moving[...])).astype(BF16)
    out[1] = dot(inverses[1], jnp.where(fixed_first, moving[...], fixed[...])).astype(BF16)


def core_kernel(order, solved, swapped, first, second, v21, v12, out, edge, *, last_col):
    rank, width = v21.shape
    count = width // rank
    swap_first = lax.rem(lax.axis_index("row"), 2) == 1
    step_of = jnp.where(order[0, 1] == last_col, 0, 1)
    for s, more in enumerate((v21, v12)):
        which = step_of if s == 0 else 1 - step_of
        lines = [jnp.concatenate([tiles[which, 1, k * rank:(k + 1) * rank, :] for k in range(count)], axis=1) for tiles in (first, second)]
        tall = jnp.concatenate(lines + [more[...]], axis=0)
        mine, other = solved[s], swapped[s]
        wide = jnp.concatenate([jnp.where(swap_first, other, mine), jnp.where(swap_first, mine, other)], axis=1)
        got = dot(tall, wide).astype(BF16)
        out[s] = got
        late = lax.rem(order[1 - s, 1], 2) == 1
        pivot = jnp.where(late, got[:, rank:], got[:, :rank])
        if s == 0:
            edge[:2 * rank] = pivot[:2 * rank]
        else:
            edge[2 * rank:] = pivot


def final_kernel(order, ranks, u, v, first, second, vp1, vp2, cores, edge, out, *, last_col):
    i, j = pl.program_id(0), pl.program_id(1)
    rank, width = v.shape[2:]
    row = lax.axis_index("row") * pl.num_programs(0) + i
    col = lax.axis_index("col") * pl.num_programs(1) + j
    open1 = jnp.logical_and(row != order[0, 0], col != order[0, 1])
    open2 = jnp.logical_and(open1, jnp.logical_and(row != order[1, 0], col != order[1, 1]))
    m1 = jnp.where(open1, F32(1), F32(0))
    m2 = jnp.where(open2, F32(1), F32(0))
    foot = (cores.shape[1] // rank - 1) * rank
    top = pl.ds(pl.multiple_of(i * rank, rank), rank)
    below = pl.ds(pl.multiple_of(2 * rank + i * rank, rank), rank)

    def left(s, lines):
        return jnp.where(j == 0, cores[s, lines, :rank], cores[s, lines, rank:])

    c1_ij, c1_iq2, c1_p2j = left(0, top), edge[top], left(0, pl.ds(foot, rank))
    high_a, high_b = left(1, top), edge[below]
    low_a = -dot(c1_iq2, left(1, pl.ds(foot, rank)))
    low_b = -dot(c1_iq2, edge[4 * rank:])
    q1p1 = m2 * dot(low_b.astype(BF16), c1_p2j) - m1 * c1_ij.astype(F32)
    q2p1 = m2 * dot(high_b, c1_p2j)
    mix = jnp.concatenate([
        jnp.concatenate([q1p1, -m2 * low_a], axis=1),
        jnp.concatenate([q2p1, -m2 * high_a.astype(F32)], axis=1)], axis=0).astype(BF16)
    change = dot(mix, jnp.concatenate([vp1[0], vp2[0]], axis=0)).astype(BF16)
    line = lax.broadcasted_iota(jnp.int32, (rank, width), 0)
    own = jnp.where(line < ranks[i, j], v[0, 0], jnp.zeros((), BF16))
    right = jnp.concatenate([own, change], axis=0)
    w1 = jnp.where(order[0, 1] == last_col, 0, 1)
    uq1, uq2 = (jnp.where(i == 0, first[w, 0], second[w, 0]) for w in (w1, 1 - w1))
    out[0, 0] = dot(jnp.concatenate([u[0, 0], uq1, uq2], axis=1), right).astype(BF16)


def make(rows_n, cols_n):
    def on_device(tile_u, tile_v, tile_ranks, inverses, panel_order):
        rows, cols, width, rank = tile_u.shape
        last = dict(last_row=rows_n * rows - 1, last_col=cols_n * cols - 1)
        me_row, me_col = lax.axis_index("row"), lax.axis_index("col")
        q1, q2 = panel_order[0, 1], panel_order[1, 1]
        row_first = panel_order[0, 0] == last["last_row"]
        col_first = q1 == last["last_col"]
        row_root = jnp.where(row_first, panel_order[1, 0], panel_order[0, 0]) // rows
        col_root = jnp.where(col_first, q2, q1) // cols
        side_r, side_c = me_row % 2, me_col % 2

        tall = jax.ShapeDtypeStruct((width, rank), BF16)
        flat = jax.ShapeDtypeStruct((rank, width), BF16)
        quad = jax.ShapeDtypeStruct((2, 2, width, rank), BF16)
        anywhere = pl.BlockSpec(memory_space=pl.ANY)
        cut = pl.pallas_call(
            functools.partial(prep_kernel, **last),
            out_shape=[tall] * 4 + [flat] * 4 + [quad] * 2,
            in_specs=[SCALARS, SCALARS, anywhere, anywhere],
            out_specs=[WHOLE] * 10,
            scratch_shapes=[pltpu.VMEM(tile_v.shape, BF16), pltpu.SemaphoreType.DMA(()), pltpu.SemaphoreType.DMA((8,))],
            compiler_params=params(),
        )(panel_order, tile_ranks, tile_u, tile_v)
        rs_uk, rs_ug, rd_uk, rd_ug, rs_vk, rs_vg, rd_vk, rd_vg, c_k, c_g = cut

        def lanes(fixed_keep, fixed_give, moving_keep, moving_give):
            return (Lane(fixed_keep, fixed_give, "row", rows_n, rows_n - 1),
                    Lane(moving_keep, moving_give, "row", rows_n, row_root))

        def by_col(keep, give, roots):
            lane = Lane(keep, give, "col", cols_n, roots)
            for k in range(len(lane.bits)):
                lane.step(k)
            other = swap(lane.mine, "col", cols_n, 1)
            return jnp.where(side_c == 0, lane.mine, other), jnp.where(side_c == 0, other, lane.mine)

        def cross(one, two):
            shape = one.shape[1:]
            cand = jnp.stack([jnp.where(q1 % cols == 0, two[0], two[1]), jnp.where(q2 % cols == 0, one[0], one[1])])
            cand = cand.reshape(2, 2, shape[0] // 2, shape[1])
            keep = jnp.where(side_c == 0, cand[:, 0], cand[:, 1])
            give = jnp.where(side_c == 0, cand[:, 1], cand[:, 0])
            both = jnp.concatenate(by_col(keep, give, jnp.stack([q1 // cols, q2 // cols])[:, None, None]), axis=1)
            return both[0], both[1]

        v_lanes = lanes(rs_vk, rs_vg, rd_vk, rd_vg)
        arrived = [lane.mine for lane in v_lanes]
        u_lanes = lanes(rs_uk, after(rs_ug, *arrived), rd_uk, after(rd_ug, *arrived))
        first, second = by_col(c_k, after(c_g, arrived[1]), jnp.stack([cols_n - 1, col_root])[:, None, None, None])
        for k in range(len(upper_bits(rows_n))):
            for lane in v_lanes:
                lane.step(k)
            arrived = [lane.mine for lane in v_lanes]
            for lane in u_lanes:
                lane.step(k, *arrived)
        fixed, moving = arrived
        mine = jnp.stack([jnp.where(row_first, fixed, moving), jnp.where(row_first, moving, fixed)])
        other = swap(mine, "row", rows_n, 1)
        vp1, vp2 = (jnp.stack([jnp.where(side_r == 0, mine[s], other[s]), jnp.where(side_r == 0, other[s], mine[s])]) for s in range(2))
        v21, v12 = cross(vp1, vp2)

        solved = pl.pallas_call(
            functools.partial(solve_kernel, last_row=last["last_row"]),
            out_shape=jax.ShapeDtypeStruct((2, width, rank), BF16),
            in_specs=[SCALARS] + [WHOLE] * 3,
            out_specs=WHOLE,
            compiler_params=params(),
        )(panel_order, inverses, u_lanes[0].mine, u_lanes[1].mine)
        swapped = swap(solved, "row", rows_n, 1)
        cores, edge = pl.pallas_call(
            functools.partial(core_kernel, last_col=last["last_col"]),
            out_shape=[jax.ShapeDtypeStruct((2, 3 * rank, 2 * rank), BF16), jax.ShapeDtypeStruct((5 * rank, rank), BF16)],
            in_specs=[SCALARS] + [WHOLE] * 6,
            out_specs=[WHOLE] * 2,
            compiler_params=params(),
        )(panel_order, solved, swapped, first, second, v21, v12)
        edge_root = jnp.where(jnp.arange(5 * rank)[:, None] < 2 * rank, q2 // cols, q1 // cols)
        for bit in [1] + upper_bits(cols_n):
            got = swap(edge, "col", cols_n, bit)
            edge = jnp.where(((edge_root ^ me_col) & bit) == 0, edge, got)

        return pl.pallas_call(
            functools.partial(final_kernel, last_col=last["last_col"]),
            out_shape=jax.ShapeDtypeStruct((rows, cols, width, width), BF16),
            grid=(rows, cols),
            in_specs=[
                SCALARS, SCALARS,
                pl.BlockSpec((1, 1, width, rank), lambda i, j: (i, j, 0, 0)),
                pl.BlockSpec((1, 1, rank, width), lambda i, j: (i, j, 0, 0)),
                WHOLE, WHOLE,
                pl.BlockSpec((1, rank, width), lambda i, j: (j, 0, 0)),
                pl.BlockSpec((1, rank, width), lambda i, j: (j, 0, 0)),
                WHOLE, WHOLE],
            out_specs=pl.BlockSpec((1, 1, width, width), lambda i, j: (i, j, 0, 0)),
            compiler_params=params(),
        )(panel_order, tile_ranks, tile_u, tile_v, first, second, vp1, vp2, cores, edge)

    return on_device


def solution(mesh):
    placed = (P("row", "col", None, None), P("row", "col", None, None), P("row", "col"), P(), P())
    return jax.shard_map(
        make(mesh.shape["row"], mesh.shape["col"]),
        mesh=mesh,
        in_specs=placed,
        out_specs=P("row", "col", None, None),
        check_vma=False,
    )
```

```python
import functools

import jax
import jax.numpy as jnp
from jax import lax
from jax.experimental import pallas as pl
from jax.experimental.pallas import tpu as pltpu
from jax.sharding import PartitionSpec as P

F32 = jnp.float32
BF16 = jnp.bfloat16
VMEM_BYTES = 48 * 1024 * 1024
WHOLE = pl.BlockSpec(memory_space=pltpu.VMEM)
SCALARS = pl.BlockSpec(memory_space=pltpu.SMEM)


def params():
    return pltpu.CompilerParams(vmem_limit_bytes=VMEM_BYTES)


def dot(a, b):
    return jnp.dot(a, b, preferred_element_type=F32)


def swap(block, axis, n, bit, senders=None):
    senders = range(n) if senders is None else sorted(senders)
    return lax.ppermute(block, axis, [(s, s ^ bit) for s in senders])


def upper_bits(n):
    return [1 << b for b in range(1, n.bit_length() - 1)]


def after(value, *others):
    return lax.optimization_barrier((value,) + others)[0]


def all_bits(n):
    return [1] + upper_bits(n)


class Lane:
    def __init__(self, keep, give, axis, n, same, root=None, got=None):
        self.mine, self.axis, self.n, self.same = keep, axis, n, same
        self.holders = None if root is None else {root}
        self.bits = upper_bits(n) if root is None else upper_bits(n)[::-1]
        self.move(1, give, got)

    def move(self, bit, value, got=None):
        got = swap(value, self.axis, self.n, bit, self.holders) if got is None else got
        if self.holders:
            self.holders = self.holders | {h ^ bit for h in self.holders}
        self.mine = jnp.where(self.same(bit, self.mine), self.mine, got)

    def step(self, k, *others):
        if others:
            self.mine = after(self.mine, *others)
        self.move(self.bits[k], self.mine)


def flag_names(rows_n, cols_n):
    names = ["row_first", "side_r", "side_c", "q1_low", "q2_low"]
    names += [(kind, bit) for kind in ("rs", "rd") for bit in all_bits(rows_n)]
    names += [(kind, bit) for kind in ("cs", "cd", "q1", "q2") for bit in all_bits(cols_n)]
    return names


def prep_kernel(order, ranks, u, v, *refs, rows_n, cols_n):
    flags, rs_uk, rs_ug, rd_uk, rd_ug, rs_vk, rs_vg, rd_vk, rd_vg, c_k, c_g, held, v_sem, u_sems = refs
    rows, cols = u.shape[:2]
    rank, width = v.shape[2:]
    me_row, me_col = lax.axis_index("row"), lax.axis_index("col")
    row_first = order[0, 0] == rows_n * rows - 1
    row_other = jnp.where(row_first, order[1, 0], order[0, 0])
    col_other = jnp.where(order[0, 1] == cols_n * cols - 1, order[1, 1], order[0, 1])
    row_dyn, col_dyn = lax.rem(row_other, rows), lax.rem(col_other, cols)
    row_side, col_side = lax.rem(me_row, 2), lax.rem(me_col, 2)

    fetch = pltpu.make_async_copy(v, held, v_sem)
    fetch.start()
    copies = []
    for i, outs in ((rows - 1, (rs_uk, rs_ug)), (row_dyn, (rd_uk, rd_ug))):
        for slot, j in enumerate((row_side, 1 - row_side)):
            copies.append((u.at[i, j], outs[slot]))
    for which, j in enumerate((cols - 1, col_dyn)):
        for slot, i in enumerate((col_side, 1 - col_side)):
            copies.append((u.at[i, j], (c_k, c_g)[slot].at[which, 0]))
    copies = [pltpu.make_async_copy(a, b, u_sems.at[k]) for k, (a, b) in enumerate(copies)]
    for copy in copies:
        copy.start()

    q1, q2 = order[0, 1], order[1, 1]
    truth = {
        "row_first": row_first, "side_r": row_side == 0, "side_c": col_side == 0,
        "q1_low": lax.rem(q1, cols) == 0, "q2_low": lax.rem(q2, cols) == 0}
    for bit in all_bits(rows_n):
        truth["rs", bit] = (me_row & bit) == (rows_n - 1) & bit
        truth["rd", bit] = (me_row & bit) == (lax.div(row_other, rows) & bit)
    truth["rs", 1] = me_row != (rows_n - 1) ^ 1
    for bit in all_bits(cols_n):
        truth["cs", bit] = (me_col & bit) == (cols_n - 1) & bit
        for kind, where in (("cd", col_other), ("q1", q1), ("q2", q2)):
            truth[kind, bit] = (me_col & bit) == (lax.div(where, cols) & bit)
    for k, name in enumerate(flag_names(rows_n, cols_n)):
        flags[k:k + 1, :] = jnp.full((1, width), jnp.where(truth[name], 1, 0), jnp.int32)
    fetch.wait()

    def kept(i, j):
        row = lax.broadcasted_iota(jnp.int32, (rank, width), 0)
        return jnp.where(row < ranks[i, j], held[i, j], jnp.zeros((), v.dtype))

    for i, outs in ((rows - 1, (rs_vk, rs_vg)), (row_dyn, (rd_vk, rd_vg))):
        for slot, j in enumerate((row_side, 1 - row_side)):
            outs[slot][...] = kept(i, j)
    for which, j in enumerate((cols - 1, col_dyn)):
        for slot, i in enumerate((col_side, 1 - col_side)):
            value = kept(i, j)
            for k in range(width // rank):
                (c_k, c_g)[slot][which, 1, k * rank:(k + 1) * rank, :] = value[:, k * rank:(k + 1) * rank]
    for copy in copies:
        copy.wait()


def solve_kernel(order, inverses, fixed, moving, out, *, last_row):
    fixed_first = order[0, 0] == last_row
    out[0] = dot(inverses[0], jnp.where(fixed_first, fixed[...], moving[...])).astype(BF16)
    out[1] = dot(inverses[1], jnp.where(fixed_first, moving[...], fixed[...])).astype(BF16)


def core_kernel(order, solved, swapped, first, second, v21, v12, out, edge, *, last_col):
    rank, width = v21.shape
    count = width // rank
    swap_first = lax.rem(lax.axis_index("row"), 2) == 1
    step_of = jnp.where(order[0, 1] == last_col, 0, 1)
    for s, more in enumerate((v21, v12)):
        which = step_of if s == 0 else 1 - step_of
        lines = [jnp.concatenate([tiles[which, 1, k * rank:(k + 1) * rank, :] for k in range(count)], axis=1) for tiles in (first, second)]
        tall = jnp.concatenate(lines + [more[...]], axis=0)
        mine, other = solved[s], swapped[s]
        wide = jnp.concatenate([jnp.where(swap_first, other, mine), jnp.where(swap_first, mine, other)], axis=1)
        got = dot(tall, wide).astype(BF16)
        out[s] = got
        late = lax.rem(order[1 - s, 1], 2) == 1
        pivot = jnp.where(late, got[:, rank:], got[:, :rank])
        if s == 0:
            edge[:2 * rank] = pivot[:2 * rank]
        else:
            edge[2 * rank:] = pivot


def final_kernel(order, ranks, u, v, first, second, vp1, vp2, cores, edge, out, *, last_col):
    i, j = pl.program_id(0), pl.program_id(1)
    rank, width = v.shape[2:]
    row = lax.axis_index("row") * pl.num_programs(0) + i
    col = lax.axis_index("col") * pl.num_programs(1) + j
    open1 = jnp.logical_and(row != order[0, 0], col != order[0, 1])
    open2 = jnp.logical_and(open1, jnp.logical_and(row != order[1, 0], col != order[1, 1]))
    m1 = jnp.where(open1, F32(1), F32(0))
    m2 = jnp.where(open2, F32(1), F32(0))
    foot = (cores.shape[1] // rank - 1) * rank
    top = pl.ds(pl.multiple_of(i * rank, rank), rank)
    below = pl.ds(pl.multiple_of(2 * rank + i * rank, rank), rank)

    def left(s, lines):
        return jnp.where(j == 0, cores[s, lines, :rank], cores[s, lines, rank:])

    c1_ij, c1_iq2, c1_p2j = left(0, top), edge[top], left(0, pl.ds(foot, rank))
    high_a, high_b = left(1, top), edge[below]
    low_a = -dot(c1_iq2, left(1, pl.ds(foot, rank)))
    low_b = -dot(c1_iq2, edge[4 * rank:])
    q1p1 = m2 * dot(low_b.astype(BF16), c1_p2j) - m1 * c1_ij.astype(F32)
    q2p1 = m2 * dot(high_b, c1_p2j)
    mix = jnp.concatenate([
        jnp.concatenate([q1p1, -m2 * low_a], axis=1),
        jnp.concatenate([q2p1, -m2 * high_a.astype(F32)], axis=1)], axis=0).astype(BF16)
    change = dot(mix, jnp.concatenate([vp1[0], vp2[0]], axis=0)).astype(BF16)
    line = lax.broadcasted_iota(jnp.int32, (rank, width), 0)
    own = jnp.where(line < ranks[i, j], v[0, 0], jnp.zeros((), BF16))
    right = jnp.concatenate([own, change], axis=0)
    w1 = jnp.where(order[0, 1] == last_col, 0, 1)
    uq1, uq2 = (jnp.where(i == 0, first[w, 0], second[w, 0]) for w in (w1, 1 - w1))
    out[0, 0] = dot(jnp.concatenate([u[0, 0], uq1, uq2], axis=1), right).astype(BF16)


def make(rows_n, cols_n):
    def on_device(tile_u, tile_v, tile_ranks, inverses, panel_order):
        rows, cols, width, rank = tile_u.shape
        last = dict(last_row=rows_n * rows - 1, last_col=cols_n * cols - 1)
        tall = jax.ShapeDtypeStruct((width, rank), BF16)
        flat = jax.ShapeDtypeStruct((rank, width), BF16)
        quad = jax.ShapeDtypeStruct((2, 2, width, rank), BF16)
        anywhere = pl.BlockSpec(memory_space=pl.ANY)
        names = flag_names(rows_n, cols_n)
        cut = pl.pallas_call(
            functools.partial(prep_kernel, rows_n=rows_n, cols_n=cols_n),
            out_shape=[jax.ShapeDtypeStruct((len(names), width), jnp.int32)] + [tall] * 4 + [flat] * 4 + [quad] * 2,
            in_specs=[SCALARS, SCALARS, anywhere, anywhere],
            out_specs=[WHOLE] * 11,
            scratch_shapes=[pltpu.VMEM(tile_v.shape, BF16), pltpu.SemaphoreType.DMA(()), pltpu.SemaphoreType.DMA((8,))],
            compiler_params=params(),
        )(panel_order, tile_ranks, tile_u, tile_v)
        flags, rs_uk, rs_ug, rd_uk, rd_ug, rs_vk, rs_vg, rd_vk, rd_vg, c_k, c_g = cut

        def flag(name, like):
            k = names.index(name)
            return flags[k:k + 1, :like.shape[-1]] != 0

        def choose(name, one, two):
            return jnp.where(flag(name, one), one, two)

        def same(kind):
            return lambda bit, like: flag((kind, bit), like)

        def lanes(fixed_keep, fixed_give, moving_keep, moving_give):
            return (Lane(moving_keep, moving_give, "row", rows_n, same("rd")),
                    Lane(fixed_keep, fixed_give, "row", rows_n, same("rs"), rows_n - 1))

        def joined(mine, axis, n, side):
            other = swap(mine, axis, n, 1)
            return choose(side, mine, other), choose(side, other, mine)

        def both_q(bit, like):
            return jnp.stack([flag(("q1", bit), like), flag(("q2", bit), like)])

        def cross(one, two):
            shape = one.shape[1:]
            cand = jnp.stack([choose("q1_low", two[0], two[1]), choose("q2_low", one[0], one[1])])
            cand = cand.reshape(2, 2, shape[0] // 2, shape[1])
            lane = Lane(choose("side_c", cand[:, 0], cand[:, 1]), choose("side_c", cand[:, 1], cand[:, 0]), "col", cols_n, both_q)
            for k in range(len(lane.bits)):
                lane.step(k)
            both = jnp.concatenate(joined(lane.mine, "col", cols_n, "side_c"), axis=1)
            return both[0], both[1]

        v_lanes = lanes(rs_vk, rs_vg, rd_vk, rd_vg)
        c_got = swap(c_g, "col", cols_n, 1)
        c_lanes = [Lane(c_k[k], None, "col", cols_n, same(kind), got=c_got[k]) for k, kind in enumerate(("cs", "cd"))]
        arrived = [lane.mine for lane in v_lanes]
        u_lanes = lanes(rs_uk, after(rs_ug, *arrived), rd_uk, after(rd_ug, *arrived))

        mark = []
        ties = [lane.mine for lane in c_lanes]
        for k in range(len(upper_bits(rows_n))):
            for lane in v_lanes:
                lane.step(k, *ties)
            if k == 0:
                for lane, before in zip(c_lanes, ((), (c_lanes[0],))):
                    for m in range(len(lane.bits)):
                        lane.step(m, *(other.mine for other in before))
                ties = [lane.mine for lane in u_lanes] + [c_lanes[0].mine]
            arrived = [lane.mine for lane in v_lanes]
            if k > 0:
                ties = [lane.mine for lane in u_lanes]
                mark = ties
            for lane in u_lanes:
                lane.step(k, *arrived)
            if k == 0:
                mark = [lane.mine for lane in u_lanes]
        moving, fixed = (after(x, *mark, c_lanes[1].mine) for x in arrived)
        mine = jnp.stack([choose("row_first", fixed, moving), choose("row_first", moving, fixed)])
        vj0, vj1 = joined(mine, "row", rows_n, "side_r")
        vp1, vp2 = (jnp.stack([vj0[s], vj1[s]]) for s in range(2))
        first, second = joined(jnp.stack([lane.mine for lane in c_lanes]), "col", cols_n, "side_c")
        waits = [lane.mine for lane in u_lanes]
        v21, v12 = cross(after(vp1, *waits), after(vp2, *waits))

        solved = pl.pallas_call(
            functools.partial(solve_kernel, last_row=last["last_row"]),
            out_shape=jax.ShapeDtypeStruct((2, width, rank), BF16),
            in_specs=[SCALARS] + [WHOLE] * 3,
            out_specs=WHOLE,
            compiler_params=params(),
        )(panel_order, inverses, u_lanes[1].mine, u_lanes[0].mine)
        swapped = swap(solved, "row", rows_n, 1)
        cores, edge = pl.pallas_call(
            functools.partial(core_kernel, last_col=last["last_col"]),
            out_shape=[jax.ShapeDtypeStruct((2, 3 * rank, 2 * rank), BF16), jax.ShapeDtypeStruct((5 * rank, rank), BF16)],
            in_specs=[SCALARS] + [WHOLE] * 6,
            out_specs=[WHOLE] * 2,
            compiler_params=params(),
        )(panel_order, solved, swapped, first, second, v21, v12)
        for bit in all_bits(cols_n):
            got = swap(edge, "col", cols_n, bit)
            early = jnp.arange(5 * rank)[:, None] < 2 * rank
            stays = jnp.where(early, flag(("q2", bit), edge), flag(("q1", bit), edge))
            edge = jnp.where(stays, edge, got)

        return pl.pallas_call(
            functools.partial(final_kernel, last_col=last["last_col"]),
            out_shape=jax.ShapeDtypeStruct((rows, cols, width, width), BF16),
            grid=(rows, cols),
            in_specs=[
                SCALARS, SCALARS,
                pl.BlockSpec((1, 1, width, rank), lambda i, j: (i, j, 0, 0)),
                pl.BlockSpec((1, 1, rank, width), lambda i, j: (i, j, 0, 0)),
                WHOLE, WHOLE,
                pl.BlockSpec((1, rank, width), lambda i, j: (j, 0, 0)),
                pl.BlockSpec((1, rank, width), lambda i, j: (j, 0, 0)),
                WHOLE, WHOLE],
            out_specs=pl.BlockSpec((1, 1, width, width), lambda i, j: (i, j, 0, 0)),
            compiler_params=params(),
        )(panel_order, tile_ranks, tile_u, tile_v, first, second, vp1, vp2, cores, edge)

    return on_device


def solution(mesh):
    placed = (P("row", "col", None, None), P("row", "col", None, None), P("row", "col"), P(), P())
    return jax.shard_map(
        make(mesh.shape["row"], mesh.shape["col"]),
        mesh=mesh,
        in_specs=placed,
        out_specs=P("row", "col", None, None),
        check_vma=False,
    )
```

```python
import functools

import jax
import jax.numpy as jnp
from jax import lax
from jax.experimental import pallas as pl
from jax.experimental.pallas import tpu as pltpu
from jax.sharding import PartitionSpec as P

F32 = jnp.float32
BF16 = jnp.bfloat16
BRANCHES = 8
VMEM_BYTES = 48 * 1024 * 1024
WHOLE = pl.BlockSpec(memory_space=pltpu.VMEM)
SCALARS = pl.BlockSpec(memory_space=pltpu.SMEM)


def params():
    return pltpu.CompilerParams(vmem_limit_bytes=VMEM_BYTES)


def dot(a, b):
    return jnp.dot(a, b, preferred_element_type=F32)


def swap(block, axis, n, bit, senders=None):
    senders = range(n) if senders is None else sorted(senders)
    return lax.ppermute(block, axis, [(s, s ^ bit) for s in senders])


def upper_bits(n):
    return [1 << b for b in range(1, n.bit_length() - 1)]


def after(value, *others):
    return lax.optimization_barrier((value,) + others)[0]


def all_bits(n):
    return [1] + upper_bits(n)


class Lane:
    def __init__(self, keep, give, axis, n, same, root=None, got=None):
        self.mine, self.axis, self.n, self.same = keep, axis, n, same
        self.holders = None if root is None else {root}
        self.bits = upper_bits(n) if root is None else upper_bits(n)[::-1]
        self.move(1, give, got)

    def move(self, bit, value, got=None):
        got = swap(value, self.axis, self.n, bit, self.holders) if got is None else got
        if self.holders:
            self.holders = self.holders | {h ^ bit for h in self.holders}
        self.mine = jnp.where(self.same(bit, self.mine), self.mine, got)

    def step(self, k, *others):
        if others:
            self.mine = after(self.mine, *others)
        self.move(self.bits[k], self.mine)


class KnownPair:
    def __init__(self, keeps, gives, axis, n, roots, member):
        self.mine, self.axis, self.n, self.member = list(keeps), axis, n, member
        self.holders = [{r} for r in roots]
        self.bits = upper_bits(n)[::-1]
        self.move(1, gives)

    def move(self, bit, values):
        one, two = self.holders
        if one & two:
            got = [swap(v, self.axis, self.n, bit, h) for v, h in zip(values, self.holders)]
        else:
            both = jnp.where(self.member(two, values[1]), values[1], values[0])
            got = [swap(both, self.axis, self.n, bit, one | two)] * 2
        targets = [{h ^ bit for h in hold} for hold in self.holders]
        self.mine = [jnp.where(self.member(t, m), g, m) for t, g, m in zip(targets, got, self.mine)]
        self.holders = [h | t for h, t in zip(self.holders, targets)]

    def step(self, k, *others):
        if others:
            self.mine = [after(m, *others) for m in self.mine]
        self.move(self.bits[k], self.mine)


class MovingPair:
    def __init__(self, *lanes):
        self.lanes = lanes

    @property
    def mine(self):
        return [lane.mine for lane in self.lanes]

    def step(self, k, *others):
        for lane in self.lanes:
            lane.step(k, *others)


def flag_names(rows_n, cols_n):
    names = ["row_first", "side_r", "side_c", "q1_low", "q2_low"]
    names += [("at", d) for d in range(rows_n if rows_n <= BRANCHES else 0)]
    names += [(kind, bit) for kind in ("rs", "rd") for bit in all_bits(rows_n)]
    names += [(kind, bit) for kind in ("cs", "cd", "q1", "q2") for bit in all_bits(cols_n)]
    return names


def prep_kernel(order, ranks, u, v, *refs, rows_n, cols_n):
    flags, rs_uk, rs_ug, rd_uk, rd_ug, rs_vk, rs_vg, rd_vk, rd_vg, c_k, c_g, held, v_sem, u_sems = refs
    rows, cols = u.shape[:2]
    rank, width = v.shape[2:]
    me_row, me_col = lax.axis_index("row"), lax.axis_index("col")
    row_first = order[0, 0] == rows_n * rows - 1
    row_other = jnp.where(row_first, order[1, 0], order[0, 0])
    col_other = jnp.where(order[0, 1] == cols_n * cols - 1, order[1, 1], order[0, 1])
    row_dyn, col_dyn = lax.rem(row_other, rows), lax.rem(col_other, cols)
    row_side, col_side = lax.rem(me_row, 2), lax.rem(me_col, 2)

    fetch = pltpu.make_async_copy(v, held, v_sem)
    fetch.start()
    copies = []
    for i, outs in ((rows - 1, (rs_uk, rs_ug)), (row_dyn, (rd_uk, rd_ug))):
        for slot, j in enumerate((row_side, 1 - row_side)):
            copies.append((u.at[i, j], outs[slot]))
    for which, j in enumerate((cols - 1, col_dyn)):
        for slot, i in enumerate((col_side, 1 - col_side)):
            copies.append((u.at[i, j], (c_k, c_g)[slot].at[which, 0]))
    copies = [pltpu.make_async_copy(a, b, u_sems.at[k]) for k, (a, b) in enumerate(copies)]
    for copy in copies:
        copy.start()

    q1, q2 = order[0, 1], order[1, 1]
    truth = {
        "row_first": row_first, "side_r": row_side == 0, "side_c": col_side == 0,
        "q1_low": lax.rem(q1, cols) == 0, "q2_low": lax.rem(q2, cols) == 0}
    for bit in all_bits(rows_n):
        truth["rs", bit] = (me_row & bit) == (rows_n - 1) & bit
        truth["rd", bit] = (me_row & bit) == (lax.div(row_other, rows) & bit)
    for d in range(rows_n):
        truth["at", d] = me_row == d
    truth["rs", 1] = me_row != (rows_n - 1) ^ 1
    for bit in all_bits(cols_n):
        truth["cs", bit] = (me_col & bit) == (cols_n - 1) & bit
        for kind, where in (("cd", col_other), ("q1", q1), ("q2", q2)):
            truth[kind, bit] = (me_col & bit) == (lax.div(where, cols) & bit)
    for k, name in enumerate(flag_names(rows_n, cols_n)):
        flags[k:k + 1, :] = jnp.full((1, width), jnp.where(truth[name], 1, 0), jnp.int32)
    fetch.wait()

    def kept(i, j):
        row = lax.broadcasted_iota(jnp.int32, (rank, width), 0)
        return jnp.where(row < ranks[i, j], held[i, j], jnp.zeros((), v.dtype))

    for i, outs in ((rows - 1, (rs_vk, rs_vg)), (row_dyn, (rd_vk, rd_vg))):
        for slot, j in enumerate((row_side, 1 - row_side)):
            outs[slot][...] = kept(i, j)
    for which, j in enumerate((cols - 1, col_dyn)):
        for slot, i in enumerate((col_side, 1 - col_side)):
            value = kept(i, j)
            for k in range(width // rank):
                (c_k, c_g)[slot][which, 1, k * rank:(k + 1) * rank, :] = value[:, k * rank:(k + 1) * rank]
    for copy in copies:
        copy.wait()


def solve_kernel(order, inverses, fixed, moving, out, *, last_row):
    fixed_first = order[0, 0] == last_row
    out[0] = dot(inverses[0], jnp.where(fixed_first, fixed[...], moving[...])).astype(BF16)
    out[1] = dot(inverses[1], jnp.where(fixed_first, moving[...], fixed[...])).astype(BF16)


def core_kernel(order, solved, swapped, first, second, v21, v12, out, edge, *, last_col):
    rank, width = v21.shape
    count = width // rank
    swap_first = lax.rem(lax.axis_index("row"), 2) == 1
    step_of = jnp.where(order[0, 1] == last_col, 0, 1)
    for s, more in enumerate((v21, v12)):
        which = step_of if s == 0 else 1 - step_of
        lines = [jnp.concatenate([tiles[which, 1, k * rank:(k + 1) * rank, :] for k in range(count)], axis=1) for tiles in (first, second)]
        tall = jnp.concatenate(lines + [more[...]], axis=0)
        mine, other = solved[s], swapped[s]
        wide = jnp.concatenate([jnp.where(swap_first, other, mine), jnp.where(swap_first, mine, other)], axis=1)
        got = dot(tall, wide).astype(BF16)
        out[s] = got
        late = lax.rem(order[1 - s, 1], 2) == 1
        pivot = jnp.where(late, got[:, rank:], got[:, :rank])
        if s == 0:
            edge[:2 * rank] = pivot[:2 * rank]
        else:
            edge[2 * rank:] = pivot


def final_kernel(order, ranks, u, v, first, second, vp1, vp2, cores, edge, out, *, last_col):
    i, j = pl.program_id(0), pl.program_id(1)
    rank, width = v.shape[2:]
    row = lax.axis_index("row") * pl.num_programs(0) + i
    col = lax.axis_index("col") * pl.num_programs(1) + j
    open1 = jnp.logical_and(row != order[0, 0], col != order[0, 1])
    open2 = jnp.logical_and(open1, jnp.logical_and(row != order[1, 0], col != order[1, 1]))
    m1 = jnp.where(open1, F32(1), F32(0))
    m2 = jnp.where(open2, F32(1), F32(0))
    foot = (cores.shape[1] // rank - 1) * rank
    top = pl.ds(pl.multiple_of(i * rank, rank), rank)
    below = pl.ds(pl.multiple_of(2 * rank + i * rank, rank), rank)

    def left(s, lines):
        return jnp.where(j == 0, cores[s, lines, :rank], cores[s, lines, rank:])

    c1_ij, c1_iq2, c1_p2j = left(0, top), edge[top], left(0, pl.ds(foot, rank))
    high_a, high_b = left(1, top), edge[below]
    low_a = -dot(c1_iq2, left(1, pl.ds(foot, rank)))
    low_b = -dot(c1_iq2, edge[4 * rank:])
    q1p1 = m2 * dot(low_b.astype(BF16), c1_p2j) - m1 * c1_ij.astype(F32)
    q2p1 = m2 * dot(high_b, c1_p2j)
    mix = jnp.concatenate([
        jnp.concatenate([q1p1, -m2 * low_a], axis=1),
        jnp.concatenate([q2p1, -m2 * high_a.astype(F32)], axis=1)], axis=0).astype(BF16)
    change = dot(mix, jnp.concatenate([vp1[0], vp2[0]], axis=0)).astype(BF16)
    line = lax.broadcasted_iota(jnp.int32, (rank, width), 0)
    own = jnp.where(line < ranks[i, j], v[0, 0], jnp.zeros((), BF16))
    right = jnp.concatenate([own, change], axis=0)
    w1 = jnp.where(order[0, 1] == last_col, 0, 1)
    uq1, uq2 = (jnp.where(i == 0, first[w, 0], second[w, 0]) for w in (w1, 1 - w1))
    out[0, 0] = dot(jnp.concatenate([u[0, 0], uq1, uq2], axis=1), right).astype(BF16)


def rest(rows_n, cols_n, root, tile_u, tile_v, tile_ranks, inverses, panel_order, flags, *cut):
    rs_uk, rs_ug, rd_uk, rd_ug, rs_vk, rs_vg, rd_vk, rd_vg, c_k, c_g = cut
    rows, cols, width, rank = tile_u.shape
    last = dict(last_row=rows_n * rows - 1, last_col=cols_n * cols - 1)
    names = flag_names(rows_n, cols_n)

    def flag(name, like):
        k = names.index(name)
        return flags[k:k + 1, :like.shape[-1]] != 0

    def choose(name, one, two):
        return jnp.where(flag(name, one), one, two)

    def same(kind):
        return lambda bit, like: flag((kind, bit), like)

    def member(devices, like):
        return sum(flags[names.index(("at", d)), :like.shape[-1]] for d in sorted(devices)) != 0

    def pair(fixed_keep, fixed_give, moving_keep, moving_give):
        if root is None:
            return MovingPair(Lane(fixed_keep, fixed_give, "row", rows_n, same("rs"), rows_n - 1),
                              Lane(moving_keep, moving_give, "row", rows_n, same("rd")))
        return KnownPair((fixed_keep, moving_keep), (fixed_give, moving_give), "row", rows_n, (rows_n - 1, root), member)

    def joined(mine, axis, n, side):
        other = swap(mine, axis, n, 1)
        return choose(side, mine, other), choose(side, other, mine)

    def both_q(bit, like):
        return jnp.stack([flag(("q1", bit), like), flag(("q2", bit), like)])

    def cross(one, two):
        shape = one.shape[1:]
        cand = jnp.stack([choose("q1_low", two[0], two[1]), choose("q2_low", one[0], one[1])])
        cand = cand.reshape(2, 2, shape[0] // 2, shape[1])
        lane = Lane(choose("side_c", cand[:, 0], cand[:, 1]), choose("side_c", cand[:, 1], cand[:, 0]), "col", cols_n, both_q)
        for k in range(len(lane.bits)):
            lane.step(k)
        both = jnp.concatenate(joined(lane.mine, "col", cols_n, "side_c"), axis=1)
        return both[0], both[1]

    v_pair = pair(rs_vk, rs_vg, rd_vk, rd_vg)
    c_got = swap(c_g, "col", cols_n, 1)
    c_lanes = [Lane(c_k[k], None, "col", cols_n, same(kind), got=c_got[k]) for k, kind in enumerate(("cs", "cd"))]
    arrived = v_pair.mine
    u_pair = pair(rs_uk, after(rs_ug, *arrived), rd_uk, after(rd_ug, *arrived))

    mark = []
    ties = [lane.mine for lane in c_lanes]
    for k in range(len(upper_bits(rows_n))):
        v_pair.step(k, *ties)
        ties = list(u_pair.mine)
        if k == 0:
            for lane, before in zip(c_lanes, ((), (c_lanes[0],))):
                for m in range(len(lane.bits)):
                    lane.step(m, *(other.mine for other in before))
            ties.append(c_lanes[0].mine)
        else:
            mark = list(u_pair.mine)
        arrived = v_pair.mine
        u_pair.step(k, *arrived)
        if k == 0:
            mark = list(u_pair.mine)
    fixed, moving = (after(x, *mark, c_lanes[1].mine) for x in arrived)
    mine = jnp.stack([choose("row_first", fixed, moving), choose("row_first", moving, fixed)])
    vj0, vj1 = joined(mine, "row", rows_n, "side_r")
    vp1, vp2 = (jnp.stack([vj0[s], vj1[s]]) for s in range(2))
    first, second = joined(jnp.stack([lane.mine for lane in c_lanes]), "col", cols_n, "side_c")
    waits = u_pair.mine
    v21, v12 = cross(after(vp1, *waits), after(vp2, *waits))

    solved = pl.pallas_call(
        functools.partial(solve_kernel, last_row=last["last_row"]),
        out_shape=jax.ShapeDtypeStruct((2, width, rank), BF16),
        in_specs=[SCALARS] + [WHOLE] * 3,
        out_specs=WHOLE,
        compiler_params=params(),
    )(panel_order, inverses, *u_pair.mine)
    swapped = swap(solved, "row", rows_n, 1)
    cores, edge = pl.pallas_call(
        functools.partial(core_kernel, last_col=last["last_col"]),
        out_shape=[jax.ShapeDtypeStruct((2, 3 * rank, 2 * rank), BF16), jax.ShapeDtypeStruct((5 * rank, rank), BF16)],
        in_specs=[SCALARS] + [WHOLE] * 6,
        out_specs=[WHOLE] * 2,
        compiler_params=params(),
    )(panel_order, solved, swapped, first, second, v21, v12)
    for bit in all_bits(cols_n):
        got = swap(edge, "col", cols_n, bit)
        early = jnp.arange(5 * rank)[:, None] < 2 * rank
        stays = jnp.where(early, flag(("q2", bit), edge), flag(("q1", bit), edge))
        edge = jnp.where(stays, edge, got)

    return pl.pallas_call(
        functools.partial(final_kernel, last_col=last["last_col"]),
        out_shape=jax.ShapeDtypeStruct((rows, cols, width, width), BF16),
        grid=(rows, cols),
        in_specs=[
            SCALARS, SCALARS,
            pl.BlockSpec((1, 1, width, rank), lambda i, j: (i, j, 0, 0)),
            pl.BlockSpec((1, 1, rank, width), lambda i, j: (i, j, 0, 0)),
            WHOLE, WHOLE,
            pl.BlockSpec((1, rank, width), lambda i, j: (j, 0, 0)),
            pl.BlockSpec((1, rank, width), lambda i, j: (j, 0, 0)),
            WHOLE, WHOLE],
        out_specs=pl.BlockSpec((1, 1, width, width), lambda i, j: (i, j, 0, 0)),
        compiler_params=params(),
    )(panel_order, tile_ranks, tile_u, tile_v, first, second, vp1, vp2, cores, edge)


def make(rows_n, cols_n):
    def on_device(tile_u, tile_v, tile_ranks, inverses, panel_order):
        rows, cols, width, rank = tile_u.shape
        last = dict(last_row=rows_n * rows - 1, last_col=cols_n * cols - 1)
        tall = jax.ShapeDtypeStruct((width, rank), BF16)
        flat = jax.ShapeDtypeStruct((rank, width), BF16)
        quad = jax.ShapeDtypeStruct((2, 2, width, rank), BF16)
        anywhere = pl.BlockSpec(memory_space=pl.ANY)
        names = flag_names(rows_n, cols_n)
        cut = pl.pallas_call(
            functools.partial(prep_kernel, rows_n=rows_n, cols_n=cols_n),
            out_shape=[jax.ShapeDtypeStruct((len(names), width), jnp.int32)] + [tall] * 4 + [flat] * 4 + [quad] * 2,
            in_specs=[SCALARS, SCALARS, anywhere, anywhere],
            out_specs=[WHOLE] * 11,
            scratch_shapes=[pltpu.VMEM(tile_v.shape, BF16), pltpu.SemaphoreType.DMA(()), pltpu.SemaphoreType.DMA((8,))],
            compiler_params=params(),
        )(panel_order, tile_ranks, tile_u, tile_v)
        run = functools.partial(rest, rows_n, cols_n)
        operands = (tile_u, tile_v, tile_ranks, inverses, panel_order, *cut)
        if rows_n > BRANCHES:
            return run(None, *operands)
        other = jnp.where(panel_order[0, 0] == last["last_row"], panel_order[1, 0], panel_order[0, 0])
        return lax.switch(other // rows, [functools.partial(run, r) for r in range(rows_n)], *operands)

    return on_device


def solution(mesh):
    placed = (P("row", "col", None, None), P("row", "col", None, None), P("row", "col"), P(), P())
    return jax.shard_map(
        make(mesh.shape["row"], mesh.shape["col"]),
        mesh=mesh,
        in_specs=placed,
        out_specs=P("row", "col", None, None),
        check_vma=False,
    )
```

```python
import functools

import jax
import jax.numpy as jnp
from jax import lax
from jax.experimental import pallas as pl
from jax.experimental.pallas import tpu as pltpu
from jax.sharding import PartitionSpec as P

F32 = jnp.float32
BF16 = jnp.bfloat16
BRANCHES = 8
VMEM_BYTES = 48 * 1024 * 1024
VMEM_MOST = 54 * 1024 * 1024
WHOLE = pl.BlockSpec(memory_space=pltpu.VMEM)
SCALARS = pl.BlockSpec(memory_space=pltpu.SMEM)


def params(vmem=VMEM_BYTES):
    return pltpu.CompilerParams(vmem_limit_bytes=vmem)


def dot(a, b):
    return jnp.dot(a, b, preferred_element_type=F32)


def swap(block, axis, n, bit, senders=None):
    senders = range(n) if senders is None else sorted(senders)
    return lax.ppermute(block, axis, [(s, s ^ bit) for s in senders])


def upper_bits(n):
    return [1 << b for b in range(1, n.bit_length() - 1)]


def after(value, *others):
    return lax.optimization_barrier((value,) + others)[0]


def all_bits(n):
    return [1] + upper_bits(n)


class Lane:
    def __init__(self, keep, give, axis, n, same, root=None, got=None):
        self.mine, self.axis, self.n, self.same = keep, axis, n, same
        self.holders = None if root is None else {root}
        self.bits = upper_bits(n) if root is None else upper_bits(n)[::-1]
        self.move(1, give, got)

    def move(self, bit, value, got=None):
        got = swap(value, self.axis, self.n, bit, self.holders) if got is None else got
        if self.holders:
            self.holders = self.holders | {h ^ bit for h in self.holders}
        self.mine = jnp.where(self.same(bit, self.mine), self.mine, got)

    def step(self, k, *others):
        if others:
            self.mine = after(self.mine, *others)
        self.move(self.bits[k], self.mine)


class KnownPair:
    def __init__(self, keeps, gives, axis, n, roots, member):
        self.mine, self.axis, self.n, self.member = list(keeps), axis, n, member
        self.holders = [{r} for r in roots]
        self.bits = upper_bits(n)[::-1]
        self.move(1, gives)

    def move(self, bit, values):
        one, two = self.holders
        if one & two:
            got = [swap(v, self.axis, self.n, bit, h) for v, h in zip(values, self.holders)]
        else:
            both = jnp.where(self.member(two, values[1]), values[1], values[0])
            got = [swap(both, self.axis, self.n, bit, one | two)] * 2
        targets = [{h ^ bit for h in hold} for hold in self.holders]
        self.mine = [jnp.where(self.member(t, m), g, m) for t, g, m in zip(targets, got, self.mine)]
        self.holders = [h | t for h, t in zip(self.holders, targets)]

    def step(self, k, *others):
        if others:
            self.mine = [after(m, *others) for m in self.mine]
        self.move(self.bits[k], self.mine)


class MovingPair:
    def __init__(self, *lanes):
        self.lanes = lanes

    @property
    def mine(self):
        return [lane.mine for lane in self.lanes]

    def step(self, k, *others):
        for lane in self.lanes:
            lane.step(k, *others)


def flag_names(rows_n, cols_n):
    names = ["row_first", "side_r", "side_c", "q1_low", "q2_low"]
    names += [("at", d) for d in range(rows_n if rows_n <= BRANCHES else 0)]
    names += [(kind, bit) for kind in ("rs", "rd") for bit in all_bits(rows_n)]
    names += [(kind, bit) for kind in ("cs", "cd", "q1", "q2") for bit in all_bits(cols_n)]
    return names


def prep_kernel(order, ranks, u, v, *refs, rows_n, cols_n):
    flags, rs_uk, rs_ug, rd_uk, rd_ug, rs_vk, rs_vg, rd_vk, rd_vg, c_k, c_g, held, v_sem, u_sems = refs
    rows, cols = u.shape[:2]
    rank, width = v.shape[2:]
    me_row, me_col = lax.axis_index("row"), lax.axis_index("col")
    row_first = order[0, 0] == rows_n * rows - 1
    row_other = jnp.where(row_first, order[1, 0], order[0, 0])
    col_other = jnp.where(order[0, 1] == cols_n * cols - 1, order[1, 1], order[0, 1])
    row_dyn, col_dyn = lax.rem(row_other, rows), lax.rem(col_other, cols)
    row_side, col_side = lax.rem(me_row, 2), lax.rem(me_col, 2)

    fetch = pltpu.make_async_copy(v, held, v_sem)
    fetch.start()
    copies = []
    for i, outs in ((rows - 1, (rs_uk, rs_ug)), (row_dyn, (rd_uk, rd_ug))):
        for slot, j in enumerate((row_side, 1 - row_side)):
            copies.append((u.at[i, j], outs[slot]))
    for which, j in enumerate((cols - 1, col_dyn)):
        for slot, i in enumerate((col_side, 1 - col_side)):
            copies.append((u.at[i, j], (c_k, c_g)[slot].at[which, 0]))
    copies = [pltpu.make_async_copy(a, b, u_sems.at[k]) for k, (a, b) in enumerate(copies)]
    for copy in copies:
        copy.start()

    q1, q2 = order[0, 1], order[1, 1]
    truth = {
        "row_first": row_first, "side_r": row_side == 0, "side_c": col_side == 0,
        "q1_low": lax.rem(q1, cols) == 0, "q2_low": lax.rem(q2, cols) == 0}
    for bit in all_bits(rows_n):
        truth["rs", bit] = (me_row & bit) == (rows_n - 1) & bit
        truth["rd", bit] = (me_row & bit) == (lax.div(row_other, rows) & bit)
    for d in range(rows_n):
        truth["at", d] = me_row == d
    truth["rs", 1] = me_row != (rows_n - 1) ^ 1
    for bit in all_bits(cols_n):
        truth["cs", bit] = (me_col & bit) == (cols_n - 1) & bit
        for kind, where in (("cd", col_other), ("q1", q1), ("q2", q2)):
            truth[kind, bit] = (me_col & bit) == (lax.div(where, cols) & bit)
    for k, name in enumerate(flag_names(rows_n, cols_n)):
        flags[k:k + 1, :] = jnp.full((1, width), jnp.where(truth[name], 1, 0), jnp.int32)
    fetch.wait()

    def kept(i, j):
        row = lax.broadcasted_iota(jnp.int32, (rank, width), 0)
        return jnp.where(row < ranks[i, j], held[i, j], jnp.zeros((), v.dtype))

    for i, outs in ((rows - 1, (rs_vk, rs_vg)), (row_dyn, (rd_vk, rd_vg))):
        for slot, j in enumerate((row_side, 1 - row_side)):
            outs[slot][...] = kept(i, j)
    for which, j in enumerate((cols - 1, col_dyn)):
        for slot, i in enumerate((col_side, 1 - col_side)):
            value = kept(i, j)
            for k in range(width // rank):
                (c_k, c_g)[slot][which, 1, k * rank:(k + 1) * rank, :] = value[:, k * rank:(k + 1) * rank]
    for copy in copies:
        copy.wait()


def solve_kernel(order, inverses, fixed, moving, out, *, last_row):
    fixed_first = order[0, 0] == last_row
    out[0] = dot(inverses[0], jnp.where(fixed_first, fixed[...], moving[...])).astype(BF16)
    out[1] = dot(inverses[1], jnp.where(fixed_first, moving[...], fixed[...])).astype(BF16)


def core_kernel(order, solved, swapped, first, second, v21, v12, out, edge, *, last_col):
    rank, width = v21.shape
    count = width // rank
    swap_first = lax.rem(lax.axis_index("row"), 2) == 1
    step_of = jnp.where(order[0, 1] == last_col, 0, 1)
    for s, more in enumerate((v21, v12)):
        which = step_of if s == 0 else 1 - step_of
        lines = [jnp.concatenate([tiles[which, 1, k * rank:(k + 1) * rank, :] for k in range(count)], axis=1) for tiles in (first, second)]
        tall = jnp.concatenate(lines + [more[...]], axis=0)
        mine, other = solved[s], swapped[s]
        wide = jnp.concatenate([jnp.where(swap_first, other, mine), jnp.where(swap_first, mine, other)], axis=1)
        got = dot(tall, wide).astype(BF16)
        out[s] = got
        late = lax.rem(order[1 - s, 1], 2) == 1
        pivot = jnp.where(late, got[:, rank:], got[:, :rank])
        if s == 0:
            edge[:2 * rank] = pivot[:2 * rank]
        else:
            edge[2 * rank:] = pivot


def final_kernel(order, ranks, u, v, first, second, vp1, vp2, cores, edge, out, *, last_col):
    i, j = pl.program_id(0), pl.program_id(1)
    rank, width = v.shape[2:]
    row = lax.axis_index("row") * pl.num_programs(0) + i
    col = lax.axis_index("col") * pl.num_programs(1) + j
    open1 = jnp.logical_and(row != order[0, 0], col != order[0, 1])
    open2 = jnp.logical_and(open1, jnp.logical_and(row != order[1, 0], col != order[1, 1]))
    m1 = jnp.where(open1, F32(1), F32(0))
    m2 = jnp.where(open2, F32(1), F32(0))
    foot = (cores.shape[1] // rank - 1) * rank
    top = pl.ds(pl.multiple_of(i * rank, rank), rank)
    below = pl.ds(pl.multiple_of(2 * rank + i * rank, rank), rank)

    def left(s, lines):
        return jnp.where(j == 0, cores[s, lines, :rank], cores[s, lines, rank:])

    c1_ij, c1_iq2, c1_p2j = left(0, top), edge[top], left(0, pl.ds(foot, rank))
    high_a, high_b = left(1, top), edge[below]
    low_a = -dot(c1_iq2, left(1, pl.ds(foot, rank)))
    low_b = -dot(c1_iq2, edge[4 * rank:])
    q1p1 = m2 * dot(low_b.astype(BF16), c1_p2j) - m1 * c1_ij.astype(F32)
    q2p1 = m2 * dot(high_b, c1_p2j)
    mix = jnp.concatenate([
        jnp.concatenate([q1p1, -m2 * low_a], axis=1),
        jnp.concatenate([q2p1, -m2 * high_a.astype(F32)], axis=1)], axis=0).astype(BF16)
    change = dot(mix, jnp.concatenate([vp1[0], vp2[0]], axis=0)).astype(BF16)
    line = lax.broadcasted_iota(jnp.int32, (rank, width), 0)
    own = jnp.where(line < ranks[i, j], v[0, 0], jnp.zeros((), BF16))
    right = jnp.concatenate([own, change], axis=0)
    w1 = jnp.where(order[0, 1] == last_col, 0, 1)
    uq1, uq2 = (jnp.where(i == 0, first[w, 0], second[w, 0]) for w in (w1, 1 - w1))
    out[0, 0] = dot(jnp.concatenate([u[0, 0], uq1, uq2], axis=1), right).astype(BF16)


def rest(rows_n, cols_n, root, tile_u, tile_v, tile_ranks, inverses, panel_order, flags, *cut):
    rs_uk, rs_ug, rd_uk, rd_ug, rs_vk, rs_vg, rd_vk, rd_vg, c_k, c_g = cut
    rows, cols, width, rank = tile_u.shape
    last = dict(last_row=rows_n * rows - 1, last_col=cols_n * cols - 1)
    names = flag_names(rows_n, cols_n)

    def flag(name, like):
        k = names.index(name)
        return flags[k:k + 1, :like.shape[-1]] != 0

    def choose(name, one, two):
        return jnp.where(flag(name, one), one, two)

    def same(kind):
        return lambda bit, like: flag((kind, bit), like)

    def member(devices, like):
        return sum(flags[names.index(("at", d)), :like.shape[-1]] for d in sorted(devices)) != 0

    def pair(fixed_keep, fixed_give, moving_keep, moving_give):
        if root is None:
            return MovingPair(Lane(fixed_keep, fixed_give, "row", rows_n, same("rs"), rows_n - 1),
                              Lane(moving_keep, moving_give, "row", rows_n, same("rd")))
        return KnownPair((fixed_keep, moving_keep), (fixed_give, moving_give), "row", rows_n, (rows_n - 1, root), member)

    def joined(mine, axis, n, side):
        other = swap(mine, axis, n, 1)
        return choose(side, mine, other), choose(side, other, mine)

    def both_q(bit, like):
        return jnp.stack([flag(("q1", bit), like), flag(("q2", bit), like)])

    def cross(one, two):
        shape = one.shape[1:]
        cand = jnp.stack([choose("q1_low", two[0], two[1]), choose("q2_low", one[0], one[1])])
        cand = cand.reshape(2, 2, shape[0] // 2, shape[1])
        lane = Lane(choose("side_c", cand[:, 0], cand[:, 1]), choose("side_c", cand[:, 1], cand[:, 0]), "col", cols_n, both_q)
        for k in range(len(lane.bits)):
            lane.step(k)
        both = jnp.concatenate(joined(lane.mine, "col", cols_n, "side_c"), axis=1)
        return both[0], both[1]

    v_pair = pair(rs_vk, rs_vg, rd_vk, rd_vg)
    c_got = swap(c_g, "col", cols_n, 1)
    c_lanes = [Lane(c_k[k], None, "col", cols_n, same(kind), got=c_got[k]) for k, kind in enumerate(("cs", "cd"))]
    arrived = v_pair.mine
    u_pair = pair(rs_uk, after(rs_ug, *arrived), rd_uk, after(rd_ug, *arrived))

    mark = []
    ties = [lane.mine for lane in c_lanes]
    for k in range(len(upper_bits(rows_n))):
        v_pair.step(k, *ties)
        ties = list(u_pair.mine)
        if k == 0:
            for lane, before in zip(c_lanes, ((), (c_lanes[0],))):
                for m in range(len(lane.bits)):
                    lane.step(m, *(other.mine for other in before))
            ties.append(c_lanes[0].mine)
        else:
            mark = list(u_pair.mine)
        arrived = v_pair.mine
        u_pair.step(k, *arrived)
        if k == 0:
            mark = list(u_pair.mine)
    fixed, moving = (after(x, *mark, c_lanes[1].mine) for x in arrived)
    mine = jnp.stack([choose("row_first", fixed, moving), choose("row_first", moving, fixed)])
    vj0, vj1 = joined(mine, "row", rows_n, "side_r")
    vp1, vp2 = (jnp.stack([vj0[s], vj1[s]]) for s in range(2))
    first, second = joined(jnp.stack([lane.mine for lane in c_lanes]), "col", cols_n, "side_c")
    waits = u_pair.mine
    v21, v12 = cross(after(vp1, *waits), after(vp2, *waits))

    solved = pl.pallas_call(
        functools.partial(solve_kernel, last_row=last["last_row"]),
        out_shape=jax.ShapeDtypeStruct((2, width, rank), BF16),
        in_specs=[SCALARS] + [WHOLE] * 3,
        out_specs=WHOLE,
        compiler_params=params(),
    )(panel_order, inverses, *u_pair.mine)
    swapped = swap(solved, "row", rows_n, 1)
    cores, edge = pl.pallas_call(
        functools.partial(core_kernel, last_col=last["last_col"]),
        out_shape=[jax.ShapeDtypeStruct((2, 3 * rank, 2 * rank), BF16), jax.ShapeDtypeStruct((5 * rank, rank), BF16)],
        in_specs=[SCALARS] + [WHOLE] * 6,
        out_specs=[WHOLE] * 2,
        compiler_params=params(),
    )(panel_order, solved, swapped, first, second, v21, v12)
    for bit in all_bits(cols_n):
        got = swap(edge, "col", cols_n, bit)
        early = jnp.arange(5 * rank)[:, None] < 2 * rank
        stays = jnp.where(early, flag(("q2", bit), edge), flag(("q1", bit), edge))
        edge = jnp.where(stays, edge, got)

    return pl.pallas_call(
        functools.partial(final_kernel, last_col=last["last_col"]),
        out_shape=jax.ShapeDtypeStruct((rows, cols, width, width), BF16),
        grid=(rows, cols),
        in_specs=[
            SCALARS, SCALARS,
            pl.BlockSpec((1, 1, width, rank), lambda i, j: (i, j, 0, 0)),
            pl.BlockSpec((1, 1, rank, width), lambda i, j: (i, j, 0, 0)),
            WHOLE, WHOLE,
            pl.BlockSpec((1, rank, width), lambda i, j: (j, 0, 0)),
            pl.BlockSpec((1, rank, width), lambda i, j: (j, 0, 0)),
            WHOLE, WHOLE],
        out_specs=pl.BlockSpec((1, 1, width, width), lambda i, j: (i, j, 0, 0)),
        compiler_params=params(VMEM_MOST),
    )(panel_order, tile_ranks, tile_u, tile_v, first, second, vp1, vp2, cores, edge)


def make(rows_n, cols_n):
    def on_device(tile_u, tile_v, tile_ranks, inverses, panel_order):
        rows, cols, width, rank = tile_u.shape
        last = dict(last_row=rows_n * rows - 1, last_col=cols_n * cols - 1)
        tall = jax.ShapeDtypeStruct((width, rank), BF16)
        flat = jax.ShapeDtypeStruct((rank, width), BF16)
        quad = jax.ShapeDtypeStruct((2, 2, width, rank), BF16)
        anywhere = pl.BlockSpec(memory_space=pl.ANY)
        names = flag_names(rows_n, cols_n)
        cut = pl.pallas_call(
            functools.partial(prep_kernel, rows_n=rows_n, cols_n=cols_n),
            out_shape=[jax.ShapeDtypeStruct((len(names), width), jnp.int32)] + [tall] * 4 + [flat] * 4 + [quad] * 2,
            in_specs=[SCALARS, SCALARS, anywhere, anywhere],
            out_specs=[WHOLE] * 11,
            scratch_shapes=[pltpu.VMEM(tile_v.shape, BF16), pltpu.SemaphoreType.DMA(()), pltpu.SemaphoreType.DMA((8,))],
            compiler_params=params(),
        )(panel_order, tile_ranks, tile_u, tile_v)
        run = functools.partial(rest, rows_n, cols_n)
        operands = (tile_u, tile_v, tile_ranks, inverses, panel_order, *cut)
        if rows_n > BRANCHES:
            return run(None, *operands)
        other = jnp.where(panel_order[0, 0] == last["last_row"], panel_order[1, 0], panel_order[0, 0])
        return lax.switch(other // rows, [functools.partial(run, r) for r in range(rows_n)], *operands)

    return on_device


def solution(mesh):
    placed = (P("row", "col", None, None), P("row", "col", None, None), P("row", "col"), P(), P())
    return jax.shard_map(
        make(mesh.shape["row"], mesh.shape["col"]),
        mesh=mesh,
        in_specs=placed,
        out_specs=P("row", "col", None, None),
        check_vma=False,
    )
```

```python
import functools

import jax
import jax.numpy as jnp
from jax import lax
from jax.experimental import pallas as pl
from jax.experimental.pallas import tpu as pltpu
from jax.sharding import PartitionSpec as P

F32 = jnp.float32
BF16 = jnp.bfloat16
VMEM_BYTES = 48 * 1024 * 1024
WHOLE = pl.BlockSpec(memory_space=pltpu.VMEM)
SCALARS = pl.BlockSpec(memory_space=pltpu.SMEM)


def params():
    return pltpu.CompilerParams(vmem_limit_bytes=VMEM_BYTES)


def dot(a, b):
    return jnp.dot(a, b, preferred_element_type=F32)


def swap(block, axis, n, bit, senders=None):
    senders = range(n) if senders is None else sorted(senders)
    return lax.ppermute(block, axis, [(s, s ^ bit) for s in senders])


def upper_bits(n):
    return [1 << b for b in range(1, n.bit_length() - 1)]


def after(value, *others):
    return lax.optimization_barrier((value,) + others)[0]


def all_bits(n):
    return [1] + upper_bits(n)


class Lane:
    def __init__(self, keep, give, axis, n, same, root=None, got=None):
        self.mine, self.axis, self.n, self.same = keep, axis, n, same
        self.holders = None if root is None else {root}
        self.bits = upper_bits(n) if root is None else upper_bits(n)[::-1]
        self.move(1, give, got)

    def move(self, bit, value, got=None):
        got = swap(value, self.axis, self.n, bit, self.holders) if got is None else got
        if self.holders:
            self.holders = self.holders | {h ^ bit for h in self.holders}
        self.mine = jnp.where(self.same(bit, self.mine), self.mine, got)

    def step(self, k, *others):
        if others:
            self.mine = after(self.mine, *others)
        self.move(self.bits[k], self.mine)


def flag_names(rows_n, cols_n):
    names = ["row_first", "side_r", "side_c", "q1_side", "q2_side"]
    names += [(kind, bit) for kind in ("p1", "p2") for bit in upper_bits(rows_n)]
    names += [(kind, bit) for kind in ("rs", "rd") for bit in all_bits(rows_n)]
    names += [(kind, bit) for kind in ("cs", "cd", "q1", "q2") for bit in all_bits(cols_n)]
    return names


def prep_kernel(order, ranks, u, v, *refs, rows_n, cols_n):
    flags, rs_uk, rs_ug, rd_uk, rd_ug, rs_vk, rs_vg, rd_vk, rd_vg, cu_k, cu_g, cv_k, cv_g, held, v_sem, u_sems = refs
    rows, cols = u.shape[:2]
    rank, width = v.shape[2:]
    me_row, me_col = lax.axis_index("row"), lax.axis_index("col")
    row_first = order[0, 0] == rows_n * rows - 1
    row_other = jnp.where(row_first, order[1, 0], order[0, 0])
    col_other = jnp.where(order[0, 1] == cols_n * cols - 1, order[1, 1], order[0, 1])
    row_dyn, col_dyn = lax.rem(row_other, rows), lax.rem(col_other, cols)
    row_side, col_side = lax.rem(me_row, 2), lax.rem(me_col, 2)

    fetch = pltpu.make_async_copy(v, held, v_sem)
    fetch.start()
    copies = []
    for i, outs in ((rows - 1, (rs_uk, rs_ug)), (row_dyn, (rd_uk, rd_ug))):
        for slot, j in enumerate((row_side, 1 - row_side)):
            copies.append((u.at[i, j], outs[slot]))
    for which, j in enumerate((cols - 1, col_dyn)):
        for slot, i in enumerate((col_side, 1 - col_side)):
            copies.append((u.at[i, j], (cu_k, cu_g)[slot].at[which]))
    copies = [pltpu.make_async_copy(a, b, u_sems.at[k]) for k, (a, b) in enumerate(copies)]
    for copy in copies:
        copy.start()

    q1, q2 = order[0, 1], order[1, 1]
    truth = {
        "row_first": row_first, "side_r": row_side == 0, "side_c": col_side == 0,
        "q1_side": lax.rem(q1, cols) == row_side, "q2_side": lax.rem(q2, cols) == row_side}
    for bit in all_bits(rows_n):
        truth["rs", bit] = (me_row & bit) == (rows_n - 1) & bit
        truth["p1", bit] = (me_row & bit) == (lax.div(order[0, 0], rows) & bit)
        truth["p2", bit] = (me_row & bit) == (lax.div(order[1, 0], rows) & bit)
        truth["rd", bit] = (me_row & bit) == (lax.div(row_other, rows) & bit)
    truth["rs", 1] = me_row != (rows_n - 1) ^ 1
    for bit in all_bits(cols_n):
        truth["cs", bit] = (me_col & bit) == (cols_n - 1) & bit
        for kind, where in (("cd", col_other), ("q1", q1), ("q2", q2)):
            truth[kind, bit] = (me_col & bit) == (lax.div(where, cols) & bit)
    for k, name in enumerate(flag_names(rows_n, cols_n)):
        flags[k:k + 1, :] = jnp.full((1, width), jnp.where(truth[name], 1, 0), jnp.int32)
    fetch.wait()

    def kept(i, j):
        row = lax.broadcasted_iota(jnp.int32, (rank, width), 0)
        return jnp.where(row < ranks[i, j], held[i, j], jnp.zeros((), v.dtype))

    for i, outs in ((rows - 1, (rs_vk, rs_vg)), (row_dyn, (rd_vk, rd_vg))):
        for slot, j in enumerate((row_side, 1 - row_side)):
            outs[slot][...] = kept(i, j)
    for which, j in enumerate((cols - 1, col_dyn)):
        for slot, i in enumerate((col_side, 1 - col_side)):
            value = kept(i, j)
            for k in range(width // rank):
                (cv_k, cv_g)[slot][which, k * rank:(k + 1) * rank, :] = value[:, k * rank:(k + 1) * rank]
    for copy in copies:
        copy.wait()


def solve_kernel(order, inverses, fixed, moving, out, *, last_row):
    fixed_first = order[0, 0] == last_row
    out[0] = dot(inverses[0], jnp.where(fixed_first, fixed[...], moving[...])).astype(BF16)
    out[1] = dot(inverses[1], jnp.where(fixed_first, moving[...], fixed[...])).astype(BF16)


def core_kernel(order, solved, first, second, out, foot, *, last_col):
    rank = out.shape[2]
    count = solved.shape[1] // rank
    me = lax.axis_index("row")
    step_of = jnp.where(order[0, 1] == last_col, 0, 1)
    for s in range(2):
        which = step_of if s == 0 else 1 - step_of
        lines = [
            jnp.concatenate([tiles[which + far, k * rank:(k + 1) * rank, :] for k in range(count)], axis=1)
            for far in (0, 2) for tiles in (first, second)]
        out[s] = dot(jnp.concatenate(lines, axis=0), solved[s]).astype(BF16)
        row = order[1 - s, 0]
        far = lax.rem(lax.div(row, 2) + me, 2)
        foot[s] = out[s, pl.ds(pl.multiple_of((2 * far + lax.rem(row, 2)) * rank, rank), rank), :]


def final_kernel(order, ranks, u, v, first, second, vp1, vp2, cores, swapped, edge, out, *, last_col):
    i, j = pl.program_id(0), pl.program_id(1)
    rank, width = v.shape[2:]
    row = lax.axis_index("row") * pl.num_programs(0) + i
    col = lax.axis_index("col") * pl.num_programs(1) + j
    open1 = jnp.logical_and(row != order[0, 0], col != order[0, 1])
    open2 = jnp.logical_and(open1, jnp.logical_and(row != order[1, 0], col != order[1, 1]))
    m1 = jnp.where(open1, F32(1), F32(0))
    m2 = jnp.where(open2, F32(1), F32(0))
    foot = (cores.shape[1] // rank - 1) * rank
    top = pl.ds(pl.multiple_of(i * rank, rank), rank)
    below = pl.ds(pl.multiple_of(2 * rank + i * rank, rank), rank)

    here = j == lax.rem(lax.axis_index("row"), 2)

    def left(s, lines):
        return jnp.where(here, cores[s, lines, :], swapped[s, lines, :])

    c1_ij, c1_iq2, c1_p2j = left(0, top), edge[top], left(0, pl.ds(foot, rank))
    high_a, high_b = left(1, top), edge[below]
    low_a = -dot(c1_iq2, left(1, pl.ds(foot, rank)))
    low_b = -dot(c1_iq2, edge[4 * rank:])
    q1p1 = m2 * dot(low_b.astype(BF16), c1_p2j) - m1 * c1_ij.astype(F32)
    q2p1 = m2 * dot(high_b, c1_p2j)
    mix = jnp.concatenate([
        jnp.concatenate([q1p1, -m2 * low_a], axis=1),
        jnp.concatenate([q2p1, -m2 * high_a.astype(F32)], axis=1)], axis=0).astype(BF16)
    change = dot(mix, jnp.concatenate([vp1[0], vp2[0]], axis=0)).astype(BF16)
    line = lax.broadcasted_iota(jnp.int32, (rank, width), 0)
    own = jnp.where(line < ranks[i, j], v[0, 0], jnp.zeros((), BF16))
    right = jnp.concatenate([own, change], axis=0)
    w1 = jnp.where(order[0, 1] == last_col, 0, 1)
    uq1, uq2 = (jnp.where(i == 0, first[w], second[w]) for w in (w1, 1 - w1))
    out[0, 0] = dot(jnp.concatenate([u[0, 0], uq1, uq2], axis=1), right).astype(BF16)


def make(rows_n, cols_n):
    def on_device(tile_u, tile_v, tile_ranks, inverses, panel_order):
        rows, cols, width, rank = tile_u.shape
        last = dict(last_row=rows_n * rows - 1, last_col=cols_n * cols - 1)
        tall = jax.ShapeDtypeStruct((width, rank), BF16)
        flat = jax.ShapeDtypeStruct((rank, width), BF16)
        pair = jax.ShapeDtypeStruct((2, width, rank), BF16)
        anywhere = pl.BlockSpec(memory_space=pl.ANY)
        names = flag_names(rows_n, cols_n)
        cut = pl.pallas_call(
            functools.partial(prep_kernel, rows_n=rows_n, cols_n=cols_n),
            out_shape=[jax.ShapeDtypeStruct((len(names), width), jnp.int32)] + [tall] * 4 + [flat] * 4 + [pair] * 4,
            in_specs=[SCALARS, SCALARS, anywhere, anywhere],
            out_specs=[WHOLE] * 13,
            scratch_shapes=[pltpu.VMEM(tile_v.shape, BF16), pltpu.SemaphoreType.DMA(()), pltpu.SemaphoreType.DMA((8,))],
            compiler_params=params(),
        )(panel_order, tile_ranks, tile_u, tile_v)
        flags, rs_uk, rs_ug, rd_uk, rd_ug, rs_vk, rs_vg, rd_vk, rd_vg, cu_k, cu_g, cv_k, cv_g = cut

        def flag(name, like):
            k = names.index(name)
            return flags[k:k + 1, :like.shape[-1]] != 0

        def choose(name, one, two):
            return jnp.where(flag(name, one), one, two)

        def same(kind):
            return lambda bit, like: flag((kind, bit), like)

        def lanes(fixed_keep, fixed_give, moving_keep, moving_give):
            return (Lane(moving_keep, moving_give, "row", rows_n, same("rd")),
                    Lane(fixed_keep, fixed_give, "row", rows_n, same("rs"), rows_n - 1))

        def joined(mine, axis, n, side):
            other = swap(mine, axis, n, 1)
            return choose(side, mine, other), choose(side, other, mine)

        def same_both(bit, like):
            return jnp.stack([flag(("cs", bit), like), flag(("cd", bit), like)])

        def mines(pair):
            return [lane.mine for lane in pair]

        u_lanes = lanes(rs_uk, rs_ug, rd_uk, rd_ug)
        cv = Lane(cv_k, cv_g, "col", cols_n, same_both)
        ties = mines(u_lanes)
        v_lanes = lanes(rs_vk, after(rs_vg, *ties), rd_vk, after(rd_vg, *ties))
        ties = [cv.mine]
        for k in range(len(upper_bits(rows_n))):
            for lane in u_lanes:
                lane.step(k, *ties)
            ties = mines(v_lanes)
            follow = mines(u_lanes)
            if k == 0:
                for m in range(len(cv.bits)):
                    cv.step(m)
                ties.append(cv.mine)
                near = swap(cv.mine, "row", rows_n, 1)
                cu = Lane(cu_k, after(cu_g, cv.mine), "col", cols_n, same_both)
            else:
                follow.append(near)
            if k < len(upper_bits(rows_n)) - 1:
                for lane in v_lanes:
                    lane.step(k, *follow)
        v_lanes[1].step(k, *follow)
        for m in range(len(cu.bits)):
            cu.step(m)
        cv_first, cv_second = joined(jnp.concatenate([cv.mine, near]), "col", cols_n, "side_c")
        cu_first, cu_second = joined(cu.mine, "col", cols_n, "side_c")

        moving, fixed = mines(u_lanes)
        solved = pl.pallas_call(
            functools.partial(solve_kernel, last_row=last["last_row"]),
            out_shape=jax.ShapeDtypeStruct((2, width, rank), BF16),
            in_specs=[SCALARS] + [WHOLE] * 3,
            out_specs=WHOLE,
            compiler_params=params(),
        )(panel_order, inverses, fixed, moving)
        cores, foot = pl.pallas_call(
            functools.partial(core_kernel, last_col=last["last_col"]),
            out_shape=[jax.ShapeDtypeStruct((2, 4 * rank, rank), BF16), jax.ShapeDtypeStruct((2, rank, rank), BF16)],
            in_specs=[SCALARS] + [WHOLE] * 3,
            out_specs=[WHOLE] * 2,
            compiler_params=params(),
        )(panel_order, solved, cv_first, cv_second)
        for m, bit in enumerate(upper_bits(rows_n)):
            got = swap(foot, "row", rows_n, bit)
            foot = jnp.where(jnp.stack([flag(("p2", bit), foot), flag(("p1", bit), foot)]), foot, got)
            if m == 0:
                v_lanes[0].step(k, foot, *follow)
        swapped = swap(jnp.concatenate([cores[:, 2 * rank:], foot], axis=1), "row", rows_n, 1)
        cores = jnp.concatenate([cores[:, :2 * rank], foot], axis=1)
        edge = jnp.concatenate([choose("q2_side", cores[0, :2 * rank], swapped[0, :2 * rank]), choose("q1_side", cores[1], swapped[1])])
        for bit in all_bits(cols_n):
            got = swap(edge, "col", cols_n, bit)
            early = jnp.arange(5 * rank)[:, None] < 2 * rank
            stays = jnp.where(early, flag(("q2", bit), edge), flag(("q1", bit), edge))
            edge = jnp.where(stays, edge, got)

        moving, fixed = mines(v_lanes)
        mine = jnp.stack([choose("row_first", fixed, moving), choose("row_first", moving, fixed)])
        vj0, vj1 = joined(mine, "row", rows_n, "side_r")
        vp1, vp2 = (jnp.stack([vj0[s], vj1[s]]) for s in range(2))

        return pl.pallas_call(
            functools.partial(final_kernel, last_col=last["last_col"]),
            out_shape=jax.ShapeDtypeStruct((rows, cols, width, width), BF16),
            grid=(rows, cols),
            in_specs=[
                SCALARS, SCALARS,
                pl.BlockSpec((1, 1, width, rank), lambda i, j: (i, j, 0, 0)),
                pl.BlockSpec((1, 1, rank, width), lambda i, j: (i, j, 0, 0)),
                WHOLE, WHOLE,
                pl.BlockSpec((1, rank, width), lambda i, j: (j, 0, 0)),
                pl.BlockSpec((1, rank, width), lambda i, j: (j, 0, 0)),
                WHOLE, WHOLE, WHOLE],
            out_specs=pl.BlockSpec((1, 1, width, width), lambda i, j: (i, j, 0, 0)),
            compiler_params=params(),
        )(panel_order, tile_ranks, tile_u, tile_v, cu_first, cu_second, vp1, vp2, cores, swapped, edge)

    return on_device


def solution(mesh):
    placed = (P("row", "col", None, None), P("row", "col", None, None), P("row", "col"), P(), P())
    return jax.shard_map(
        make(mesh.shape["row"], mesh.shape["col"]),
        mesh=mesh,
        in_specs=placed,
        out_specs=P("row", "col", None, None),
        check_vma=False,
    )
```

```python
import functools

import jax
import jax.numpy as jnp
from jax import lax
from jax.experimental import pallas as pl
from jax.experimental.pallas import tpu as pltpu
from jax.sharding import PartitionSpec as P

F32 = jnp.float32
BF16 = jnp.bfloat16
VMEM_BYTES = 48 * 1024 * 1024
WHOLE = pl.BlockSpec(memory_space=pltpu.VMEM)
SCALARS = pl.BlockSpec(memory_space=pltpu.SMEM)


def params():
    return pltpu.CompilerParams(vmem_limit_bytes=VMEM_BYTES)


def dot(a, b):
    return jnp.dot(a, b, preferred_element_type=F32)


def swap(block, axis, n, bit, senders=None):
    senders = range(n) if senders is None else sorted(senders)
    return lax.ppermute(block, axis, [(s, s ^ bit) for s in senders])


def upper_bits(n):
    return [1 << b for b in range(1, n.bit_length() - 1)]


def after(value, *others):
    return lax.optimization_barrier((value,) + others)[0]


def all_bits(n):
    return [1] + upper_bits(n)


class Lane:
    def __init__(self, keep, give, axis, n, same, root=None, got=None):
        self.mine, self.axis, self.n, self.same = keep, axis, n, same
        self.holders = None if root is None else {root}
        self.bits = upper_bits(n) if root is None else upper_bits(n)[::-1]
        self.move(1, give, got)

    def move(self, bit, value, got=None):
        got = swap(value, self.axis, self.n, bit, self.holders) if got is None else got
        if self.holders:
            self.holders = self.holders | {h ^ bit for h in self.holders}
        self.mine = jnp.where(self.same(bit, self.mine), self.mine, got)

    def step(self, k, *others):
        if others:
            self.mine = after(self.mine, *others)
        self.move(self.bits[k], self.mine)


def flag_names(rows_n, cols_n):
    names = ["row_first", "side_r", "side_c", "q1_side", "q2_side"]
    names += [(kind, bit) for kind in ("p1", "p2") for bit in upper_bits(rows_n)]
    names += [(kind, bit) for kind in ("rs", "rd") for bit in all_bits(rows_n)]
    names += [(kind, bit) for kind in ("cs", "cd", "q1", "q2") for bit in all_bits(cols_n)]
    return names


def prep_kernel(order, ranks, u, v, *refs, rows_n, cols_n):
    flags, rs_uk, rs_ug, rd_uk, rd_ug, rs_vk, rs_vg, rd_vk, rd_vg, cu_k, cu_g, cv_k, cv_g, held, v_sem, u_sems = refs
    rows, cols = u.shape[:2]
    rank, width = v.shape[2:]
    me_row, me_col = lax.axis_index("row"), lax.axis_index("col")
    row_first = order[0, 0] == rows_n * rows - 1
    row_other = jnp.where(row_first, order[1, 0], order[0, 0])
    col_other = jnp.where(order[0, 1] == cols_n * cols - 1, order[1, 1], order[0, 1])
    row_dyn, col_dyn = lax.rem(row_other, rows), lax.rem(col_other, cols)
    row_side, col_side = lax.rem(me_row, 2), lax.rem(me_col, 2)

    fetch = pltpu.make_async_copy(v, held, v_sem)
    fetch.start()
    copies = []
    for i, outs in ((rows - 1, (rs_uk, rs_ug)), (row_dyn, (rd_uk, rd_ug))):
        for slot, j in enumerate((row_side, 1 - row_side)):
            copies.append((u.at[i, j], outs[slot]))
    for which, j in enumerate((cols - 1, col_dyn)):
        for slot, i in enumerate((col_side, 1 - col_side)):
            copies.append((u.at[i, j], (cu_k, cu_g)[slot].at[which]))
    copies = [pltpu.make_async_copy(a, b, u_sems.at[k]) for k, (a, b) in enumerate(copies)]
    for copy in copies:
        copy.start()

    q1, q2 = order[0, 1], order[1, 1]
    truth = {
        "row_first": row_first, "side_r": row_side == 0, "side_c": col_side == 0,
        "q1_side": lax.rem(q1, cols) == row_side, "q2_side": lax.rem(q2, cols) == row_side}
    for bit in all_bits(rows_n):
        truth["rs", bit] = (me_row & bit) == (rows_n - 1) & bit
        truth["p1", bit] = (me_row & bit) == (lax.div(order[0, 0], rows) & bit)
        truth["p2", bit] = (me_row & bit) == (lax.div(order[1, 0], rows) & bit)
        truth["rd", bit] = (me_row & bit) == (lax.div(row_other, rows) & bit)
    truth["rs", 1] = me_row != (rows_n - 1) ^ 1
    for bit in all_bits(cols_n):
        truth["cs", bit] = (me_col & bit) == (cols_n - 1) & bit
        for kind, where in (("cd", col_other), ("q1", q1), ("q2", q2)):
            truth[kind, bit] = (me_col & bit) == (lax.div(where, cols) & bit)
    for k, name in enumerate(flag_names(rows_n, cols_n)):
        flags[k:k + 1, :] = jnp.full((1, width), jnp.where(truth[name], 1, 0), jnp.int32)
    fetch.wait()

    def kept(i, j):
        row = lax.broadcasted_iota(jnp.int32, (rank, width), 0)
        return jnp.where(row < ranks[i, j], held[i, j], jnp.zeros((), v.dtype))

    for i, outs in ((rows - 1, (rs_vk, rs_vg)), (row_dyn, (rd_vk, rd_vg))):
        for slot, j in enumerate((row_side, 1 - row_side)):
            outs[slot][...] = kept(i, j)
    for which, j in enumerate((cols - 1, col_dyn)):
        for slot, i in enumerate((col_side, 1 - col_side)):
            value = kept(i, j)
            for k in range(width // rank):
                (cv_k, cv_g)[slot][which, k * rank:(k + 1) * rank, :] = value[:, k * rank:(k + 1) * rank]
    for copy in copies:
        copy.wait()


def solve_kernel(order, inverses, fixed, moving, out, *, last_row):
    fixed_first = order[0, 0] == last_row
    out[0] = dot(inverses[0], jnp.where(fixed_first, fixed[...], moving[...])).astype(BF16)
    out[1] = dot(inverses[1], jnp.where(fixed_first, moving[...], fixed[...])).astype(BF16)


def core_kernel(order, solved, first, second, out, foot, *, last_col):
    rank = out.shape[2]
    count = solved.shape[1] // rank
    me = lax.axis_index("row")
    step_of = jnp.where(order[0, 1] == last_col, 0, 1)
    for s in range(2):
        which = step_of if s == 0 else 1 - step_of
        lines = [
            jnp.concatenate([tiles[which + far, k * rank:(k + 1) * rank, :] for k in range(count)], axis=1)
            for far in (0, 2) for tiles in (first, second)]
        out[s] = dot(jnp.concatenate(lines, axis=0), solved[s]).astype(BF16)
        row = order[1 - s, 0]
        far = lax.rem(lax.div(row, 2) + me, 2)
        foot[s] = out[s, pl.ds(pl.multiple_of((2 * far + lax.rem(row, 2)) * rank, rank), rank), :]


def final_kernel(order, ranks, u, v, first, second, vp1, vp2, cores, swapped, edge, out, *, last_col):
    i, j = pl.program_id(0), pl.program_id(1)
    rank, width = v.shape[2:]
    row = lax.axis_index("row") * pl.num_programs(0) + i
    col = lax.axis_index("col") * pl.num_programs(1) + j
    open1 = jnp.logical_and(row != order[0, 0], col != order[0, 1])
    open2 = jnp.logical_and(open1, jnp.logical_and(row != order[1, 0], col != order[1, 1]))
    m1 = jnp.where(open1, F32(1), F32(0))
    m2 = jnp.where(open2, F32(1), F32(0))
    foot = (cores.shape[1] // rank - 1) * rank
    top = pl.ds(pl.multiple_of(i * rank, rank), rank)
    below = pl.ds(pl.multiple_of(2 * rank + i * rank, rank), rank)

    here = j == lax.rem(lax.axis_index("row"), 2)

    def left(s, lines):
        return jnp.where(here, cores[s, lines, :], swapped[s, lines, :])

    c1_ij, c1_iq2, c1_p2j = left(0, top), edge[top], left(0, pl.ds(foot, rank))
    high_a, high_b = left(1, top), edge[below]
    low_a = -dot(c1_iq2, left(1, pl.ds(foot, rank)))
    low_b = -dot(c1_iq2, edge[4 * rank:])
    q1p1 = m2 * dot(low_b.astype(BF16), c1_p2j) - m1 * c1_ij.astype(F32)
    q2p1 = m2 * dot(high_b, c1_p2j)
    mix = jnp.concatenate([
        jnp.concatenate([q1p1, -m2 * low_a], axis=1),
        jnp.concatenate([q2p1, -m2 * high_a.astype(F32)], axis=1)], axis=0).astype(BF16)
    change = dot(mix, jnp.concatenate([vp1[0], vp2[0]], axis=0)).astype(BF16)
    line = lax.broadcasted_iota(jnp.int32, (rank, width), 0)
    own = jnp.where(line < ranks[i, j], v[0, 0], jnp.zeros((), BF16))
    right = jnp.concatenate([own, change], axis=0)
    w1 = jnp.where(order[0, 1] == last_col, 0, 1)
    uq1, uq2 = (jnp.where(i == 0, first[w], second[w]) for w in (w1, 1 - w1))
    out[0, 0] = dot(jnp.concatenate([u[0, 0], uq1, uq2], axis=1), right).astype(BF16)


def make(rows_n, cols_n):
    def on_device(tile_u, tile_v, tile_ranks, inverses, panel_order):
        rows, cols, width, rank = tile_u.shape
        last = dict(last_row=rows_n * rows - 1, last_col=cols_n * cols - 1)
        tall = jax.ShapeDtypeStruct((width, rank), BF16)
        flat = jax.ShapeDtypeStruct((rank, width), BF16)
        pair = jax.ShapeDtypeStruct((2, width, rank), BF16)
        anywhere = pl.BlockSpec(memory_space=pl.ANY)
        names = flag_names(rows_n, cols_n)
        cut = pl.pallas_call(
            functools.partial(prep_kernel, rows_n=rows_n, cols_n=cols_n),
            out_shape=[jax.ShapeDtypeStruct((len(names), width), jnp.int32)] + [tall] * 4 + [flat] * 4 + [pair] * 4,
            in_specs=[SCALARS, SCALARS, anywhere, anywhere],
            out_specs=[WHOLE] * 13,
            scratch_shapes=[pltpu.VMEM(tile_v.shape, BF16), pltpu.SemaphoreType.DMA(()), pltpu.SemaphoreType.DMA((8,))],
            compiler_params=params(),
        )(panel_order, tile_ranks, tile_u, tile_v)
        flags, rs_uk, rs_ug, rd_uk, rd_ug, rs_vk, rs_vg, rd_vk, rd_vg, cu_k, cu_g, cv_k, cv_g = cut

        def flag(name, like):
            k = names.index(name)
            return flags[k:k + 1, :like.shape[-1]] != 0

        def choose(name, one, two):
            return jnp.where(flag(name, one), one, two)

        def same(kind):
            return lambda bit, like: flag((kind, bit), like)

        def lanes(fixed_keep, fixed_give, moving_keep, moving_give):
            return (Lane(moving_keep, moving_give, "row", rows_n, same("rd")),
                    Lane(fixed_keep, fixed_give, "row", rows_n, same("rs"), rows_n - 1))

        def joined(mine, axis, n, side):
            other = swap(mine, axis, n, 1)
            return choose(side, mine, other), choose(side, other, mine)

        def same_both(bit, like):
            return jnp.stack([flag(("cs", bit), like), flag(("cd", bit), like)])

        def mines(pair):
            return [lane.mine for lane in pair]

        u_lanes = lanes(rs_uk, rs_ug, rd_uk, rd_ug)
        cv = Lane(cv_k, cv_g, "col", cols_n, same_both)
        ties = mines(u_lanes)
        v_lanes = lanes(rs_vk, after(rs_vg, *ties), rd_vk, after(rd_vg, *ties))
        ties = [cv.mine]
        for k in range(len(upper_bits(rows_n))):
            for lane in u_lanes:
                lane.step(k, *ties)
            ties = mines(v_lanes)
            follow = mines(u_lanes)
            if k == 0:
                for m in range(len(cv.bits)):
                    cv.step(m)
                ties.append(cv.mine)
                near = swap(cv.mine, "row", rows_n, 1)
                cu = Lane(cu_k, after(cu_g, cv.mine), "col", cols_n, same_both)
                cv_first, cv_second = joined(jnp.concatenate([cv.mine, near]), "col", cols_n, "side_c")
            else:
                follow.append(cv_first)
            for lane in v_lanes:
                lane.step(k, *follow)
        for m in range(len(cu.bits)):
            cu.step(m)
        cu_first, cu_second = joined(cu.mine, "col", cols_n, "side_c")

        moving, fixed = mines(u_lanes)
        solved = pl.pallas_call(
            functools.partial(solve_kernel, last_row=last["last_row"]),
            out_shape=jax.ShapeDtypeStruct((2, width, rank), BF16),
            in_specs=[SCALARS] + [WHOLE] * 3,
            out_specs=WHOLE,
            compiler_params=params(),
        )(panel_order, inverses, fixed, moving)
        cores, foot = pl.pallas_call(
            functools.partial(core_kernel, last_col=last["last_col"]),
            out_shape=[jax.ShapeDtypeStruct((2, 4 * rank, rank), BF16), jax.ShapeDtypeStruct((2, rank, rank), BF16)],
            in_specs=[SCALARS] + [WHOLE] * 3,
            out_specs=[WHOLE] * 2,
            compiler_params=params(),
        )(panel_order, solved, cv_first, cv_second)
        def at_root(bit):
            return jnp.stack([flag(("p2", bit), foot), flag(("p1", bit), foot)])

        bits = upper_bits(rows_n)
        if len(bits) == 2:
            one, two, three = (swap(foot, "row", rows_n, bit) for bit in (*bits, sum(bits)))
            foot = jnp.where(at_root(bits[1]), jnp.where(at_root(bits[0]), foot, one), jnp.where(at_root(bits[0]), two, three))
        else:
            for bit in bits:
                foot = jnp.where(at_root(bit), foot, swap(foot, "row", rows_n, bit))
        swapped = swap(jnp.concatenate([cores[:, 2 * rank:], foot], axis=1), "row", rows_n, 1)
        cores = jnp.concatenate([cores[:, :2 * rank], foot], axis=1)
        edge = jnp.concatenate([choose("q2_side", cores[0, :2 * rank], swapped[0, :2 * rank]), choose("q1_side", cores[1], swapped[1])])
        for bit in all_bits(cols_n):
            got = swap(edge, "col", cols_n, bit)
            early = jnp.arange(5 * rank)[:, None] < 2 * rank
            stays = jnp.where(early, flag(("q2", bit), edge), flag(("q1", bit), edge))
            edge = jnp.where(stays, edge, got)

        moving, fixed = (after(x, foot) for x in mines(v_lanes))
        mine = jnp.stack([choose("row_first", fixed, moving), choose("row_first", moving, fixed)])
        vj0, vj1 = joined(mine, "row", rows_n, "side_r")
        vp1, vp2 = (jnp.stack([vj0[s], vj1[s]]) for s in range(2))

        return pl.pallas_call(
            functools.partial(final_kernel, last_col=last["last_col"]),
            out_shape=jax.ShapeDtypeStruct((rows, cols, width, width), BF16),
            grid=(rows, cols),
            in_specs=[
                SCALARS, SCALARS,
                pl.BlockSpec((1, 1, width, rank), lambda i, j: (i, j, 0, 0)),
                pl.BlockSpec((1, 1, rank, width), lambda i, j: (i, j, 0, 0)),
                WHOLE, WHOLE,
                pl.BlockSpec((1, rank, width), lambda i, j: (j, 0, 0)),
                pl.BlockSpec((1, rank, width), lambda i, j: (j, 0, 0)),
                WHOLE, WHOLE, WHOLE],
            out_specs=pl.BlockSpec((1, 1, width, width), lambda i, j: (i, j, 0, 0)),
            compiler_params=params(),
        )(panel_order, tile_ranks, tile_u, tile_v, cu_first, cu_second, vp1, vp2, cores, swapped, edge)

    return on_device


def solution(mesh):
    placed = (P("row", "col", None, None), P("row", "col", None, None), P("row", "col"), P(), P())
    return jax.shard_map(
        make(mesh.shape["row"], mesh.shape["col"]),
        mesh=mesh,
        in_specs=placed,
        out_specs=P("row", "col", None, None),
        check_vma=False,
    )
```

```python
import functools

import jax
import jax.numpy as jnp
from jax import lax
from jax.experimental import pallas as pl
from jax.experimental.pallas import tpu as pltpu
from jax.sharding import PartitionSpec as P

F32 = jnp.float32
BF16 = jnp.bfloat16
VMEM_BYTES = 48 * 1024 * 1024
WHOLE = pl.BlockSpec(memory_space=pltpu.VMEM)
SCALARS = pl.BlockSpec(memory_space=pltpu.SMEM)


def params():
    return pltpu.CompilerParams(vmem_limit_bytes=VMEM_BYTES)


def dot(a, b):
    return jnp.dot(a, b, preferred_element_type=F32)


def swap(block, axis, n, bit, senders=None):
    senders = range(n) if senders is None else sorted(senders)
    return lax.ppermute(block, axis, [(s, s ^ bit) for s in senders])


def upper_bits(n):
    return [1 << b for b in range(1, n.bit_length() - 1)]


def after(value, *others):
    return lax.optimization_barrier((value,) + others)[0]


def all_bits(n):
    return [1] + upper_bits(n)


class Lane:
    def __init__(self, keep, give, axis, n, same, root=None, got=None):
        self.mine, self.axis, self.n, self.same = keep, axis, n, same
        self.holders = None if root is None else {root}
        self.bits = upper_bits(n) if root is None else upper_bits(n)[::-1]
        self.move(1, give, got)

    def move(self, bit, value, got=None):
        got = swap(value, self.axis, self.n, bit, self.holders) if got is None else got
        if self.holders:
            self.holders = self.holders | {h ^ bit for h in self.holders}
        self.mine = jnp.where(self.same(bit, self.mine), self.mine, got)

    def step(self, k, *others):
        if others:
            self.mine = after(self.mine, *others)
        self.move(self.bits[k], self.mine)


def flag_names(rows_n, cols_n):
    names = ["row_first", "side_r", "side_c", "q1_side", "q2_side"]
    names += [(kind, bit) for kind in ("p1", "p2") for bit in upper_bits(rows_n)]
    names += [(kind, bit) for kind in ("rs", "rd") for bit in all_bits(rows_n)]
    names += [(kind, bit) for kind in ("cs", "cd", "q1", "q2") for bit in all_bits(cols_n)]
    return names


def prep_kernel(order, ranks, u, v, *refs, rows_n, cols_n):
    flags, rs_uk, rs_ug, rd_uk, rd_ug, rs_vk, rs_vg, rd_vk, rd_vg, cu_k, cu_g, cv_k, cv_g, held, v_sem, u_sems = refs
    rows, cols = u.shape[:2]
    rank, width = v.shape[2:]
    me_row, me_col = lax.axis_index("row"), lax.axis_index("col")
    row_first = order[0, 0] == rows_n * rows - 1
    row_other = jnp.where(row_first, order[1, 0], order[0, 0])
    col_other = jnp.where(order[0, 1] == cols_n * cols - 1, order[1, 1], order[0, 1])
    row_dyn, col_dyn = lax.rem(row_other, rows), lax.rem(col_other, cols)
    row_side, col_side = lax.rem(me_row, 2), lax.rem(me_col, 2)

    fetch = pltpu.make_async_copy(v, held, v_sem)
    fetch.start()
    copies = []
    for i, outs in ((rows - 1, (rs_uk, rs_ug)), (row_dyn, (rd_uk, rd_ug))):
        for slot, j in enumerate((row_side, 1 - row_side)):
            copies.append((u.at[i, j], outs[slot]))
    for which, j in enumerate((cols - 1, col_dyn)):
        for slot, i in enumerate((col_side, 1 - col_side)):
            copies.append((u.at[i, j], (cu_k, cu_g)[slot].at[which]))
    copies = [pltpu.make_async_copy(a, b, u_sems.at[k]) for k, (a, b) in enumerate(copies)]
    for copy in copies:
        copy.start()

    q1, q2 = order[0, 1], order[1, 1]
    truth = {
        "row_first": row_first, "side_r": row_side == 0, "side_c": col_side == 0,
        "q1_side": lax.rem(q1, cols) == row_side, "q2_side": lax.rem(q2, cols) == row_side}
    for bit in all_bits(rows_n):
        truth["rs", bit] = (me_row & bit) == (rows_n - 1) & bit
        truth["p1", bit] = (me_row & bit) == (lax.div(order[0, 0], rows) & bit)
        truth["p2", bit] = (me_row & bit) == (lax.div(order[1, 0], rows) & bit)
        truth["rd", bit] = (me_row & bit) == (lax.div(row_other, rows) & bit)
    truth["rs", 1] = me_row != (rows_n - 1) ^ 1
    for bit in all_bits(cols_n):
        truth["cs", bit] = (me_col & bit) == (cols_n - 1) & bit
        for kind, where in (("cd", col_other), ("q1", q1), ("q2", q2)):
            truth[kind, bit] = (me_col & bit) == (lax.div(where, cols) & bit)
    for k, name in enumerate(flag_names(rows_n, cols_n)):
        flags[k:k + 1, :] = jnp.full((1, width), jnp.where(truth[name], 1, 0), jnp.int32)
    fetch.wait()

    def kept(i, j):
        row = lax.broadcasted_iota(jnp.int32, (rank, width), 0)
        return jnp.where(row < ranks[i, j], held[i, j], jnp.zeros((), v.dtype))

    for i, outs in ((rows - 1, (rs_vk, rs_vg)), (row_dyn, (rd_vk, rd_vg))):
        for slot, j in enumerate((row_side, 1 - row_side)):
            outs[slot][...] = kept(i, j)
    for which, j in enumerate((cols - 1, col_dyn)):
        for slot, i in enumerate((col_side, 1 - col_side)):
            value = kept(i, j)
            for k in range(width // rank):
                (cv_k, cv_g)[slot][which, k * rank:(k + 1) * rank, :] = value[:, k * rank:(k + 1) * rank]
    for copy in copies:
        copy.wait()


def solve_kernel(order, inverses, fixed, moving, out, *, last_row):
    fixed_first = order[0, 0] == last_row
    out[0] = dot(inverses[0], jnp.where(fixed_first, fixed[...], moving[...])).astype(BF16)
    out[1] = dot(inverses[1], jnp.where(fixed_first, moving[...], fixed[...])).astype(BF16)


def core_kernel(order, solved, first, second, out, foot, *, last_col):
    rank = out.shape[2]
    count = solved.shape[1] // rank
    me = lax.axis_index("row")
    step_of = jnp.where(order[0, 1] == last_col, 0, 1)
    for s in range(2):
        which = step_of if s == 0 else 1 - step_of
        lines = [
            jnp.concatenate([tiles[which + far, k * rank:(k + 1) * rank, :] for k in range(count)], axis=1)
            for far in (0, 2) for tiles in (first, second)]
        out[s] = dot(jnp.concatenate(lines, axis=0), solved[s]).astype(BF16)
        row = order[1 - s, 0]
        far = lax.rem(lax.div(row, 2) + me, 2)
        foot[s] = out[s, pl.ds(pl.multiple_of((2 * far + lax.rem(row, 2)) * rank, rank), rank), :]


def final_kernel(order, ranks, u, v, first, second, vp1, vp2, cores, swapped, edge, out, *, last_col):
    i, j = pl.program_id(0), pl.program_id(1)
    rank, width = v.shape[2:]
    row = lax.axis_index("row") * pl.num_programs(0) + i
    col = lax.axis_index("col") * pl.num_programs(1) + j
    open1 = jnp.logical_and(row != order[0, 0], col != order[0, 1])
    open2 = jnp.logical_and(open1, jnp.logical_and(row != order[1, 0], col != order[1, 1]))
    m1 = jnp.where(open1, F32(1), F32(0))
    m2 = jnp.where(open2, F32(1), F32(0))
    foot = (cores.shape[1] // rank - 1) * rank
    top = pl.ds(pl.multiple_of(i * rank, rank), rank)
    below = pl.ds(pl.multiple_of(2 * rank + i * rank, rank), rank)

    here = j == lax.rem(lax.axis_index("row"), 2)

    def left(s, lines):
        return jnp.where(here, cores[s, lines, :], swapped[s, lines, :])

    c1_ij, c1_iq2, c1_p2j = left(0, top), edge[top], left(0, pl.ds(foot, rank))
    high_a, high_b = left(1, top), edge[below]
    low_a = -dot(c1_iq2, left(1, pl.ds(foot, rank)))
    low_b = -dot(c1_iq2, edge[4 * rank:])
    q1p1 = m2 * dot(low_b.astype(BF16), c1_p2j) - m1 * c1_ij.astype(F32)
    q2p1 = m2 * dot(high_b, c1_p2j)
    mix = jnp.concatenate([
        jnp.concatenate([q1p1, -m2 * low_a], axis=1),
        jnp.concatenate([q2p1, -m2 * high_a.astype(F32)], axis=1)], axis=0).astype(BF16)
    change = dot(mix, jnp.concatenate([vp1[0], vp2[0]], axis=0)).astype(BF16)
    line = lax.broadcasted_iota(jnp.int32, (rank, width), 0)
    own = jnp.where(line < ranks[i, j], v[0, 0], jnp.zeros((), BF16))
    right = jnp.concatenate([own, change], axis=0)
    w1 = jnp.where(order[0, 1] == last_col, 0, 1)
    uq1, uq2 = (jnp.where(i == 0, first[w], second[w]) for w in (w1, 1 - w1))
    out[0, 0] = dot(jnp.concatenate([u[0, 0], uq1, uq2], axis=1), right).astype(BF16)


def make(rows_n, cols_n):
    def on_device(tile_u, tile_v, tile_ranks, inverses, panel_order):
        rows, cols, width, rank = tile_u.shape
        last = dict(last_row=rows_n * rows - 1, last_col=cols_n * cols - 1)
        tall = jax.ShapeDtypeStruct((width, rank), BF16)
        flat = jax.ShapeDtypeStruct((rank, width), BF16)
        pair = jax.ShapeDtypeStruct((2, width, rank), BF16)
        anywhere = pl.BlockSpec(memory_space=pl.ANY)
        names = flag_names(rows_n, cols_n)
        cut = pl.pallas_call(
            functools.partial(prep_kernel, rows_n=rows_n, cols_n=cols_n),
            out_shape=[jax.ShapeDtypeStruct((len(names), width), jnp.int32)] + [tall] * 4 + [flat] * 4 + [pair] * 4,
            in_specs=[SCALARS, SCALARS, anywhere, anywhere],
            out_specs=[WHOLE] * 13,
            scratch_shapes=[pltpu.VMEM(tile_v.shape, BF16), pltpu.SemaphoreType.DMA(()), pltpu.SemaphoreType.DMA((8,))],
            compiler_params=params(),
        )(panel_order, tile_ranks, tile_u, tile_v)
        flags, rs_uk, rs_ug, rd_uk, rd_ug, rs_vk, rs_vg, rd_vk, rd_vg, cu_k, cu_g, cv_k, cv_g = cut

        def flag(name, like):
            k = names.index(name)
            return flags[k:k + 1, :like.shape[-1]] != 0

        def choose(name, one, two):
            return jnp.where(flag(name, one), one, two)

        def same(kind):
            return lambda bit, like: flag((kind, bit), like)

        def lanes(fixed_keep, fixed_give, moving_keep, moving_give):
            lane = Lane(moving_keep, moving_give, "row", rows_n, same("rd"))
            return lane, Lane(fixed_keep, after(fixed_give, lane.mine), "row", rows_n, same("rs"), rows_n - 1)

        def joined(mine, axis, n, side):
            other = swap(mine, axis, n, 1)
            return choose(side, mine, other), choose(side, other, mine)

        def same_both(bit, like):
            return jnp.stack([flag(("cs", bit), like), flag(("cd", bit), like)])

        def mines(pair):
            return [lane.mine for lane in pair]

        u_lanes = lanes(rs_uk, rs_ug, rd_uk, rd_ug)
        cv = Lane(cv_k, cv_g, "col", cols_n, same_both)
        ties = mines(u_lanes)
        v_lanes = lanes(rs_vk, after(rs_vg, *ties), rd_vk, after(rd_vg, *ties))
        ties = [cv.mine]
        for k in range(len(upper_bits(rows_n))):
            for lane in u_lanes:
                lane.step(k, *ties)
            ties = [v_lanes[0].mine]
            follow = mines(u_lanes)
            if k == 0:
                for m in range(len(cv.bits)):
                    cv.step(m)
                ties.append(cv.mine)
                near = swap(cv.mine, "row", rows_n, 1)
                cu = Lane(cu_k, after(cu_g, cv.mine), "col", cols_n, same_both)
                follow.append(near)
                cv_first, cv_second = joined(jnp.concatenate([cv.mine, near]), "col", cols_n, "side_c")
            else:
                follow.append(cv_first)
            for lane in v_lanes:
                lane.step(k, *follow)
        for m in range(len(cu.bits)):
            cu.step(m)
        cu_first, cu_second = joined(cu.mine, "col", cols_n, "side_c")

        moving, fixed = mines(u_lanes)
        solved = pl.pallas_call(
            functools.partial(solve_kernel, last_row=last["last_row"]),
            out_shape=jax.ShapeDtypeStruct((2, width, rank), BF16),
            in_specs=[SCALARS] + [WHOLE] * 3,
            out_specs=WHOLE,
            compiler_params=params(),
        )(panel_order, inverses, fixed, moving)
        cores, foot = pl.pallas_call(
            functools.partial(core_kernel, last_col=last["last_col"]),
            out_shape=[jax.ShapeDtypeStruct((2, 4 * rank, rank), BF16), jax.ShapeDtypeStruct((2, rank, rank), BF16)],
            in_specs=[SCALARS] + [WHOLE] * 3,
            out_specs=[WHOLE] * 2,
            compiler_params=params(),
        )(panel_order, solved, cv_first, cv_second)
        def at_root(bit):
            return jnp.stack([flag(("p2", bit), foot), flag(("p1", bit), foot)])

        bits = upper_bits(rows_n)
        if len(bits) == 2:
            one, two, three = (swap(foot, "row", rows_n, bit) for bit in (*bits, sum(bits)))
            foot = jnp.where(at_root(bits[1]), jnp.where(at_root(bits[0]), foot, one), jnp.where(at_root(bits[0]), two, three))
        else:
            for bit in bits:
                foot = jnp.where(at_root(bit), foot, swap(foot, "row", rows_n, bit))
        swapped = swap(jnp.concatenate([cores[:, 2 * rank:], foot], axis=1), "row", rows_n, 1)
        cores = jnp.concatenate([cores[:, :2 * rank], foot], axis=1)
        edge = jnp.concatenate([choose("q2_side", cores[0, :2 * rank], swapped[0, :2 * rank]), choose("q1_side", cores[1], swapped[1])])
        for bit in all_bits(cols_n):
            got = swap(edge, "col", cols_n, bit)
            early = jnp.arange(5 * rank)[:, None] < 2 * rank
            stays = jnp.where(early, flag(("q2", bit), edge), flag(("q1", bit), edge))
            edge = jnp.where(stays, edge, got)

        moving, fixed = (after(x, foot) for x in mines(v_lanes))
        mine = jnp.stack([choose("row_first", fixed, moving), choose("row_first", moving, fixed)])
        vj0, vj1 = joined(mine, "row", rows_n, "side_r")
        vp1, vp2 = (jnp.stack([vj0[s], vj1[s]]) for s in range(2))

        return pl.pallas_call(
            functools.partial(final_kernel, last_col=last["last_col"]),
            out_shape=jax.ShapeDtypeStruct((rows, cols, width, width), BF16),
            grid=(rows, cols),
            in_specs=[
                SCALARS, SCALARS,
                pl.BlockSpec((1, 1, width, rank), lambda i, j: (i, j, 0, 0)),
                pl.BlockSpec((1, 1, rank, width), lambda i, j: (i, j, 0, 0)),
                WHOLE, WHOLE,
                pl.BlockSpec((1, rank, width), lambda i, j: (j, 0, 0)),
                pl.BlockSpec((1, rank, width), lambda i, j: (j, 0, 0)),
                WHOLE, WHOLE, WHOLE],
            out_specs=pl.BlockSpec((1, 1, width, width), lambda i, j: (i, j, 0, 0)),
            compiler_params=params(),
        )(panel_order, tile_ranks, tile_u, tile_v, cu_first, cu_second, vp1, vp2, cores, swapped, edge)

    return on_device


def solution(mesh):
    placed = (P("row", "col", None, None), P("row", "col", None, None), P("row", "col"), P(), P())
    return jax.shard_map(
        make(mesh.shape["row"], mesh.shape["col"]),
        mesh=mesh,
        in_specs=placed,
        out_specs=P("row", "col", None, None),
        check_vma=False,
    )
```

```python
import functools

import jax
import jax.numpy as jnp
from jax import lax
from jax.experimental import pallas as pl
from jax.experimental.pallas import tpu as pltpu
from jax.sharding import PartitionSpec as P

F32 = jnp.float32
BF16 = jnp.bfloat16
VMEM_BYTES = 48 * 1024 * 1024
WHOLE = pl.BlockSpec(memory_space=pltpu.VMEM)
SCALARS = pl.BlockSpec(memory_space=pltpu.SMEM)


def params():
    return pltpu.CompilerParams(vmem_limit_bytes=VMEM_BYTES)


def dot(a, b):
    return jnp.dot(a, b, preferred_element_type=F32)


def swap(block, axis, n, bit, senders=None):
    senders = range(n) if senders is None else sorted(senders)
    return lax.ppermute(block, axis, [(s, s ^ bit) for s in senders])


def upper_bits(n):
    return [1 << b for b in range(1, n.bit_length() - 1)]


def after(value, *others):
    return lax.optimization_barrier((value,) + others)[0]


def all_bits(n):
    return [1] + upper_bits(n)


class Lane:
    def __init__(self, keep, give, axis, n, same, root=None, got=None):
        self.mine, self.axis, self.n, self.same = keep, axis, n, same
        self.holders = None if root is None else {root}
        self.bits = upper_bits(n) if root is None else upper_bits(n)[::-1]
        self.move(1, give, got)

    def move(self, bit, value, got=None):
        got = swap(value, self.axis, self.n, bit, self.holders) if got is None else got
        if self.holders:
            self.holders = self.holders | {h ^ bit for h in self.holders}
        self.mine = jnp.where(self.same(bit, self.mine), self.mine, got)

    def step(self, k, *others):
        if others:
            self.mine = after(self.mine, *others)
        self.move(self.bits[k], self.mine)


def flag_names(rows_n, cols_n):
    names = ["row_first", "side_r", "side_c", "q1_side", "q2_side"]
    names += [(kind, bit) for kind in ("p1", "p2") for bit in upper_bits(rows_n)]
    names += [(kind, bit) for kind in ("rs", "rd") for bit in all_bits(rows_n)]
    names += [(kind, bit) for kind in ("cs", "cd", "q1", "q2") for bit in all_bits(cols_n)]
    return names


def prep_kernel(order, ranks, u, v, *refs, rows_n, cols_n):
    flags, rs_uk, rs_ug, rd_uk, rd_ug, rs_vk, rs_vg, rd_vk, rd_vg, cu_k, cu_g, cv_k, cv_g, held, v_sem, u_sems = refs
    rows, cols = u.shape[:2]
    rank, width = v.shape[2:]
    me_row, me_col = lax.axis_index("row"), lax.axis_index("col")
    row_first = order[0, 0] == rows_n * rows - 1
    row_other = jnp.where(row_first, order[1, 0], order[0, 0])
    col_other = jnp.where(order[0, 1] == cols_n * cols - 1, order[1, 1], order[0, 1])
    row_dyn, col_dyn = lax.rem(row_other, rows), lax.rem(col_other, cols)
    row_side, col_side = lax.rem(me_row, 2), lax.rem(me_col, 2)

    fetch = pltpu.make_async_copy(v, held, v_sem)
    fetch.start()
    copies = []
    for i, outs in ((rows - 1, (rs_uk, rs_ug)), (row_dyn, (rd_uk, rd_ug))):
        for slot, j in enumerate((row_side, 1 - row_side)):
            copies.append((u.at[i, j], outs[slot]))
    for which, j in enumerate((cols - 1, col_dyn)):
        for slot, i in enumerate((col_side, 1 - col_side)):
            copies.append((u.at[i, j], (cu_k, cu_g)[slot].at[which]))
    copies = [pltpu.make_async_copy(a, b, u_sems.at[k]) for k, (a, b) in enumerate(copies)]
    for copy in copies:
        copy.start()

    q1, q2 = order[0, 1], order[1, 1]
    truth = {
        "row_first": row_first, "side_r": row_side == 0, "side_c": col_side == 0,
        "q1_side": lax.rem(q1, cols) == row_side, "q2_side": lax.rem(q2, cols) == row_side}
    for bit in all_bits(rows_n):
        truth["rs", bit] = (me_row & bit) == (rows_n - 1) & bit
        truth["p1", bit] = (me_row & bit) == (lax.div(order[0, 0], rows) & bit)
        truth["p2", bit] = (me_row & bit) == (lax.div(order[1, 0], rows) & bit)
        truth["rd", bit] = (me_row & bit) == (lax.div(row_other, rows) & bit)
    truth["rs", 1] = me_row != (rows_n - 1) ^ 1
    for bit in all_bits(cols_n):
        truth["cs", bit] = (me_col & bit) == (cols_n - 1) & bit
        for kind, where in (("cd", col_other), ("q1", q1), ("q2", q2)):
            truth[kind, bit] = (me_col & bit) == (lax.div(where, cols) & bit)
    for k, name in enumerate(flag_names(rows_n, cols_n)):
        flags[k:k + 1, :] = jnp.full((1, width), jnp.where(truth[name], 1, 0), jnp.int32)
    fetch.wait()

    def kept(i, j):
        row = lax.broadcasted_iota(jnp.int32, (rank, width), 0)
        return jnp.where(row < ranks[i, j], held[i, j], jnp.zeros((), v.dtype))

    for i, outs in ((rows - 1, (rs_vk, rs_vg)), (row_dyn, (rd_vk, rd_vg))):
        for slot, j in enumerate((row_side, 1 - row_side)):
            outs[slot][...] = kept(i, j)
    for which, j in enumerate((cols - 1, col_dyn)):
        for slot, i in enumerate((col_side, 1 - col_side)):
            value = kept(i, j)
            for k in range(width // rank):
                (cv_k, cv_g)[slot][which, k * rank:(k + 1) * rank, :] = value[:, k * rank:(k + 1) * rank]
    for copy in copies:
        copy.wait()


def solve_kernel(order, inverses, fixed, moving, out, *, last_row):
    fixed_first = order[0, 0] == last_row
    out[0] = dot(inverses[0], jnp.where(fixed_first, fixed[...], moving[...])).astype(BF16)
    out[1] = dot(inverses[1], jnp.where(fixed_first, moving[...], fixed[...])).astype(BF16)


def core_kernel(order, solved, first, second, out, foot, *, last_col):
    rank = out.shape[2]
    count = solved.shape[1] // rank
    me = lax.axis_index("row")
    step_of = jnp.where(order[0, 1] == last_col, 0, 1)
    for s in range(2):
        which = step_of if s == 0 else 1 - step_of
        lines = [
            jnp.concatenate([tiles[which + far, k * rank:(k + 1) * rank, :] for k in range(count)], axis=1)
            for far in (0, 2) for tiles in (first, second)]
        out[s] = dot(jnp.concatenate(lines, axis=0), solved[s]).astype(BF16)
        row = order[1 - s, 0]
        far = lax.rem(lax.div(row, 2) + me, 2)
        foot[s] = out[s, pl.ds(pl.multiple_of((2 * far + lax.rem(row, 2)) * rank, rank), rank), :]


def final_kernel(order, ranks, u, v, first, second, vp1, vp2, cores, swapped, edge, out, *, last_col):
    i, j = pl.program_id(0), pl.program_id(1)
    rank, width = v.shape[2:]
    row = lax.axis_index("row") * pl.num_programs(0) + i
    col = lax.axis_index("col") * pl.num_programs(1) + j
    open1 = jnp.logical_and(row != order[0, 0], col != order[0, 1])
    open2 = jnp.logical_and(open1, jnp.logical_and(row != order[1, 0], col != order[1, 1]))
    m1 = jnp.where(open1, F32(1), F32(0))
    m2 = jnp.where(open2, F32(1), F32(0))
    foot = (cores.shape[1] // rank - 1) * rank
    top = pl.ds(pl.multiple_of(i * rank, rank), rank)
    below = pl.ds(pl.multiple_of(2 * rank + i * rank, rank), rank)

    here = j == lax.rem(lax.axis_index("row"), 2)

    def left(s, lines):
        return jnp.where(here, cores[s, lines, :], swapped[s, lines, :])

    c1_ij, c1_iq2, c1_p2j = left(0, top), edge[top], left(0, pl.ds(foot, rank))
    high_a, high_b = left(1, top), edge[below]
    low_a = -dot(c1_iq2, left(1, pl.ds(foot, rank)))
    low_b = -dot(c1_iq2, edge[4 * rank:])
    q1p1 = m2 * dot(low_b.astype(BF16), c1_p2j) - m1 * c1_ij.astype(F32)
    q2p1 = m2 * dot(high_b, c1_p2j)
    mix = jnp.concatenate([
        jnp.concatenate([q1p1, -m2 * low_a], axis=1),
        jnp.concatenate([q2p1, -m2 * high_a.astype(F32)], axis=1)], axis=0).astype(BF16)
    change = dot(mix, jnp.concatenate([vp1[0], vp2[0]], axis=0)).astype(BF16)
    line = lax.broadcasted_iota(jnp.int32, (rank, width), 0)
    own = jnp.where(line < ranks[i, j], v[0, 0], jnp.zeros((), BF16))
    right = jnp.concatenate([own, change], axis=0)
    w1 = jnp.where(order[0, 1] == last_col, 0, 1)
    uq1, uq2 = (jnp.where(i == 0, first[w], second[w]) for w in (w1, 1 - w1))
    out[0, 0] = dot(jnp.concatenate([u[0, 0], uq1, uq2], axis=1), right).astype(BF16)


def make(rows_n, cols_n):
    def on_device(tile_u, tile_v, tile_ranks, inverses, panel_order):
        rows, cols, width, rank = tile_u.shape
        last = dict(last_row=rows_n * rows - 1, last_col=cols_n * cols - 1)
        tall = jax.ShapeDtypeStruct((width, rank), BF16)
        flat = jax.ShapeDtypeStruct((rank, width), BF16)
        pair = jax.ShapeDtypeStruct((2, width, rank), BF16)
        anywhere = pl.BlockSpec(memory_space=pl.ANY)
        names = flag_names(rows_n, cols_n)
        cut = pl.pallas_call(
            functools.partial(prep_kernel, rows_n=rows_n, cols_n=cols_n),
            out_shape=[jax.ShapeDtypeStruct((len(names), width), jnp.int32)] + [tall] * 4 + [flat] * 4 + [pair] * 4,
            in_specs=[SCALARS, SCALARS, anywhere, anywhere],
            out_specs=[WHOLE] * 13,
            scratch_shapes=[pltpu.VMEM(tile_v.shape, BF16), pltpu.SemaphoreType.DMA(()), pltpu.SemaphoreType.DMA((8,))],
            compiler_params=params(),
        )(panel_order, tile_ranks, tile_u, tile_v)
        flags, rs_uk, rs_ug, rd_uk, rd_ug, rs_vk, rs_vg, rd_vk, rd_vg, cu_k, cu_g, cv_k, cv_g = cut

        def flag(name, like):
            k = names.index(name)
            return flags[k:k + 1, :like.shape[-1]] != 0

        def choose(name, one, two):
            return jnp.where(flag(name, one), one, two)

        def same(kind):
            return lambda bit, like: flag((kind, bit), like)

        def lanes(fixed_keep, fixed_give, moving_keep, moving_give, first=None):
            lane = Lane(moving_keep, moving_give, "row", rows_n, same("rd"))
            return lane, Lane(fixed_keep, after(fixed_give, lane.mine if first is None else first), "row", rows_n, same("rs"), rows_n - 1)

        def joined(mine, axis, n, side):
            other = swap(mine, axis, n, 1)
            return choose(side, mine, other), choose(side, other, mine)

        def same_both(bit, like):
            return jnp.stack([flag(("cs", bit), like), flag(("cd", bit), like)])

        def mines(pair):
            return [lane.mine for lane in pair]

        u_lanes = lanes(rs_uk, rs_ug, rd_uk, rd_ug)
        cv = Lane(cv_k, cv_g, "col", cols_n, same_both)
        ties = [cv.mine]
        for k in range(len(upper_bits(rows_n))):
            for lane in u_lanes:
                lane.step(k, *ties)
            ties = []
            follow = mines(u_lanes)
            if k == 0:
                v_lanes = lanes(rs_vk, rs_vg, rd_vk, after(rd_vg, u_lanes[0].mine), u_lanes[0].mine)
                for m in range(len(cv.bits)):
                    cv.step(m)
                near = swap(cv.mine, "row", rows_n, 1)
                cu = Lane(cu_k, after(cu_g, cv.mine), "col", cols_n, same_both)
                follow.append(near)
                cv_first, cv_second = joined(jnp.concatenate([cv.mine, near]), "col", cols_n, "side_c")
            else:
                follow.append(cv_first)
            for lane in v_lanes:
                lane.step(k, *follow)
        for m in range(len(cu.bits)):
            cu.step(m)
        cu_first, cu_second = joined(cu.mine, "col", cols_n, "side_c")

        moving, fixed = mines(u_lanes)
        solved = pl.pallas_call(
            functools.partial(solve_kernel, last_row=last["last_row"]),
            out_shape=jax.ShapeDtypeStruct((2, width, rank), BF16),
            in_specs=[SCALARS] + [WHOLE] * 3,
            out_specs=WHOLE,
            compiler_params=params(),
        )(panel_order, inverses, fixed, moving)
        cores, foot = pl.pallas_call(
            functools.partial(core_kernel, last_col=last["last_col"]),
            out_shape=[jax.ShapeDtypeStruct((2, 4 * rank, rank), BF16), jax.ShapeDtypeStruct((2, rank, rank), BF16)],
            in_specs=[SCALARS] + [WHOLE] * 3,
            out_specs=[WHOLE] * 2,
            compiler_params=params(),
        )(panel_order, solved, cv_first, cv_second)
        def at_root(bit):
            return jnp.stack([flag(("p2", bit), foot), flag(("p1", bit), foot)])

        bits = upper_bits(rows_n)
        if len(bits) == 2:
            one, two, three = (swap(foot, "row", rows_n, bit) for bit in (*bits, sum(bits)))
            foot = jnp.where(at_root(bits[1]), jnp.where(at_root(bits[0]), foot, one), jnp.where(at_root(bits[0]), two, three))
        else:
            for bit in bits:
                foot = jnp.where(at_root(bit), foot, swap(foot, "row", rows_n, bit))
        swapped = swap(jnp.concatenate([cores[:, 2 * rank:], foot], axis=1), "row", rows_n, 1)
        cores = jnp.concatenate([cores[:, :2 * rank], foot], axis=1)
        edge = jnp.concatenate([choose("q2_side", cores[0, :2 * rank], swapped[0, :2 * rank]), choose("q1_side", cores[1], swapped[1])])
        for bit in all_bits(cols_n):
            got = swap(edge, "col", cols_n, bit)
            early = jnp.arange(5 * rank)[:, None] < 2 * rank
            stays = jnp.where(early, flag(("q2", bit), edge), flag(("q1", bit), edge))
            edge = jnp.where(stays, edge, got)

        moving, fixed = (after(x, foot) for x in mines(v_lanes))
        mine = jnp.stack([choose("row_first", fixed, moving), choose("row_first", moving, fixed)])
        vj0, vj1 = joined(mine, "row", rows_n, "side_r")
        vp1, vp2 = (jnp.stack([vj0[s], vj1[s]]) for s in range(2))

        return pl.pallas_call(
            functools.partial(final_kernel, last_col=last["last_col"]),
            out_shape=jax.ShapeDtypeStruct((rows, cols, width, width), BF16),
            grid=(rows, cols),
            in_specs=[
                SCALARS, SCALARS,
                pl.BlockSpec((1, 1, width, rank), lambda i, j: (i, j, 0, 0)),
                pl.BlockSpec((1, 1, rank, width), lambda i, j: (i, j, 0, 0)),
                WHOLE, WHOLE,
                pl.BlockSpec((1, rank, width), lambda i, j: (j, 0, 0)),
                pl.BlockSpec((1, rank, width), lambda i, j: (j, 0, 0)),
                WHOLE, WHOLE, WHOLE],
            out_specs=pl.BlockSpec((1, 1, width, width), lambda i, j: (i, j, 0, 0)),
            compiler_params=params(),
        )(panel_order, tile_ranks, tile_u, tile_v, cu_first, cu_second, vp1, vp2, cores, swapped, edge)

    return on_device


def solution(mesh):
    placed = (P("row", "col", None, None), P("row", "col", None, None), P("row", "col"), P(), P())
    return jax.shard_map(
        make(mesh.shape["row"], mesh.shape["col"]),
        mesh=mesh,
        in_specs=placed,
        out_specs=P("row", "col", None, None),
        check_vma=False,
    )
```

```python
import functools

import jax
import jax.numpy as jnp
from jax import lax
from jax.experimental import pallas as pl
from jax.experimental.pallas import tpu as pltpu
from jax.sharding import PartitionSpec as P

F32 = jnp.float32
BF16 = jnp.bfloat16
VMEM_BYTES = 48 * 1024 * 1024
WHOLE = pl.BlockSpec(memory_space=pltpu.VMEM)
SCALARS = pl.BlockSpec(memory_space=pltpu.SMEM)


def params():
    return pltpu.CompilerParams(vmem_limit_bytes=VMEM_BYTES)


def dot(a, b):
    return jnp.dot(a, b, preferred_element_type=F32)


def swap(block, axis, n, bit, senders=None):
    senders = range(n) if senders is None else sorted(senders)
    return lax.ppermute(block, axis, [(s, s ^ bit) for s in senders])


def upper_bits(n):
    return [1 << b for b in range(1, n.bit_length() - 1)]


def after(value, *others):
    return lax.optimization_barrier((value,) + others)[0]


def all_bits(n):
    return [1] + upper_bits(n)


class Lane:
    def __init__(self, keep, give, axis, n, same, root=None, got=None):
        self.mine, self.axis, self.n, self.same = keep, axis, n, same
        self.holders = None if root is None else {root}
        self.bits = upper_bits(n) if root is None else upper_bits(n)[::-1]
        self.move(1, give, got)

    def move(self, bit, value, got=None):
        got = swap(value, self.axis, self.n, bit, self.holders) if got is None else got
        if self.holders:
            self.holders = self.holders | {h ^ bit for h in self.holders}
        self.mine = jnp.where(self.same(bit, self.mine), self.mine, got)

    def step(self, k, *others):
        if others:
            self.mine = after(self.mine, *others)
        self.move(self.bits[k], self.mine)


def flag_names(rows_n, cols_n):
    names = ["row_first", "side_r", "side_c", "q1_side", "q2_side"]
    names += [(kind, bit) for kind in ("p1", "p2") for bit in upper_bits(rows_n)]
    names += [(kind, bit) for kind in ("rs", "rd") for bit in all_bits(rows_n)]
    names += [(kind, bit) for kind in ("cs", "cd", "q1", "q2") for bit in all_bits(cols_n)]
    return names


def prep_kernel(order, ranks, u, v, *refs, rows_n, cols_n):
    flags, rs_uk, rs_ug, rd_uk, rd_ug, rs_vk, rs_vg, rd_vk, rd_vg, cu_k, cu_g, cv_k, cv_g, held, v_sem, u_sems = refs
    rows, cols = u.shape[:2]
    rank, width = v.shape[2:]
    me_row, me_col = lax.axis_index("row"), lax.axis_index("col")
    row_first = order[0, 0] == rows_n * rows - 1
    row_other = jnp.where(row_first, order[1, 0], order[0, 0])
    col_other = jnp.where(order[0, 1] == cols_n * cols - 1, order[1, 1], order[0, 1])
    row_dyn, col_dyn = lax.rem(row_other, rows), lax.rem(col_other, cols)
    row_side, col_side = lax.rem(me_row, 2), lax.rem(me_col, 2)

    fetch = pltpu.make_async_copy(v, held, v_sem)
    fetch.start()
    copies = []
    for i, outs in ((rows - 1, (rs_uk, rs_ug)), (row_dyn, (rd_uk, rd_ug))):
        for slot, j in enumerate((row_side, 1 - row_side)):
            copies.append((u.at[i, j], outs[slot]))
    for which, j in enumerate((cols - 1, col_dyn)):
        for slot, i in enumerate((col_side, 1 - col_side)):
            copies.append((u.at[i, j], (cu_k, cu_g)[slot].at[which]))
    copies = [pltpu.make_async_copy(a, b, u_sems.at[k]) for k, (a, b) in enumerate(copies)]
    for copy in copies:
        copy.start()

    q1, q2 = order[0, 1], order[1, 1]
    truth = {
        "row_first": row_first, "side_r": row_side == 0, "side_c": col_side == 0,
        "q1_side": lax.rem(q1, cols) == row_side, "q2_side": lax.rem(q2, cols) == row_side}
    for bit in all_bits(rows_n):
        truth["rs", bit] = (me_row & bit) == (rows_n - 1) & bit
        truth["p1", bit] = (me_row & bit) == (lax.div(order[0, 0], rows) & bit)
        truth["p2", bit] = (me_row & bit) == (lax.div(order[1, 0], rows) & bit)
        truth["rd", bit] = (me_row & bit) == (lax.div(row_other, rows) & bit)
    truth["rs", 1] = me_row != (rows_n - 1) ^ 1
    for bit in all_bits(cols_n):
        truth["cs", bit] = (me_col & bit) == (cols_n - 1) & bit
        for kind, where in (("cd", col_other), ("q1", q1), ("q2", q2)):
            truth[kind, bit] = (me_col & bit) == (lax.div(where, cols) & bit)
    for k, name in enumerate(flag_names(rows_n, cols_n)):
        flags[k:k + 1, :] = jnp.full((1, width), jnp.where(truth[name], 1, 0), jnp.int32)
    fetch.wait()

    def kept(i, j):
        row = lax.broadcasted_iota(jnp.int32, (rank, width), 0)
        return jnp.where(row < ranks[i, j], held[i, j], jnp.zeros((), v.dtype))

    for i, outs in ((rows - 1, (rs_vk, rs_vg)), (row_dyn, (rd_vk, rd_vg))):
        for slot, j in enumerate((row_side, 1 - row_side)):
            outs[slot][...] = kept(i, j)
    for which, j in enumerate((cols - 1, col_dyn)):
        for slot, i in enumerate((col_side, 1 - col_side)):
            value = kept(i, j)
            for k in range(width // rank):
                (cv_k, cv_g)[slot][which, k * rank:(k + 1) * rank, :] = value[:, k * rank:(k + 1) * rank]
    for copy in copies:
        copy.wait()


def solve_kernel(order, inverses, fixed, moving, out, *, last_row):
    fixed_first = order[0, 0] == last_row
    out[0] = dot(inverses[0], jnp.where(fixed_first, fixed[...], moving[...])).astype(BF16)
    out[1] = dot(inverses[1], jnp.where(fixed_first, moving[...], fixed[...])).astype(BF16)


def core_kernel(order, solved, first, second, out, foot, *, last_col):
    rank = out.shape[2]
    count = solved.shape[1] // rank
    me = lax.axis_index("row")
    step_of = jnp.where(order[0, 1] == last_col, 0, 1)
    for s in range(2):
        which = step_of if s == 0 else 1 - step_of
        lines = [
            jnp.concatenate([tiles[which + far, k * rank:(k + 1) * rank, :] for k in range(count)], axis=1)
            for far in (0, 2) for tiles in (first, second)]
        out[s] = dot(jnp.concatenate(lines, axis=0), solved[s]).astype(BF16)
        row = order[1 - s, 0]
        far = lax.rem(lax.div(row, 2) + me, 2)
        foot[s] = out[s, pl.ds(pl.multiple_of((2 * far + lax.rem(row, 2)) * rank, rank), rank), :]


def final_kernel(order, ranks, u, v, first, second, vp1, vp2, cores, swapped, edge, out, *, last_col):
    i, j = pl.program_id(0), pl.program_id(1)
    rank, width = v.shape[2:]
    row = lax.axis_index("row") * pl.num_programs(0) + i
    col = lax.axis_index("col") * pl.num_programs(1) + j
    open1 = jnp.logical_and(row != order[0, 0], col != order[0, 1])
    open2 = jnp.logical_and(open1, jnp.logical_and(row != order[1, 0], col != order[1, 1]))
    m1 = jnp.where(open1, F32(1), F32(0))
    m2 = jnp.where(open2, F32(1), F32(0))
    foot = (cores.shape[1] // rank - 1) * rank
    top = pl.ds(pl.multiple_of(i * rank, rank), rank)
    below = pl.ds(pl.multiple_of(2 * rank + i * rank, rank), rank)

    here = j == lax.rem(lax.axis_index("row"), 2)

    def left(s, lines):
        return jnp.where(here, cores[s, lines, :], swapped[s, lines, :])

    c1_ij, c1_iq2, c1_p2j = left(0, top), edge[top], left(0, pl.ds(foot, rank))
    high_a, high_b = left(1, top), edge[below]
    low_a = -dot(c1_iq2, left(1, pl.ds(foot, rank)))
    low_b = -dot(c1_iq2, edge[4 * rank:])
    q1p1 = m2 * dot(low_b.astype(BF16), c1_p2j) - m1 * c1_ij.astype(F32)
    q2p1 = m2 * dot(high_b, c1_p2j)
    mix = jnp.concatenate([
        jnp.concatenate([q1p1, -m2 * low_a], axis=1),
        jnp.concatenate([q2p1, -m2 * high_a.astype(F32)], axis=1)], axis=0).astype(BF16)
    change = dot(mix, jnp.concatenate([vp1[0], vp2[0]], axis=0)).astype(BF16)
    line = lax.broadcasted_iota(jnp.int32, (rank, width), 0)
    own = jnp.where(line < ranks[i, j], v[0, 0], jnp.zeros((), BF16))
    right = jnp.concatenate([own, change], axis=0)
    w1 = jnp.where(order[0, 1] == last_col, 0, 1)
    uq1, uq2 = (jnp.where(i == 0, first[w], second[w]) for w in (w1, 1 - w1))
    out[0, 0] = dot(jnp.concatenate([u[0, 0], uq1, uq2], axis=1), right).astype(BF16)


def make(rows_n, cols_n):
    def on_device(tile_u, tile_v, tile_ranks, inverses, panel_order):
        rows, cols, width, rank = tile_u.shape
        last = dict(last_row=rows_n * rows - 1, last_col=cols_n * cols - 1)
        tall = jax.ShapeDtypeStruct((width, rank), BF16)
        flat = jax.ShapeDtypeStruct((rank, width), BF16)
        pair = jax.ShapeDtypeStruct((2, width, rank), BF16)
        anywhere = pl.BlockSpec(memory_space=pl.ANY)
        names = flag_names(rows_n, cols_n)
        cut = pl.pallas_call(
            functools.partial(prep_kernel, rows_n=rows_n, cols_n=cols_n),
            out_shape=[jax.ShapeDtypeStruct((len(names), width), jnp.int32)] + [tall] * 4 + [flat] * 4 + [pair] * 4,
            in_specs=[SCALARS, SCALARS, anywhere, anywhere],
            out_specs=[WHOLE] * 13,
            scratch_shapes=[pltpu.VMEM(tile_v.shape, BF16), pltpu.SemaphoreType.DMA(()), pltpu.SemaphoreType.DMA((8,))],
            compiler_params=params(),
        )(panel_order, tile_ranks, tile_u, tile_v)
        flags, rs_uk, rs_ug, rd_uk, rd_ug, rs_vk, rs_vg, rd_vk, rd_vg, cu_k, cu_g, cv_k, cv_g = cut

        def flag(name, like):
            k = names.index(name)
            return flags[k:k + 1, :like.shape[-1]] != 0

        def choose(name, one, two):
            return jnp.where(flag(name, one), one, two)

        def same(kind):
            return lambda bit, like: flag((kind, bit), like)

        def lanes(fixed_keep, fixed_give, moving_keep, moving_give, first=None):
            lane = Lane(moving_keep, moving_give, "row", rows_n, same("rd"))
            return lane, Lane(fixed_keep, after(fixed_give, lane.mine if first is None else first), "row", rows_n, same("rs"), rows_n - 1)

        def joined(mine, axis, n, side):
            other = swap(mine, axis, n, 1)
            return choose(side, mine, other), choose(side, other, mine)

        def same_both(bit, like):
            return jnp.stack([flag(("cs", bit), like), flag(("cd", bit), like)])

        def mines(pair):
            return [lane.mine for lane in pair]

        u_lanes = lanes(rs_uk, rs_ug, rd_uk, rd_ug)
        cv = Lane(cv_k, cv_g, "col", cols_n, same_both)
        ties = [cv.mine]
        for k in range(len(upper_bits(rows_n))):
            for lane in u_lanes:
                lane.step(k, *ties)
            ties = []
            follow = mines(u_lanes)
            if k == 0:
                v_lanes = lanes(rs_vk, rs_vg, rd_vk, after(rd_vg, u_lanes[0].mine), u_lanes[0].mine)
                for m in range(len(cv.bits)):
                    cv.step(m)
                cu = Lane(cu_k, after(cu_g, cv.mine), "col", cols_n, same_both)
                near = swap(after(cv.mine, v_lanes[0].mine), "row", rows_n, 1)
                cv_first, cv_second = joined(jnp.concatenate([cv.mine, near]), "col", cols_n, "side_c")
            for lane in v_lanes:
                lane.step(k, *follow)
        for m in range(len(cu.bits)):
            cu.step(m)
        cu_first, cu_second = joined(cu.mine, "col", cols_n, "side_c")

        moving, fixed = mines(u_lanes)
        solved = pl.pallas_call(
            functools.partial(solve_kernel, last_row=last["last_row"]),
            out_shape=jax.ShapeDtypeStruct((2, width, rank), BF16),
            in_specs=[SCALARS] + [WHOLE] * 3,
            out_specs=WHOLE,
            compiler_params=params(),
        )(panel_order, inverses, fixed, moving)
        cores, foot = pl.pallas_call(
            functools.partial(core_kernel, last_col=last["last_col"]),
            out_shape=[jax.ShapeDtypeStruct((2, 4 * rank, rank), BF16), jax.ShapeDtypeStruct((2, rank, rank), BF16)],
            in_specs=[SCALARS] + [WHOLE] * 3,
            out_specs=[WHOLE] * 2,
            compiler_params=params(),
        )(panel_order, solved, cv_first, cv_second)
        def at_root(bit):
            return jnp.stack([flag(("p2", bit), foot), flag(("p1", bit), foot)])

        bits = upper_bits(rows_n)
        if len(bits) == 2:
            one, two, three = (swap(foot, "row", rows_n, bit) for bit in (*bits, sum(bits)))
            foot = jnp.where(at_root(bits[1]), jnp.where(at_root(bits[0]), foot, one), jnp.where(at_root(bits[0]), two, three))
        else:
            for bit in bits:
                foot = jnp.where(at_root(bit), foot, swap(foot, "row", rows_n, bit))
        swapped = swap(jnp.concatenate([cores[:, 2 * rank:], foot], axis=1), "row", rows_n, 1)
        cores = jnp.concatenate([cores[:, :2 * rank], foot], axis=1)
        edge = jnp.concatenate([choose("q2_side", cores[0, :2 * rank], swapped[0, :2 * rank]), choose("q1_side", cores[1], swapped[1])])
        for bit in all_bits(cols_n):
            got = swap(edge, "col", cols_n, bit)
            early = jnp.arange(5 * rank)[:, None] < 2 * rank
            stays = jnp.where(early, flag(("q2", bit), edge), flag(("q1", bit), edge))
            edge = jnp.where(stays, edge, got)

        moving, fixed = (after(x, foot) for x in mines(v_lanes))
        mine = jnp.stack([choose("row_first", fixed, moving), choose("row_first", moving, fixed)])
        vj0, vj1 = joined(mine, "row", rows_n, "side_r")
        vp1, vp2 = (jnp.stack([vj0[s], vj1[s]]) for s in range(2))

        return pl.pallas_call(
            functools.partial(final_kernel, last_col=last["last_col"]),
            out_shape=jax.ShapeDtypeStruct((rows, cols, width, width), BF16),
            grid=(rows, cols),
            in_specs=[
                SCALARS, SCALARS,
                pl.BlockSpec((1, 1, width, rank), lambda i, j: (i, j, 0, 0)),
                pl.BlockSpec((1, 1, rank, width), lambda i, j: (i, j, 0, 0)),
                WHOLE, WHOLE,
                pl.BlockSpec((1, rank, width), lambda i, j: (j, 0, 0)),
                pl.BlockSpec((1, rank, width), lambda i, j: (j, 0, 0)),
                WHOLE, WHOLE, WHOLE],
            out_specs=pl.BlockSpec((1, 1, width, width), lambda i, j: (i, j, 0, 0)),
            compiler_params=params(),
        )(panel_order, tile_ranks, tile_u, tile_v, cu_first, cu_second, vp1, vp2, cores, swapped, edge)

    return on_device


def solution(mesh):
    placed = (P("row", "col", None, None), P("row", "col", None, None), P("row", "col"), P(), P())
    return jax.shard_map(
        make(mesh.shape["row"], mesh.shape["col"]),
        mesh=mesh,
        in_specs=placed,
        out_specs=P("row", "col", None, None),
        check_vma=False,
    )
```

```python
import functools

import jax
import jax.numpy as jnp
from jax import lax
from jax.experimental import pallas as pl
from jax.experimental.pallas import tpu as pltpu
from jax.sharding import PartitionSpec as P

F32 = jnp.float32
BF16 = jnp.bfloat16
VMEM_BYTES = 48 * 1024 * 1024
WHOLE = pl.BlockSpec(memory_space=pltpu.VMEM)
SCALARS = pl.BlockSpec(memory_space=pltpu.SMEM)


def params():
    return pltpu.CompilerParams(vmem_limit_bytes=VMEM_BYTES)


def dot(a, b):
    return jnp.dot(a, b, preferred_element_type=F32)


def swap(block, axis, n, bit, senders=None):
    senders = range(n) if senders is None else sorted(senders)
    return lax.ppermute(block, axis, [(s, s ^ bit) for s in senders])


def upper_bits(n):
    return [1 << b for b in range(1, n.bit_length() - 1)]


def after(value, *others):
    return lax.optimization_barrier((value,) + others)[0]


def all_bits(n):
    return [1] + upper_bits(n)


class Lane:
    def __init__(self, keep, give, axis, n, same, root=None, got=None):
        self.mine, self.axis, self.n, self.same = keep, axis, n, same
        self.holders = None if root is None else {root}
        self.bits = upper_bits(n) if root is None else upper_bits(n)[::-1]
        self.move(1, give, got)

    def move(self, bit, value, got=None):
        got = swap(value, self.axis, self.n, bit, self.holders) if got is None else got
        if self.holders:
            self.holders = self.holders | {h ^ bit for h in self.holders}
        self.mine = jnp.where(self.same(bit, self.mine), self.mine, got)

    def step(self, k, *others):
        if others:
            self.mine = after(self.mine, *others)
        self.move(self.bits[k], self.mine)


def flag_names(rows_n, cols_n):
    names = ["row_first", "side_r", "side_c", "q1_side", "q2_side"]
    names += [(kind, bit) for kind in ("p1", "p2") for bit in upper_bits(rows_n)]
    names += [(kind, bit) for kind in ("rs", "rd") for bit in all_bits(rows_n)]
    names += [(kind, bit) for kind in ("cs", "cd", "q1", "q2") for bit in all_bits(cols_n)]
    return names


def prep_kernel(order, ranks, u, v, *refs, rows_n, cols_n):
    flags, rs_uk, rs_ug, rd_uk, rd_ug, rs_vk, rs_vg, rd_vk, rd_vg, cu_k, cu_g, cv_k, cv_g, held, v_sem, u_sems = refs
    rows, cols = u.shape[:2]
    rank, width = v.shape[2:]
    me_row, me_col = lax.axis_index("row"), lax.axis_index("col")
    row_first = order[0, 0] == rows_n * rows - 1
    row_other = jnp.where(row_first, order[1, 0], order[0, 0])
    col_other = jnp.where(order[0, 1] == cols_n * cols - 1, order[1, 1], order[0, 1])
    row_dyn, col_dyn = lax.rem(row_other, rows), lax.rem(col_other, cols)
    row_side, col_side = lax.rem(me_row, 2), lax.rem(me_col, 2)

    fetch = pltpu.make_async_copy(v, held, v_sem)
    fetch.start()
    copies = []
    for i, outs in ((rows - 1, (rs_uk, rs_ug)), (row_dyn, (rd_uk, rd_ug))):
        for slot, j in enumerate((row_side, 1 - row_side)):
            copies.append((u.at[i, j], outs[slot]))
    for which, j in enumerate((cols - 1, col_dyn)):
        for slot, i in enumerate((col_side, 1 - col_side)):
            copies.append((u.at[i, j], (cu_k, cu_g)[slot].at[which]))
    copies = [pltpu.make_async_copy(a, b, u_sems.at[k]) for k, (a, b) in enumerate(copies)]
    for copy in copies:
        copy.start()

    q1, q2 = order[0, 1], order[1, 1]
    truth = {
        "row_first": row_first, "side_r": row_side == 0, "side_c": col_side == 0,
        "q1_side": lax.rem(q1, cols) == row_side, "q2_side": lax.rem(q2, cols) == row_side}
    for bit in all_bits(rows_n):
        truth["rs", bit] = (me_row & bit) == (rows_n - 1) & bit
        truth["p1", bit] = (me_row & bit) == (lax.div(order[0, 0], rows) & bit)
        truth["p2", bit] = (me_row & bit) == (lax.div(order[1, 0], rows) & bit)
        truth["rd", bit] = (me_row & bit) == (lax.div(row_other, rows) & bit)
    truth["rs", 1] = me_row != (rows_n - 1) ^ 1
    for bit in all_bits(cols_n):
        truth["cs", bit] = (me_col & bit) == (cols_n - 1) & bit
        for kind, where in (("cd", col_other), ("q1", q1), ("q2", q2)):
            truth[kind, bit] = (me_col & bit) == (lax.div(where, cols) & bit)
    for k, name in enumerate(flag_names(rows_n, cols_n)):
        flags[k:k + 1, :] = jnp.full((1, width), jnp.where(truth[name], 1, 0), jnp.int32)
    fetch.wait()

    def kept(i, j):
        row = lax.broadcasted_iota(jnp.int32, (rank, width), 0)
        return jnp.where(row < ranks[i, j], held[i, j], jnp.zeros((), v.dtype))

    for i, outs in ((rows - 1, (rs_vk, rs_vg)), (row_dyn, (rd_vk, rd_vg))):
        for slot, j in enumerate((row_side, 1 - row_side)):
            outs[slot][...] = kept(i, j)
    for which, j in enumerate((cols - 1, col_dyn)):
        for slot, i in enumerate((col_side, 1 - col_side)):
            value = kept(i, j)
            for k in range(width // rank):
                (cv_k, cv_g)[slot][which, k * rank:(k + 1) * rank, :] = value[:, k * rank:(k + 1) * rank]
    for copy in copies:
        copy.wait()


def solve_kernel(order, inverses, fixed, moving, out, *, last_row):
    fixed_first = order[0, 0] == last_row
    out[0] = dot(inverses[0], jnp.where(fixed_first, fixed[...], moving[...])).astype(BF16)
    out[1] = dot(inverses[1], jnp.where(fixed_first, moving[...], fixed[...])).astype(BF16)


def core_kernel(order, solved, first, second, out, foot, *, last_col):
    rank = out.shape[2]
    count = solved.shape[1] // rank
    me = lax.axis_index("row")
    step_of = jnp.where(order[0, 1] == last_col, 0, 1)
    for s in range(2):
        which = step_of if s == 0 else 1 - step_of
        lines = [
            jnp.concatenate([tiles[which + far, k * rank:(k + 1) * rank, :] for k in range(count)], axis=1)
            for far in (0, 2) for tiles in (first, second)]
        out[s] = dot(jnp.concatenate(lines, axis=0), solved[s]).astype(BF16)
        row = order[1 - s, 0]
        far = lax.rem(lax.div(row, 2) + me, 2)
        foot[s] = out[s, pl.ds(pl.multiple_of((2 * far + lax.rem(row, 2)) * rank, rank), rank), :]


def final_kernel(order, ranks, u, v, first, second, vp1, vp2, cores, swapped, edge, out, *, last_col):
    i, j = pl.program_id(0), pl.program_id(1)
    rank, width = v.shape[2:]
    row = lax.axis_index("row") * pl.num_programs(0) + i
    col = lax.axis_index("col") * pl.num_programs(1) + j
    open1 = jnp.logical_and(row != order[0, 0], col != order[0, 1])
    open2 = jnp.logical_and(open1, jnp.logical_and(row != order[1, 0], col != order[1, 1]))
    m1 = jnp.where(open1, F32(1), F32(0))
    m2 = jnp.where(open2, F32(1), F32(0))
    foot = (cores.shape[1] // rank - 1) * rank
    top = pl.ds(pl.multiple_of(i * rank, rank), rank)
    below = pl.ds(pl.multiple_of(2 * rank + i * rank, rank), rank)

    here = j == lax.rem(lax.axis_index("row"), 2)

    def left(s, lines):
        return jnp.where(here, cores[s, lines, :], swapped[s, lines, :])

    c1_ij, c1_iq2, c1_p2j = left(0, top), edge[top], left(0, pl.ds(foot, rank))
    high_a, high_b = left(1, top), edge[below]
    low_a = -dot(c1_iq2, left(1, pl.ds(foot, rank)))
    low_b = -dot(c1_iq2, edge[4 * rank:])
    q1p1 = m2 * dot(low_b.astype(BF16), c1_p2j) - m1 * c1_ij.astype(F32)
    q2p1 = m2 * dot(high_b, c1_p2j)
    mix = jnp.concatenate([
        jnp.concatenate([q1p1, -m2 * low_a], axis=1),
        jnp.concatenate([q2p1, -m2 * high_a.astype(F32)], axis=1)], axis=0).astype(BF16)
    change = dot(mix, jnp.concatenate([vp1[0], vp2[0]], axis=0)).astype(BF16)
    line = lax.broadcasted_iota(jnp.int32, (rank, width), 0)
    own = jnp.where(line < ranks[i, j], v[0, 0], jnp.zeros((), BF16))
    right = jnp.concatenate([own, change], axis=0)
    w1 = jnp.where(order[0, 1] == last_col, 0, 1)
    uq1, uq2 = (jnp.where(i == 0, first[w], second[w]) for w in (w1, 1 - w1))
    out[0, 0] = dot(jnp.concatenate([u[0, 0], uq1, uq2], axis=1), right).astype(BF16)


def make(rows_n, cols_n):
    def on_device(tile_u, tile_v, tile_ranks, inverses, panel_order):
        rows, cols, width, rank = tile_u.shape
        last = dict(last_row=rows_n * rows - 1, last_col=cols_n * cols - 1)
        tall = jax.ShapeDtypeStruct((width, rank), BF16)
        flat = jax.ShapeDtypeStruct((rank, width), BF16)
        pair = jax.ShapeDtypeStruct((2, width, rank), BF16)
        anywhere = pl.BlockSpec(memory_space=pl.ANY)
        names = flag_names(rows_n, cols_n)
        cut = pl.pallas_call(
            functools.partial(prep_kernel, rows_n=rows_n, cols_n=cols_n),
            out_shape=[jax.ShapeDtypeStruct((len(names), width), jnp.int32)] + [tall] * 4 + [flat] * 4 + [pair] * 4,
            in_specs=[SCALARS, SCALARS, anywhere, anywhere],
            out_specs=[WHOLE] * 13,
            scratch_shapes=[pltpu.VMEM(tile_v.shape, BF16), pltpu.SemaphoreType.DMA(()), pltpu.SemaphoreType.DMA((8,))],
            compiler_params=params(),
        )(panel_order, tile_ranks, tile_u, tile_v)
        flags, rs_uk, rs_ug, rd_uk, rd_ug, rs_vk, rs_vg, rd_vk, rd_vg, cu_k, cu_g, cv_k, cv_g = cut

        def flag(name, like):
            k = names.index(name)
            return flags[k:k + 1, :like.shape[-1]] != 0

        def choose(name, one, two):
            return jnp.where(flag(name, one), one, two)

        def same(kind):
            return lambda bit, like: flag((kind, bit), like)

        def lanes(fixed_keep, fixed_give, moving_keep, moving_give, first=None):
            lane = Lane(moving_keep, moving_give, "row", rows_n, same("rd"))
            return lane, Lane(fixed_keep, after(fixed_give, lane.mine if first is None else first), "row", rows_n, same("rs"), rows_n - 1)

        def joined(mine, axis, n, side):
            other = swap(mine, axis, n, 1)
            return choose(side, mine, other), choose(side, other, mine)

        def same_both(bit, like):
            return jnp.stack([flag(("cs", bit), like), flag(("cd", bit), like)])

        def mines(pair):
            return [lane.mine for lane in pair]

        u_lanes = lanes(rs_uk, rs_ug, rd_uk, rd_ug)
        cv = Lane(cv_k, cv_g, "col", cols_n, same_both)
        ties = [cv.mine]
        for k in range(len(upper_bits(rows_n))):
            for lane in u_lanes:
                lane.step(k, *ties)
            ties = []
            follow = mines(u_lanes)
            if k == 0:
                v_lanes = lanes(rs_vk, rs_vg, rd_vk, after(rd_vg, u_lanes[0].mine), u_lanes[0].mine)
                for m in range(len(cv.bits)):
                    cv.step(m)
                cu = Lane(cu_k, after(cu_g, cv.mine), "col", cols_n, same_both)
                near = swap(after(cv.mine, v_lanes[0].mine), "row", rows_n, 1)
                cv_first, cv_second = joined(jnp.concatenate([cv.mine, near]), "col", cols_n, "side_c")
            for lane in v_lanes:
                lane.step(k, *follow)
        for m in range(len(cu.bits)):
            cu.step(m)
        moving, fixed = mines(u_lanes)
        solved = pl.pallas_call(
            functools.partial(solve_kernel, last_row=last["last_row"]),
            out_shape=jax.ShapeDtypeStruct((2, width, rank), BF16),
            in_specs=[SCALARS] + [WHOLE] * 3,
            out_specs=WHOLE,
            compiler_params=params(),
        )(panel_order, inverses, fixed, moving)
        cores, foot = pl.pallas_call(
            functools.partial(core_kernel, last_col=last["last_col"]),
            out_shape=[jax.ShapeDtypeStruct((2, 4 * rank, rank), BF16), jax.ShapeDtypeStruct((2, rank, rank), BF16)],
            in_specs=[SCALARS] + [WHOLE] * 3,
            out_specs=[WHOLE] * 2,
            compiler_params=params(),
        )(panel_order, solved, cv_first, cv_second)
        def at_root(bit):
            return jnp.stack([flag(("p2", bit), foot), flag(("p1", bit), foot)])

        bits = upper_bits(rows_n)
        if len(bits) == 2:
            one, two, three = (swap(foot, "row", rows_n, bit) for bit in (*bits, sum(bits)))
            foot = jnp.where(at_root(bits[1]), jnp.where(at_root(bits[0]), foot, one), jnp.where(at_root(bits[0]), two, three))
        else:
            for bit in bits:
                foot = jnp.where(at_root(bit), foot, swap(foot, "row", rows_n, bit))
        cu_first, cu_second = joined(after(cu.mine, foot), "col", cols_n, "side_c")
        swapped = swap(jnp.concatenate([cores[:, 2 * rank:], foot], axis=1), "row", rows_n, 1)
        cores = jnp.concatenate([cores[:, :2 * rank], foot], axis=1)
        edge = jnp.concatenate([choose("q2_side", cores[0, :2 * rank], swapped[0, :2 * rank]), choose("q1_side", cores[1], swapped[1])])
        for bit in all_bits(cols_n):
            got = swap(edge, "col", cols_n, bit)
            early = jnp.arange(5 * rank)[:, None] < 2 * rank
            stays = jnp.where(early, flag(("q2", bit), edge), flag(("q1", bit), edge))
            edge = jnp.where(stays, edge, got)

        moving, fixed = (after(x, foot) for x in mines(v_lanes))
        mine = jnp.stack([choose("row_first", fixed, moving), choose("row_first", moving, fixed)])
        vj0, vj1 = joined(mine, "row", rows_n, "side_r")
        vp1, vp2 = (jnp.stack([vj0[s], vj1[s]]) for s in range(2))

        return pl.pallas_call(
            functools.partial(final_kernel, last_col=last["last_col"]),
            out_shape=jax.ShapeDtypeStruct((rows, cols, width, width), BF16),
            grid=(rows, cols),
            in_specs=[
                SCALARS, SCALARS,
                pl.BlockSpec((1, 1, width, rank), lambda i, j: (i, j, 0, 0)),
                pl.BlockSpec((1, 1, rank, width), lambda i, j: (i, j, 0, 0)),
                WHOLE, WHOLE,
                pl.BlockSpec((1, rank, width), lambda i, j: (j, 0, 0)),
                pl.BlockSpec((1, rank, width), lambda i, j: (j, 0, 0)),
                WHOLE, WHOLE, WHOLE],
            out_specs=pl.BlockSpec((1, 1, width, width), lambda i, j: (i, j, 0, 0)),
            compiler_params=params(),
        )(panel_order, tile_ranks, tile_u, tile_v, cu_first, cu_second, vp1, vp2, cores, swapped, edge)

    return on_device


def solution(mesh):
    placed = (P("row", "col", None, None), P("row", "col", None, None), P("row", "col"), P(), P())
    return jax.shard_map(
        make(mesh.shape["row"], mesh.shape["col"]),
        mesh=mesh,
        in_specs=placed,
        out_specs=P("row", "col", None, None),
        check_vma=False,
    )
```

```python
import functools

import jax
import jax.numpy as jnp
from jax import lax
from jax.experimental import pallas as pl
from jax.experimental.pallas import tpu as pltpu
from jax.sharding import PartitionSpec as P

F32 = jnp.float32
BF16 = jnp.bfloat16
VMEM_BYTES = 48 * 1024 * 1024
WHOLE = pl.BlockSpec(memory_space=pltpu.VMEM)
SCALARS = pl.BlockSpec(memory_space=pltpu.SMEM)


def params():
    return pltpu.CompilerParams(vmem_limit_bytes=VMEM_BYTES)


def dot(a, b):
    return jnp.dot(a, b, preferred_element_type=F32)


def swap(block, axis, n, bit, senders=None):
    senders = range(n) if senders is None else sorted(senders)
    return lax.ppermute(block, axis, [(s, s ^ bit) for s in senders])


def upper_bits(n):
    return [1 << b for b in range(1, n.bit_length() - 1)]


def after(value, *others):
    return lax.optimization_barrier((value,) + others)[0]


def all_bits(n):
    return [1] + upper_bits(n)


class Lane:
    def __init__(self, keep, give, axis, n, same, root=None, got=None):
        self.mine, self.axis, self.n, self.same = keep, axis, n, same
        self.holders = None if root is None else {root}
        self.bits = upper_bits(n) if root is None else upper_bits(n)[::-1]
        self.move(1, give, got)

    def move(self, bit, value, got=None):
        got = swap(value, self.axis, self.n, bit, self.holders) if got is None else got
        if self.holders:
            self.holders = self.holders | {h ^ bit for h in self.holders}
        self.mine = jnp.where(self.same(bit, self.mine), self.mine, got)

    def step(self, k, *others):
        if others:
            self.mine = after(self.mine, *others)
        self.move(self.bits[k], self.mine)


def flag_names(rows_n, cols_n):
    names = ["row_first", "side_r", "side_c", "q1_side", "q2_side"]
    names += [(kind, bit) for kind in ("p1", "p2") for bit in upper_bits(rows_n)]
    names += [(kind, bit) for kind in ("rs", "rd") for bit in all_bits(rows_n)]
    names += [(kind, bit) for kind in ("cs", "cd", "q1", "q2") for bit in all_bits(cols_n)]
    return names


def prep_kernel(order, ranks, u, v, *refs, rows_n, cols_n):
    flags, rs_uk, rs_ug, rd_uk, rd_ug, rs_vk, rs_vg, rd_vk, rd_vg, cu_k, cu_g, cv_k, cv_g, held, v_sem, u_sems = refs
    rows, cols = u.shape[:2]
    rank, width = v.shape[2:]
    me_row, me_col = lax.axis_index("row"), lax.axis_index("col")
    row_first = order[0, 0] == rows_n * rows - 1
    row_other = jnp.where(row_first, order[1, 0], order[0, 0])
    col_other = jnp.where(order[0, 1] == cols_n * cols - 1, order[1, 1], order[0, 1])
    row_dyn, col_dyn = lax.rem(row_other, rows), lax.rem(col_other, cols)
    row_side, col_side = lax.rem(me_row, 2), lax.rem(me_col, 2)

    fetch = pltpu.make_async_copy(v, held, v_sem)
    fetch.start()
    copies = []
    for i, outs in ((rows - 1, (rs_uk, rs_ug)), (row_dyn, (rd_uk, rd_ug))):
        for slot, j in enumerate((row_side, 1 - row_side)):
            copies.append((u.at[i, j], outs[slot]))
    for which, j in enumerate((cols - 1, col_dyn)):
        for slot, i in enumerate((col_side, 1 - col_side)):
            copies.append((u.at[i, j], (cu_k, cu_g)[slot].at[which]))
    copies = [pltpu.make_async_copy(a, b, u_sems.at[k]) for k, (a, b) in enumerate(copies)]
    for copy in copies:
        copy.start()

    q1, q2 = order[0, 1], order[1, 1]
    truth = {
        "row_first": row_first, "side_r": row_side == 0, "side_c": col_side == 0,
        "q1_side": lax.rem(q1, cols) == row_side, "q2_side": lax.rem(q2, cols) == row_side}
    for bit in all_bits(rows_n):
        truth["rs", bit] = (me_row & bit) == (rows_n - 1) & bit
        truth["p1", bit] = (me_row & bit) == (lax.div(order[0, 0], rows) & bit)
        truth["p2", bit] = (me_row & bit) == (lax.div(order[1, 0], rows) & bit)
        truth["rd", bit] = (me_row & bit) == (lax.div(row_other, rows) & bit)
    truth["rs", 1] = me_row != (rows_n - 1) ^ 1
    for bit in all_bits(cols_n):
        truth["cs", bit] = (me_col & bit) == (cols_n - 1) & bit
        for kind, where in (("cd", col_other), ("q1", q1), ("q2", q2)):
            truth[kind, bit] = (me_col & bit) == (lax.div(where, cols) & bit)
    for k, name in enumerate(flag_names(rows_n, cols_n)):
        flags[k:k + 1, :] = jnp.full((1, width), jnp.where(truth[name], 1, 0), jnp.int32)
    fetch.wait()

    def kept(i, j):
        row = lax.broadcasted_iota(jnp.int32, (rank, width), 0)
        return jnp.where(row < ranks[i, j], held[i, j], jnp.zeros((), v.dtype))

    for i, outs in ((rows - 1, (rs_vk, rs_vg)), (row_dyn, (rd_vk, rd_vg))):
        for slot, j in enumerate((row_side, 1 - row_side)):
            outs[slot][...] = kept(i, j)
    for which, j in enumerate((cols - 1, col_dyn)):
        for slot, i in enumerate((col_side, 1 - col_side)):
            value = kept(i, j)
            for k in range(width // rank):
                (cv_k, cv_g)[slot][which, k * rank:(k + 1) * rank, :] = value[:, k * rank:(k + 1) * rank]
    for copy in copies:
        copy.wait()


def solve_kernel(order, inverses, fixed, moving, out, *, last_row):
    fixed_first = order[0, 0] == last_row
    out[0] = dot(inverses[0], jnp.where(fixed_first, fixed[...], moving[...])).astype(BF16)
    out[1] = dot(inverses[1], jnp.where(fixed_first, moving[...], fixed[...])).astype(BF16)


def core_kernel(order, solved, first, second, out, foot, *, last_col):
    rank = out.shape[2]
    count = solved.shape[1] // rank
    me = lax.axis_index("row")
    step_of = jnp.where(order[0, 1] == last_col, 0, 1)
    for s in range(2):
        which = step_of if s == 0 else 1 - step_of
        lines = [
            jnp.concatenate([tiles[which + far, k * rank:(k + 1) * rank, :] for k in range(count)], axis=1)
            for far in (0, 2) for tiles in (first, second)]
        out[s] = dot(jnp.concatenate(lines, axis=0), solved[s]).astype(BF16)
        row = order[1 - s, 0]
        far = lax.rem(lax.div(row, 2) + me, 2)
        foot[s] = out[s, pl.ds(pl.multiple_of((2 * far + lax.rem(row, 2)) * rank, rank), rank), :]


def final_kernel(order, ranks, u, v, first, second, vp1, vp2, cores, swapped, edge, out, *, last_col):
    i, j = pl.program_id(0), pl.program_id(1)
    rank, width = v.shape[2:]
    row = lax.axis_index("row") * pl.num_programs(0) + i
    col = lax.axis_index("col") * pl.num_programs(1) + j
    open1 = jnp.logical_and(row != order[0, 0], col != order[0, 1])
    open2 = jnp.logical_and(open1, jnp.logical_and(row != order[1, 0], col != order[1, 1]))
    m1 = jnp.where(open1, F32(1), F32(0))
    m2 = jnp.where(open2, F32(1), F32(0))
    foot = (cores.shape[1] // rank - 1) * rank
    top = pl.ds(pl.multiple_of(i * rank, rank), rank)
    below = pl.ds(pl.multiple_of(2 * rank + i * rank, rank), rank)

    here = j == lax.rem(lax.axis_index("row"), 2)

    def left(s, lines):
        return jnp.where(here, cores[s, lines, :], swapped[s, lines, :])

    c1_ij, c1_iq2, c1_p2j = left(0, top), edge[top], left(0, pl.ds(foot, rank))
    high_a, high_b = left(1, top), edge[below]
    low_a = -dot(c1_iq2, left(1, pl.ds(foot, rank)))
    low_b = -dot(c1_iq2, edge[4 * rank:])
    q1p1 = m2 * dot(low_b.astype(BF16), c1_p2j) - m1 * c1_ij.astype(F32)
    q2p1 = m2 * dot(high_b, c1_p2j)
    mix = jnp.concatenate([
        jnp.concatenate([q1p1, -m2 * low_a], axis=1),
        jnp.concatenate([q2p1, -m2 * high_a.astype(F32)], axis=1)], axis=0).astype(BF16)
    change = dot(mix, jnp.concatenate([vp1[0], vp2[0]], axis=0)).astype(BF16)
    line = lax.broadcasted_iota(jnp.int32, (rank, width), 0)
    own = jnp.where(line < ranks[i, j], v[0, 0], jnp.zeros((), BF16))
    right = jnp.concatenate([own, change], axis=0)
    w1 = jnp.where(order[0, 1] == last_col, 0, 1)
    uq1, uq2 = (jnp.where(i == 0, first[w], second[w]) for w in (w1, 1 - w1))
    out[0, 0] = dot(jnp.concatenate([u[0, 0], uq1, uq2], axis=1), right).astype(BF16)


def make(rows_n, cols_n):
    def on_device(tile_u, tile_v, tile_ranks, inverses, panel_order):
        rows, cols, width, rank = tile_u.shape
        last = dict(last_row=rows_n * rows - 1, last_col=cols_n * cols - 1)
        tall = jax.ShapeDtypeStruct((width, rank), BF16)
        flat = jax.ShapeDtypeStruct((rank, width), BF16)
        pair = jax.ShapeDtypeStruct((2, width, rank), BF16)
        anywhere = pl.BlockSpec(memory_space=pl.ANY)
        names = flag_names(rows_n, cols_n)
        cut = pl.pallas_call(
            functools.partial(prep_kernel, rows_n=rows_n, cols_n=cols_n),
            out_shape=[jax.ShapeDtypeStruct((len(names), width), jnp.int32)] + [tall] * 4 + [flat] * 4 + [pair] * 4,
            in_specs=[SCALARS, SCALARS, anywhere, anywhere],
            out_specs=[WHOLE] * 13,
            scratch_shapes=[pltpu.VMEM(tile_v.shape, BF16), pltpu.SemaphoreType.DMA(()), pltpu.SemaphoreType.DMA((8,))],
            compiler_params=params(),
        )(panel_order, tile_ranks, tile_u, tile_v)
        flags, rs_uk, rs_ug, rd_uk, rd_ug, rs_vk, rs_vg, rd_vk, rd_vg, cu_k, cu_g, cv_k, cv_g = cut

        def flag(name, like):
            k = names.index(name)
            return flags[k:k + 1, :like.shape[-1]] != 0

        def choose(name, one, two):
            return jnp.where(flag(name, one), one, two)

        def same(kind):
            return lambda bit, like: flag((kind, bit), like)

        def lanes(fixed_keep, fixed_give, moving_keep, moving_give, first=None):
            lane = Lane(moving_keep, moving_give, "row", rows_n, same("rd"))
            return lane, Lane(fixed_keep, after(fixed_give, lane.mine if first is None else first), "row", rows_n, same("rs"), rows_n - 1)

        def joined(mine, axis, n, side):
            other = swap(mine, axis, n, 1)
            return choose(side, mine, other), choose(side, other, mine)

        def same_both(bit, like):
            return jnp.stack([flag(("cs", bit), like), flag(("cd", bit), like)])

        def mines(pair):
            return [lane.mine for lane in pair]

        u_lanes = lanes(rs_uk, rs_ug, rd_uk, rd_ug)
        cv = Lane(cv_k, cv_g, "col", cols_n, same_both)
        ties = [cv.mine]
        for k in range(len(upper_bits(rows_n))):
            for lane in u_lanes:
                lane.step(k, *ties)
            ties = []
            follow = mines(u_lanes)
            if k == 0:
                v_lanes = lanes(rs_vk, rs_vg, rd_vk, after(rd_vg, u_lanes[0].mine), u_lanes[0].mine)
                for m in range(len(cv.bits)):
                    cv.step(m)
                cu = Lane(cu_k, after(cu_g, cv.mine), "col", cols_n, same_both)
                near = swap(after(cv.mine, v_lanes[0].mine), "row", rows_n, 1)
                cv_first, cv_second = joined(jnp.concatenate([cv.mine, near]), "col", cols_n, "side_c")
            if k < len(upper_bits(rows_n)) - 1:
                for lane in v_lanes:
                    lane.step(k, *follow)
        for m in range(len(cu.bits)):
            cu.step(m)
        moving, fixed = mines(u_lanes)
        solved = pl.pallas_call(
            functools.partial(solve_kernel, last_row=last["last_row"]),
            out_shape=jax.ShapeDtypeStruct((2, width, rank), BF16),
            in_specs=[SCALARS] + [WHOLE] * 3,
            out_specs=WHOLE,
            compiler_params=params(),
        )(panel_order, inverses, fixed, moving)
        cores, foot = pl.pallas_call(
            functools.partial(core_kernel, last_col=last["last_col"]),
            out_shape=[jax.ShapeDtypeStruct((2, 4 * rank, rank), BF16), jax.ShapeDtypeStruct((2, rank, rank), BF16)],
            in_specs=[SCALARS] + [WHOLE] * 3,
            out_specs=[WHOLE] * 2,
            compiler_params=params(),
        )(panel_order, solved, cv_first, cv_second)
        for lane in v_lanes:
            lane.step(len(lane.bits) - 1, foot)

        def at_root(bit):
            return jnp.stack([flag(("p2", bit), foot), flag(("p1", bit), foot)])

        bits = upper_bits(rows_n)
        if len(bits) == 2:
            one, two, three = (swap(foot, "row", rows_n, bit) for bit in (*bits, sum(bits)))
            foot = jnp.where(at_root(bits[1]), jnp.where(at_root(bits[0]), foot, one), jnp.where(at_root(bits[0]), two, three))
        else:
            for bit in bits:
                foot = jnp.where(at_root(bit), foot, swap(foot, "row", rows_n, bit))
        cu_first, cu_second = joined(after(cu.mine, foot), "col", cols_n, "side_c")
        swapped = swap(jnp.concatenate([cores[:, 2 * rank:], foot], axis=1), "row", rows_n, 1)
        cores = jnp.concatenate([cores[:, :2 * rank], foot], axis=1)
        edge = jnp.concatenate([choose("q2_side", cores[0, :2 * rank], swapped[0, :2 * rank]), choose("q1_side", cores[1], swapped[1])])
        for bit in all_bits(cols_n):
            got = swap(edge, "col", cols_n, bit)
            early = jnp.arange(5 * rank)[:, None] < 2 * rank
            stays = jnp.where(early, flag(("q2", bit), edge), flag(("q1", bit), edge))
            edge = jnp.where(stays, edge, got)

        moving, fixed = (after(x, foot) for x in mines(v_lanes))
        mine = jnp.stack([choose("row_first", fixed, moving), choose("row_first", moving, fixed)])
        vj0, vj1 = joined(mine, "row", rows_n, "side_r")
        vp1, vp2 = (jnp.stack([vj0[s], vj1[s]]) for s in range(2))

        return pl.pallas_call(
            functools.partial(final_kernel, last_col=last["last_col"]),
            out_shape=jax.ShapeDtypeStruct((rows, cols, width, width), BF16),
            grid=(rows, cols),
            in_specs=[
                SCALARS, SCALARS,
                pl.BlockSpec((1, 1, width, rank), lambda i, j: (i, j, 0, 0)),
                pl.BlockSpec((1, 1, rank, width), lambda i, j: (i, j, 0, 0)),
                WHOLE, WHOLE,
                pl.BlockSpec((1, rank, width), lambda i, j: (j, 0, 0)),
                pl.BlockSpec((1, rank, width), lambda i, j: (j, 0, 0)),
                WHOLE, WHOLE, WHOLE],
            out_specs=pl.BlockSpec((1, 1, width, width), lambda i, j: (i, j, 0, 0)),
            compiler_params=params(),
        )(panel_order, tile_ranks, tile_u, tile_v, cu_first, cu_second, vp1, vp2, cores, swapped, edge)

    return on_device


def solution(mesh):
    placed = (P("row", "col", None, None), P("row", "col", None, None), P("row", "col"), P(), P())
    return jax.shard_map(
        make(mesh.shape["row"], mesh.shape["col"]),
        mesh=mesh,
        in_specs=placed,
        out_specs=P("row", "col", None, None),
        check_vma=False,
    )
```

```python
import functools

import jax
import jax.numpy as jnp
from jax import lax
from jax.experimental import pallas as pl
from jax.experimental.pallas import tpu as pltpu
from jax.sharding import PartitionSpec as P

F32 = jnp.float32
BF16 = jnp.bfloat16
VMEM_BYTES = 48 * 1024 * 1024
WHOLE = pl.BlockSpec(memory_space=pltpu.VMEM)
SCALARS = pl.BlockSpec(memory_space=pltpu.SMEM)


def params():
    return pltpu.CompilerParams(vmem_limit_bytes=VMEM_BYTES)


def dot(a, b):
    return jnp.dot(a, b, preferred_element_type=F32)


def swap(block, axis, n, bit, senders=None):
    senders = range(n) if senders is None else sorted(senders)
    return lax.ppermute(block, axis, [(s, s ^ bit) for s in senders])


def upper_bits(n):
    return [1 << b for b in range(1, n.bit_length() - 1)]


def after(value, *others):
    return lax.optimization_barrier((value,) + others)[0]


def all_bits(n):
    return [1] + upper_bits(n)


class Lane:
    def __init__(self, keep, give, axis, n, same, root=None, got=None):
        self.mine, self.axis, self.n, self.same = keep, axis, n, same
        self.holders = None if root is None else {root}
        self.bits = upper_bits(n) if root is None else upper_bits(n)[::-1]
        self.move(1, give, got)

    def move(self, bit, value, got=None):
        got = swap(value, self.axis, self.n, bit, self.holders) if got is None else got
        if self.holders:
            self.holders = self.holders | {h ^ bit for h in self.holders}
        self.mine = jnp.where(self.same(bit, self.mine), self.mine, got)

    def step(self, k, *others):
        if others:
            self.mine = after(self.mine, *others)
        self.move(self.bits[k], self.mine)


def flag_names(rows_n, cols_n):
    names = ["row_first", "side_r", "side_c", "q1_side", "q2_side"]
    names += [(kind, bit) for kind in ("p1", "p2") for bit in upper_bits(rows_n)]
    names += [(kind, bit) for kind in ("rs", "rd") for bit in all_bits(rows_n)]
    names += [(kind, bit) for kind in ("cs", "cd", "q1", "q2") for bit in all_bits(cols_n)]
    return names


def prep_kernel(order, ranks, u, v, *refs, rows_n, cols_n):
    flags, rs_uk, rs_ug, rd_uk, rd_ug, rs_vk, rs_vg, rd_vk, rd_vg, cu_k, cu_g, cv_k, cv_g, held, v_sem, u_sems = refs
    rows, cols = u.shape[:2]
    rank, width = v.shape[2:]
    me_row, me_col = lax.axis_index("row"), lax.axis_index("col")
    row_first = order[0, 0] == rows_n * rows - 1
    row_other = jnp.where(row_first, order[1, 0], order[0, 0])
    col_other = jnp.where(order[0, 1] == cols_n * cols - 1, order[1, 1], order[0, 1])
    row_dyn, col_dyn = lax.rem(row_other, rows), lax.rem(col_other, cols)
    row_side, col_side = lax.rem(me_row, 2), lax.rem(me_col, 2)

    fetch = pltpu.make_async_copy(v, held, v_sem)
    fetch.start()
    copies = []
    for i, outs in ((rows - 1, (rs_uk, rs_ug)), (row_dyn, (rd_uk, rd_ug))):
        for slot, j in enumerate((row_side, 1 - row_side)):
            copies.append((u.at[i, j], outs[slot]))
    for which, j in enumerate((cols - 1, col_dyn)):
        for slot, i in enumerate((col_side, 1 - col_side)):
            copies.append((u.at[i, j], (cu_k, cu_g)[slot].at[which]))
    copies = [pltpu.make_async_copy(a, b, u_sems.at[k]) for k, (a, b) in enumerate(copies)]
    for copy in copies:
        copy.start()

    q1, q2 = order[0, 1], order[1, 1]
    truth = {
        "row_first": row_first, "side_r": row_side == 0, "side_c": col_side == 0,
        "q1_side": lax.rem(q1, cols) == row_side, "q2_side": lax.rem(q2, cols) == row_side}
    for bit in all_bits(rows_n):
        truth["rs", bit] = (me_row & bit) == (rows_n - 1) & bit
        truth["p1", bit] = (me_row & bit) == (lax.div(order[0, 0], rows) & bit)
        truth["p2", bit] = (me_row & bit) == (lax.div(order[1, 0], rows) & bit)
        truth["rd", bit] = (me_row & bit) == (lax.div(row_other, rows) & bit)
    truth["rs", 1] = me_row != (rows_n - 1) ^ 1
    for bit in all_bits(cols_n):
        truth["cs", bit] = (me_col & bit) == (cols_n - 1) & bit
        for kind, where in (("cd", col_other), ("q1", q1), ("q2", q2)):
            truth[kind, bit] = (me_col & bit) == (lax.div(where, cols) & bit)
    for k, name in enumerate(flag_names(rows_n, cols_n)):
        flags[k:k + 1, :] = jnp.full((1, width), jnp.where(truth[name], 1, 0), jnp.int32)
    fetch.wait()

    def kept(i, j):
        row = lax.broadcasted_iota(jnp.int32, (rank, width), 0)
        return jnp.where(row < ranks[i, j], held[i, j], jnp.zeros((), v.dtype))

    for i, outs in ((rows - 1, (rs_vk, rs_vg)), (row_dyn, (rd_vk, rd_vg))):
        for slot, j in enumerate((row_side, 1 - row_side)):
            outs[slot][...] = kept(i, j)
    for which, j in enumerate((cols - 1, col_dyn)):
        for slot, i in enumerate((col_side, 1 - col_side)):
            value = kept(i, j)
            for k in range(width // rank):
                (cv_k, cv_g)[slot][which, k * rank:(k + 1) * rank, :] = value[:, k * rank:(k + 1) * rank]
    for copy in copies:
        copy.wait()


def solve_kernel(order, inverses, fixed, moving, out, *, last_row):
    fixed_first = order[0, 0] == last_row
    out[0] = dot(inverses[0], jnp.where(fixed_first, fixed[...], moving[...])).astype(BF16)
    out[1] = dot(inverses[1], jnp.where(fixed_first, moving[...], fixed[...])).astype(BF16)


def core_kernel(order, solved, first, second, out, foot, *, last_col):
    rank = out.shape[2]
    count = solved.shape[1] // rank
    me = lax.axis_index("row")
    step_of = jnp.where(order[0, 1] == last_col, 0, 1)
    for s in range(2):
        which = step_of if s == 0 else 1 - step_of
        lines = [
            jnp.concatenate([tiles[which + far, k * rank:(k + 1) * rank, :] for k in range(count)], axis=1)
            for far in (0, 2) for tiles in (first, second)]
        out[s] = dot(jnp.concatenate(lines, axis=0), solved[s]).astype(BF16)
        row = order[1 - s, 0]
        far = lax.rem(lax.div(row, 2) + me, 2)
        foot[s] = out[s, pl.ds(pl.multiple_of((2 * far + lax.rem(row, 2)) * rank, rank), rank), :]


def final_kernel(order, ranks, u, v, first, second, vp1, vp2, cores, swapped, edge, out, *, last_col):
    i, j = pl.program_id(0), pl.program_id(1)
    rank, width = v.shape[2:]
    row = lax.axis_index("row") * pl.num_programs(0) + i
    col = lax.axis_index("col") * pl.num_programs(1) + j
    open1 = jnp.logical_and(row != order[0, 0], col != order[0, 1])
    open2 = jnp.logical_and(open1, jnp.logical_and(row != order[1, 0], col != order[1, 1]))
    m1 = jnp.where(open1, F32(1), F32(0))
    m2 = jnp.where(open2, F32(1), F32(0))
    foot = (cores.shape[1] // rank - 1) * rank
    top = pl.ds(pl.multiple_of(i * rank, rank), rank)
    below = pl.ds(pl.multiple_of(2 * rank + i * rank, rank), rank)

    here = j == lax.rem(lax.axis_index("row"), 2)

    def left(s, lines):
        return jnp.where(here, cores[s, lines, :], swapped[s, lines, :])

    c1_ij, c1_iq2, c1_p2j = left(0, top), edge[top], left(0, pl.ds(foot, rank))
    high_a, high_b = left(1, top), edge[below]
    low_a = -dot(c1_iq2, left(1, pl.ds(foot, rank)))
    low_b = -dot(c1_iq2, edge[4 * rank:])
    q1p1 = m2 * dot(low_b.astype(BF16), c1_p2j) - m1 * c1_ij.astype(F32)
    q2p1 = m2 * dot(high_b, c1_p2j)
    mix = jnp.concatenate([
        jnp.concatenate([q1p1, -m2 * low_a], axis=1),
        jnp.concatenate([q2p1, -m2 * high_a.astype(F32)], axis=1)], axis=0).astype(BF16)
    change = dot(mix, jnp.concatenate([vp1[0], vp2[0]], axis=0)).astype(BF16)
    line = lax.broadcasted_iota(jnp.int32, (rank, width), 0)
    own = jnp.where(line < ranks[i, j], v[0, 0], jnp.zeros((), BF16))
    right = jnp.concatenate([own, change], axis=0)
    w1 = jnp.where(order[0, 1] == last_col, 0, 1)
    uq1, uq2 = (jnp.where(i == 0, first[w], second[w]) for w in (w1, 1 - w1))
    out[0, 0] = dot(jnp.concatenate([u[0, 0], uq1, uq2], axis=1), right).astype(BF16)


def make(rows_n, cols_n):
    def on_device(tile_u, tile_v, tile_ranks, inverses, panel_order):
        rows, cols, width, rank = tile_u.shape
        last = dict(last_row=rows_n * rows - 1, last_col=cols_n * cols - 1)
        tall = jax.ShapeDtypeStruct((width, rank), BF16)
        flat = jax.ShapeDtypeStruct((rank, width), BF16)
        pair = jax.ShapeDtypeStruct((2, width, rank), BF16)
        anywhere = pl.BlockSpec(memory_space=pl.ANY)
        names = flag_names(rows_n, cols_n)
        cut = pl.pallas_call(
            functools.partial(prep_kernel, rows_n=rows_n, cols_n=cols_n),
            out_shape=[jax.ShapeDtypeStruct((len(names), width), jnp.int32)] + [tall] * 4 + [flat] * 4 + [pair] * 4,
            in_specs=[SCALARS, SCALARS, anywhere, anywhere],
            out_specs=[WHOLE] * 13,
            scratch_shapes=[pltpu.VMEM(tile_v.shape, BF16), pltpu.SemaphoreType.DMA(()), pltpu.SemaphoreType.DMA((8,))],
            compiler_params=params(),
        )(panel_order, tile_ranks, tile_u, tile_v)
        flags, rs_uk, rs_ug, rd_uk, rd_ug, rs_vk, rs_vg, rd_vk, rd_vg, cu_k, cu_g, cv_k, cv_g = cut

        def flag(name, like):
            k = names.index(name)
            return flags[k:k + 1, :like.shape[-1]] != 0

        def choose(name, one, two):
            return jnp.where(flag(name, one), one, two)

        def same(kind):
            return lambda bit, like: flag((kind, bit), like)

        def lanes(fixed_keep, fixed_give, moving_keep, moving_give, first=None):
            lane = Lane(moving_keep, moving_give, "row", rows_n, same("rd"))
            return lane, Lane(fixed_keep, after(fixed_give, lane.mine if first is None else first), "row", rows_n, same("rs"), rows_n - 1)

        def joined(mine, axis, n, side):
            other = swap(mine, axis, n, 1)
            return choose(side, mine, other), choose(side, other, mine)

        def same_both(bit, like):
            return jnp.stack([flag(("cs", bit), like), flag(("cd", bit), like)])

        def mines(pair):
            return [lane.mine for lane in pair]

        u_lanes = lanes(rs_uk, rs_ug, rd_uk, rd_ug)
        cv = Lane(cv_k, cv_g, "col", cols_n, same_both)
        ties = [cv.mine]
        for k in range(len(upper_bits(rows_n))):
            for lane in u_lanes:
                lane.step(k, *ties)
            ties = []
            follow = mines(u_lanes)
            if k == 0:
                v_lanes = lanes(rs_vk, rs_vg, rd_vk, after(rd_vg, u_lanes[0].mine), u_lanes[0].mine)
                for m in range(len(cv.bits)):
                    cv.step(m)
                cu = Lane(cu_k, after(cu_g, cv.mine), "col", cols_n, same_both)
                near = swap(after(cv.mine, v_lanes[0].mine), "row", rows_n, 1)
                cv_first, cv_second = joined(jnp.concatenate([cv.mine, near]), "col", cols_n, "side_c")
            for lane in v_lanes:
                lane.step(k, *follow)
        for m in range(len(cu.bits)):
            cu.step(m)
        moving, fixed = mines(u_lanes)
        solved = pl.pallas_call(
            functools.partial(solve_kernel, last_row=last["last_row"]),
            out_shape=jax.ShapeDtypeStruct((2, width, rank), BF16),
            in_specs=[SCALARS] + [WHOLE] * 3,
            out_specs=WHOLE,
            compiler_params=params(),
        )(panel_order, inverses, fixed, moving)
        cores, foot = pl.pallas_call(
            functools.partial(core_kernel, last_col=last["last_col"]),
            out_shape=[jax.ShapeDtypeStruct((2, 4 * rank, rank), BF16), jax.ShapeDtypeStruct((2, rank, rank), BF16)],
            in_specs=[SCALARS] + [WHOLE] * 3,
            out_specs=[WHOLE] * 2,
            compiler_params=params(),
        )(panel_order, solved, cv_first, cv_second)
        made = foot

        def at_root(bit):
            return jnp.stack([flag(("p2", bit), foot), flag(("p1", bit), foot)])

        bits = upper_bits(rows_n)
        if len(bits) == 2:
            one, two, three = (swap(foot, "row", rows_n, bit) for bit in (*bits, sum(bits)))
            foot = jnp.where(at_root(bits[1]), jnp.where(at_root(bits[0]), foot, one), jnp.where(at_root(bits[0]), two, three))
        else:
            for bit in bits:
                foot = jnp.where(at_root(bit), foot, swap(foot, "row", rows_n, bit))
        cu_first, cu_second = joined(after(cu.mine, foot), "col", cols_n, "side_c")
        swapped = swap(jnp.concatenate([cores[:, 2 * rank:], foot], axis=1), "row", rows_n, 1)
        cores = jnp.concatenate([cores[:, :2 * rank], foot], axis=1)
        edge = jnp.concatenate([choose("q2_side", cores[0, :2 * rank], swapped[0, :2 * rank]), choose("q1_side", cores[1], swapped[1])])
        for bit in all_bits(cols_n):
            got = swap(edge, "col", cols_n, bit)
            early = jnp.arange(5 * rank)[:, None] < 2 * rank
            stays = jnp.where(early, flag(("q2", bit), edge), flag(("q1", bit), edge))
            edge = jnp.where(stays, edge, got)

        moving, fixed = (after(x, made) for x in mines(v_lanes))
        mine = jnp.stack([choose("row_first", fixed, moving), choose("row_first", moving, fixed)])
        vj0, vj1 = joined(mine, "row", rows_n, "side_r")
        vp1, vp2 = (jnp.stack([vj0[s], vj1[s]]) for s in range(2))

        return pl.pallas_call(
            functools.partial(final_kernel, last_col=last["last_col"]),
            out_shape=jax.ShapeDtypeStruct((rows, cols, width, width), BF16),
            grid=(rows, cols),
            in_specs=[
                SCALARS, SCALARS,
                pl.BlockSpec((1, 1, width, rank), lambda i, j: (i, j, 0, 0)),
                pl.BlockSpec((1, 1, rank, width), lambda i, j: (i, j, 0, 0)),
                WHOLE, WHOLE,
                pl.BlockSpec((1, rank, width), lambda i, j: (j, 0, 0)),
                pl.BlockSpec((1, rank, width), lambda i, j: (j, 0, 0)),
                WHOLE, WHOLE, WHOLE],
            out_specs=pl.BlockSpec((1, 1, width, width), lambda i, j: (i, j, 0, 0)),
            compiler_params=params(),
        )(panel_order, tile_ranks, tile_u, tile_v, cu_first, cu_second, vp1, vp2, cores, swapped, edge)

    return on_device


def solution(mesh):
    placed = (P("row", "col", None, None), P("row", "col", None, None), P("row", "col"), P(), P())
    return jax.shard_map(
        make(mesh.shape["row"], mesh.shape["col"]),
        mesh=mesh,
        in_specs=placed,
        out_specs=P("row", "col", None, None),
        check_vma=False,
    )
```
